32 devices in a mesh: replica: 2 (over x), shard: 8 (over z, y), tensor: 2 (over core).
Axes of the slice: x: 2, y: 2, z: 4, core: 2. Of those that a mesh axis runs over, the one named last changes fastest.
Arguments:
- latent: bfloat16 [8192, 3072], P(('replica', 'shard'), 'tensor'), parts along dimension 0, may hold values from -6 to 6
- row_adapter_index: int32 [8192, 1], P(('replica', 'shard')), parts along dimension 0, may hold values from 0 to 7; in each aligned block of 512 rows (0 to 511, 512 to 1023, ...) at most 128 rows name the same one
- shared_weight: bfloat16 [3072, 3072], P(None, 'tensor'), may hold values from -0.109375 to 0.109375
- adapter_down_weight: bfloat16 [8, 3072, 64], P('shard', 'tensor'), may hold values from -0.109375 to 0.109375
- adapter_up_weight: bfloat16 [8, 64, 3072], P('shard', None, 'tensor'), may hold values from -0.75 to 0.75
Outputs:
- output_rows: bfloat16 [8192, 3072], P(('replica', 'shard'), 'tensor'), parts along dimension 0
The draws below stay inside these ranges and needn't reach their ends.
There are 2 independent parts, one for each index of `replica`. The reference program is written for one: setup_inputs(seed, part) draws one part's arguments, and reference() takes and returns one part's arrays. A program takes and returns all parts, laid end to end along the dimension named above; an argument that names none is the same for every part. Nothing has to cross between parts.
Inputs may be any that keep to these rules, and one draw needn't show every extreme that they name: `row_adapter_index`: among the 512 rows of one request group, no adapter is named by more than 128 rows, a bound that some block reaches.
All inputs are finite; a program needn't handle non-finite values.
Results may differ from the reference program's by a relative error of at most 0.005.
Values may be sent and summed in bfloat16 or wider, within the bound.
No kernel may reach another device: no remote copies, remote signals or barrier semaphores. Data moves between devices by JAX's collectives and lax.ppermute only.
A program may use at most 128 MiB of HBM per device.

```python
import math
import jax
import jax.numpy as jnp
import numpy as np
from jax import lax

MODEL_WIDTH = 3072
ADAPTER_RANK = 64
ROWS_DEV = 512
ADAPTER_COUNT = 8
MOST = 128
ROWS = 4096
N_SHARD = 8


def levels(own_key, dims, cuts, low, largest):
    gain, own = 1.0, jax.random.fold_in(own_key, 6)
    for dim, shards_of in cuts:
        steps = jnp.exp(jax.random.uniform(jax.random.fold_in(own, dim), (shards_of,), jnp.float32, low / len(cuts), largest / len(cuts)))
        gain = gain * jnp.repeat(steps, dims[dim] // shards_of).reshape([-1 if axis == dim else 1 for axis in range(len(dims))])
    return gain


def assign_block(rng, own, number, rows, count, top, most, skew):
    sequence = jax.random.permutation(rng, count)
    crowded, common = portions_of(count, rows * top, most, skew, True), portions_of(count, rows * top, most, skew, False)
    places = jnp.arange(count)

    def named(tallies, rotation):
        used = int((tallies > 0).sum())
        fixed = max(1, used // 4)
        shifted = fixed + (places - fixed + rotation * (used - fixed)) % max(1, count - fixed)
        return jnp.zeros((count,), jnp.int32).at[sequence[jnp.where(places < fixed, places, shifted)]].set(jnp.asarray(tallies, jnp.int32))

    tallies = jnp.where(number % 4 == 0, named(crowded, number // 4), named(common, number - number // 4 - 1))
    mixed = jax.random.permutation(jax.random.fold_in(own, 3), count)
    giver, sink = mixed[0:count // 2 * 2:2], mixed[1:count // 2 * 2:2]
    margin = jnp.minimum(tallies[giver] - 1, most - tallies[sink]) // 2
    margin = jnp.where((giver == sequence[0]) | (sink == sequence[0]) | (tallies[sink] == 0), 0, jnp.maximum(margin, 0))
    shifted = jax.random.randint(jax.random.fold_in(own, 4), (count // 2,), 0, 1 << 20) % (margin + 1)
    tallies = tallies.at[giver].add(-shifted).at[sink].add(shifted)
    labels = jnp.searchsorted(jnp.cumsum(tallies), jnp.arange(rows * top), side="right").astype(jnp.int32)
    grid = labels.reshape(top, rows).T
    grid = grid[jax.random.permutation(jax.random.fold_in(own, 1), rows)]
    rotation = jax.random.randint(jax.random.fold_in(own, 2), (rows, 1), 0, top)
    return jnp.take_along_axis(grid, (jnp.arange(top)[None, :] + rotation) % top, axis=1)


def portions_of(number_of, total, limit, lean, full):
    weights = [(1 << 20) // math.isqrt(grade ** lean) + 1 for grade in range(1, number_of + 1)]
    largest = limit if full else min(limit, max(-(-total // number_of), total * weights[0] // sum(weights)))
    least = 1 if total - largest >= number_of - 1 else 0
    holding, rest = [largest] + [least] * (number_of - 1), total - largest - least * (number_of - 1)
    while rest > 0:
        movable = [i for i in range(1, number_of) if holding[i] < largest] or [i for i in range(1, number_of) if holding[i] < limit]
        mass, left = sum([weights[i] for i in movable]), rest
        for i in movable:
            extra = min(limit - holding[i], max(1, left * weights[i] // mass), rest)
            holding[i] = holding[i] + extra
            rest = rest - extra
    return np.array(holding)


def centred(own_key, shape, spread, bound, pieces=(), kind=jnp.bfloat16):
    factor_of = levels(own_key, shape, pieces, -0.22, 0.18) if pieces else 1.0
    values = jax.random.normal(own_key, shape, jnp.float32) * spread * factor_of
    return jnp.minimum(jnp.maximum(values, -bound), bound).astype(kind)


def setup_inputs(seed: int = 0, part: int = 0) -> dict:
    arg_keys = jax.random.split(jax.random.key(seed), 6)
    part_keys = jax.random.split(jax.random.fold_in(arg_keys[5], part), 6)
    latent = centred(part_keys[0], (ROWS, MODEL_WIDTH), 1.0, 6.0, ((0, 8), (1, 2)))
    row_adapter_index_keys = jax.random.split(jax.random.fold_in(part_keys[1], 1), ROWS // ROWS_DEV)
    row_adapter_index_turns = jax.random.permutation(jax.random.fold_in(part_keys[1], 3), ROWS // ROWS_DEV)
    row_adapter_index = jax.vmap(lambda own, number: assign_block(jax.random.fold_in(part_keys[1], 2), own, number, ROWS_DEV, ADAPTER_COUNT, 1, MOST, 2))(row_adapter_index_keys, row_adapter_index_turns).reshape((ROWS, 1))
    shared_weight = centred(arg_keys[2], (MODEL_WIDTH, MODEL_WIDTH), MODEL_WIDTH ** -0.5, 0.109375, ((1, 2),))
    adapter_down_weight = centred(arg_keys[3], (ADAPTER_COUNT, MODEL_WIDTH, ADAPTER_RANK), MODEL_WIDTH ** -0.5, 0.109375, ((0, 8), (1, 2)))
    adapter_up_weight = centred(arg_keys[4], (ADAPTER_COUNT, ADAPTER_RANK, MODEL_WIDTH), ADAPTER_RANK ** -0.5, 0.75, ((0, 8), (2, 2)))
    return dict(latent=latent, row_adapter_index=row_adapter_index, shared_weight=shared_weight, adapter_down_weight=adapter_down_weight, adapter_up_weight=adapter_up_weight)


def slot_targets(adapter_ids):
    onehot = (adapter_ids[:, None] == jnp.arange(ADAPTER_COUNT, dtype=jnp.int32)[None, :]).astype(jnp.int32)
    position = jnp.sum((jnp.cumsum(onehot, axis=0) - 1) * onehot, axis=1).astype(jnp.int32)
    return (adapter_ids * MOST + position).astype(jnp.int32)


def reference(latent, row_adapter_index, shared_weight, adapter_down_weight, adapter_up_weight):
    down_weight_full = adapter_down_weight.astype(jnp.float32)
    up_weight_full = adapter_up_weight.astype(jnp.float32)
    blocks = latent.reshape(N_SHARD, ROWS_DEV, MODEL_WIDTH)
    id_blocks = row_adapter_index.reshape(N_SHARD, ROWS_DEV)

    def one_group(inputs):
        rows_block, adapter_ids = inputs
        base_part = jnp.dot(rows_block, shared_weight, preferred_element_type=jnp.float32)
        target = slot_targets(adapter_ids)
        packed = jnp.zeros((ADAPTER_COUNT * MOST, MODEL_WIDTH), jnp.float32).at[target].set(rows_block.astype(jnp.float32))
        packed = packed.reshape(ADAPTER_COUNT, MOST, MODEL_WIDTH)
        lowrank = jnp.einsum('kmd,kde->kme', packed, down_weight_full).astype(jnp.bfloat16)
        delta = jnp.einsum('kme,kef->kmf', lowrank.astype(jnp.float32), up_weight_full).astype(jnp.bfloat16)
        delta_rows = jnp.take(delta.reshape(ADAPTER_COUNT * MOST, MODEL_WIDTH), target, axis=0)
        return (base_part + delta_rows.astype(jnp.float32)).astype(jnp.bfloat16)

    output_rows = lax.map(one_group, (blocks, id_blocks))
    return output_rows.reshape(ROWS, MODEL_WIDTH)
```

```python
import jax
import jax.numpy as jnp
from jax import lax
from jax.experimental import pallas as pl
from jax.experimental.pallas import tpu as pltpu
from jax.sharding import PartitionSpec as P

VMEM_BYTES = 60 * 1024 * 1024
CHUNK = 512


def swap(value, axis):
    return lax.ppermute(value, axis, [(0, 1), (1, 0)])


def neighbour(value, shards):
    return lax.ppermute(value, "shard", [(i, i ^ 1) for i in range(shards)])


def along_line(value, shards, step):
    return lax.ppermute(value, "shard", [(i, (i + 2 * step) % shards) for i in range(shards)])


def routed_gather(block, shards, replica):
    half = block.shape[0] // 2
    own_half = lax.dynamic_slice_in_dim(block, replica * half, half, axis=0)
    pieces = [block, neighbour(block, shards)]
    arrived = [along_line(own_half, shards, step) for step in range(1, shards // 2)]
    for piece in arrived:
        beside = neighbour(piece, shards)
        pieces += [piece, swap(piece, "replica"), beside, swap(beside, "replica")]
    return pieces


def routed_owners(shards, index):
    owners = [index, index ^ 1]
    for step in range(1, shards // 2):
        source = (index - 2 * step) % shards
        owners += [source, source ^ 1]
    return jnp.stack(owners)


def stack_pieces(info, pieces, stack):
    offset = 0
    half = pieces[0].shape[0] // 2
    for number, piece in enumerate(pieces):
        rows = piece.shape[0]
        if number < 2 and len(pieces) > 2:
            first = pl.multiple_of(info[0] * half, half)
            second = pl.multiple_of((1 - info[0]) * half, half)
            stack[offset : offset + half, :] = piece[pl.ds(first, half), :]
            stack[offset + half : offset + rows, :] = piece[pl.ds(second, half), :]
        else:
            stack[offset : offset + rows, :] = piece[...]
        offset += rows


def down_kernel(info, ids, owners, latent, *refs):
    pieces, out, stack = refs[:-2], refs[-2], refs[-1]
    stack_pieces(info, pieces, stack)
    total = jnp.zeros(out.shape, jnp.float32)
    width = out.shape[1]
    for begin in range(0, stack.shape[0], CHUNK):
        part = lax.dot_general(
            latent[...],
            stack[begin : begin + CHUNK, :],
            (((1,), (1,)), ((), ())),
            preferred_element_type=jnp.float32,
        )
        part = jnp.where(ids[...] == owners[:, begin : begin + CHUNK], part, 0.0)
        for lane in range(0, CHUNK, width):
            total += part[:, lane : lane + width]
    out[...] = total


def base_kernel(info, own, other, own_weight, other_weight, out):
    out[...] = jnp.dot(
        own[...], own_weight[...], preferred_element_type=jnp.float32
    ) + jnp.dot(other[...], other_weight[...], preferred_element_type=jnp.float32)


def up_kernel(info, ids, owners, mine, theirs, base, *refs):
    pieces, out, stack = refs[:-2], refs[-2], refs[-1]
    stack_pieces(info, pieces, stack)
    lowrank = (mine[...] + theirs[...]).astype(jnp.bfloat16).astype(jnp.float32)
    delta = jnp.zeros(out.shape, jnp.float32)
    for begin in range(0, stack.shape[0], CHUNK):
        wide = jnp.concatenate([lowrank] * (CHUNK // lowrank.shape[1]), axis=1)
        wide = jnp.where(ids[...] == owners[:, begin : begin + CHUNK], wide, 0.0)
        delta += jnp.dot(
            wide.astype(jnp.bfloat16),
            stack[begin : begin + CHUNK, :],
            preferred_element_type=jnp.float32,
        )
    out[...] = (base[...] + delta.astype(jnp.bfloat16).astype(jnp.float32)).astype(out.dtype)


def on_device(latent, row_adapter_index, shared_weight, adapter_down_weight, adapter_up_weight):
    rows, half_width = latent.shape
    out_width = shared_weight.shape[1]
    local_adapters, _, rank = adapter_down_weight.shape
    shards = lax.axis_size("shard")
    adapters = shards * local_adapters
    replica, index = lax.axis_index("replica"), lax.axis_index("shard")
    core = lax.axis_index("tensor")
    info = jnp.stack([replica, core]).astype(jnp.int32)

    down = jnp.swapaxes(adapter_down_weight, 1, 2).reshape(local_adapters * rank, half_width)
    up = adapter_up_weight.reshape(local_adapters * rank, out_width)
    if shards == 8 and local_adapters == 1 and lax.axis_size("replica") == 2:
        down_pieces = routed_gather(down, shards, replica)
        up_pieces = routed_gather(up, shards, replica)
        owner_ids = routed_owners(shards, index)
    else:
        down_pieces = [lax.all_gather(down, "shard", axis=0, tiled=True)]
        up_pieces = [lax.all_gather(up, "shard", axis=0, tiled=True)]
        owner_ids = jnp.arange(adapters)
    owners = jnp.repeat(owner_ids.astype(jnp.int32), rank)[None, :]
    other = swap(latent, "tensor")

    smem = pl.BlockSpec(memory_space=pltpu.SMEM)
    vmem = pl.BlockSpec(memory_space=pltpu.VMEM)
    params = pltpu.CompilerParams(vmem_limit_bytes=VMEM_BYTES)
    columns = adapters * rank
    mine = pl.pallas_call(
        down_kernel,
        out_shape=jax.ShapeDtypeStruct((rows, 2 * rank), jnp.float32),
        in_specs=[smem] + [vmem] * (3 + len(down_pieces)),
        out_specs=vmem,
        scratch_shapes=[pltpu.VMEM((columns, half_width), jnp.bfloat16)],
        compiler_params=params,
        cost_estimate=pl.CostEstimate(
            flops=2 * rows * columns * half_width,
            bytes_accessed=2 * (rows + columns) * half_width,
            transcendentals=0,
        ),
    )(info, row_adapter_index, owners, latent, *down_pieces)
    theirs = swap(mine, "tensor")

    tile = 512
    base = pl.pallas_call(
        base_kernel,
        out_shape=jax.ShapeDtypeStruct((rows, out_width), jnp.float32),
        grid_spec=pltpu.PrefetchScalarGridSpec(
            num_scalar_prefetch=1,
            grid=(out_width // tile,),
            in_specs=[
                pl.BlockSpec((rows, half_width), lambda j, info: (0, 0)),
                pl.BlockSpec((rows, half_width), lambda j, info: (0, 0)),
                pl.BlockSpec((half_width, tile), lambda j, info: (info[1], j)),
                pl.BlockSpec((half_width, tile), lambda j, info: (1 - info[1], j)),
            ],
            out_specs=pl.BlockSpec((rows, tile), lambda j, info: (0, j)),
        ),
        compiler_params=params,
        cost_estimate=pl.CostEstimate(
            flops=4 * rows * half_width * out_width,
            bytes_accessed=4 * half_width * (rows + out_width) + 4 * rows * out_width,
            transcendentals=0,
        ),
    )(info, latent, other, shared_weight, shared_weight)

    return pl.pallas_call(
        up_kernel,
        out_shape=jax.ShapeDtypeStruct((rows, out_width), jnp.bfloat16),
        in_specs=[smem] + [vmem] * (5 + len(up_pieces)),
        out_specs=vmem,
        scratch_shapes=[pltpu.VMEM((columns, out_width), jnp.bfloat16)],
        compiler_params=params,
        cost_estimate=pl.CostEstimate(
            flops=2 * rows * columns * out_width,
            bytes_accessed=6 * rows * out_width + 2 * columns * out_width,
            transcendentals=0,
        ),
    )(info, row_adapter_index, owners, mine, theirs, base, *up_pieces)


def solution(mesh):
    return jax.shard_map(
        on_device,
        mesh=mesh,
        in_specs=(
            P(("replica", "shard"), "tensor"),
            P(("replica", "shard"), None),
            P(None, "tensor"),
            P("shard", "tensor", None),
            P("shard", None, "tensor"),
        ),
        out_specs=P(("replica", "shard"), "tensor"),
        check_vma=False,
    )
```

```python
import jax
import jax.numpy as jnp
from jax import lax
from jax.experimental import pallas as pl
from jax.experimental.pallas import tpu as pltpu
from jax.sharding import PartitionSpec as P

MIB = 1024 * 1024
CHUNK = 512
AXES = ("replica", "shard", "tensor")
SMEM = pl.BlockSpec(memory_space=pltpu.SMEM)
VMEM = pl.BlockSpec(memory_space=pltpu.VMEM)
ANY = pl.BlockSpec(memory_space=pl.ANY)


def swap(value, axis):
    return lax.ppermute(value, axis, [(0, 1), (1, 0)])


def along_line(value, shards, step):
    return lax.ppermute(value, "shard", [(i, (i + 2 * step) % shards) for i in range(shards)])


def in_plane(value, shards, first):
    pairs = []
    for r in range(2):
        for s in range(shards):
            for t in range(2):
                to_r, to_s = (r, s ^ 1) if (t == 0) == first else (r ^ 1, s)
                pairs.append(((r * shards + s) * 2 + t, (to_r * shards + to_s) * 2 + t))
    return lax.ppermute(value, AXES, pairs)


def call(kernel, out_shape, in_specs, limit, scratch=(), flops=0, moved=0):
    return pl.pallas_call(
        kernel,
        out_shape=out_shape,
        in_specs=in_specs,
        out_specs=jax.tree.map(lambda _: VMEM, out_shape),
        scratch_shapes=list(scratch),
        compiler_params=pltpu.CompilerParams(vmem_limit_bytes=limit * MIB),
        cost_estimate=pl.CostEstimate(flops=flops, bytes_accessed=moved, transcendentals=0),
    )


def halves_kernel(info, down, up, down_half, up_half, both):
    rank = down.shape[0]
    half = rank // 2
    first = pl.multiple_of(info[0] * half, half)
    down_half[...] = down[pl.ds(first, half), :]
    up_half[...] = up[pl.ds(first, half), :]
    both[:rank, :] = down[...]
    both[rank:, :] = up[...]


def pack_kernel(*refs):
    *pieces, _, out = refs
    rows = pieces[0].shape[0]
    for number, piece in enumerate(pieces):
        out[number * rows : (number + 1) * rows, :] = piece[...]


def stack_routed(info, own, beside, line, first, second, corner, stack):
    rank = own.shape[0]
    half = rank // 2
    mine = pl.multiple_of(info[0] * half, half)
    rest = pl.multiple_of((1 - info[0]) * half, half)
    stack[0:half, :] = own[pl.ds(mine, half), :]
    stack[half : 2 * half, :] = beside[pl.ds(mine, half), :]
    stack[2 * half : 3 * half, :] = own[pl.ds(rest, half), :]
    stack[3 * half : 4 * half, :] = beside[pl.ds(rest, half), :]
    for step in range(line.shape[0] // half):
        rows = slice(step * half, (step + 1) * half)
        base = (step + 1) * 2 * rank
        stack[base : base + half, :] = line[rows, :]
        stack[pl.ds(pl.multiple_of(base + (1 + info[1]) * half, half), half), :] = first[rows, :]
        stack[pl.ds(pl.multiple_of(base + (2 - info[1]) * half, half), half), :] = second[rows, :]
        stack[base + 3 * half : base + 4 * half, :] = corner[rows, :]


def routed_owners(shards, index, rank):
    sources = [(index - 2 * step) % shards for step in range(shards // 2)]
    owners = jnp.stack([jnp.stack([s, s ^ 1, s, s ^ 1]) for s in sources])
    return jnp.repeat(owners.reshape(-1).astype(jnp.int32), rank // 2)[None, :]


def fill_stack(info, refs, stack, which):
    if len(refs) == 1:
        stack[...] = refs[0][...]
    else:
        own, beside, *others = refs
        rank = own.shape[0]
        stack_routed(info, own, beside.at[which * rank : (which + 1) * rank], *others, stack)


def down_kernel(info, ids, owners, latent, *refs):
    *pieces, _, out, stack = refs
    fill_stack(info, pieces, stack, 0)
    total = jnp.zeros(out.shape, jnp.float32)
    width = out.shape[1]
    for begin in range(0, stack.shape[0], CHUNK):
        part = lax.dot_general(
            latent[...],
            stack[begin : begin + CHUNK, :],
            (((1,), (1,)), ((), ())),
            preferred_element_type=jnp.float32,
        )
        part = jnp.where(ids[...] == owners[:, begin : begin + CHUNK], part, 0.0)
        for lane in range(0, CHUNK, width):
            total += part[:, lane : lane + width]
    out[...] = total


def base_kernel(info, own, other, own_weight, other_weight, _, out, token):
    token[...] = jnp.zeros_like(token)
    out[...] = jnp.dot(
        own[...], own_weight[...], preferred_element_type=jnp.float32
    ) + jnp.dot(other[...], other_weight[...], preferred_element_type=jnp.float32)


def base_half(info, latent, other, weight, after, number):
    rows, half_width = latent.shape
    columns = weight.shape[1] // 2
    tile = columns // 3
    skip = number * (columns // tile)
    return pl.pallas_call(
        base_kernel,
        out_shape=[
            jax.ShapeDtypeStruct((rows, columns), jnp.float32),
            jax.ShapeDtypeStruct((8, 128), jnp.float32),
        ],
        grid_spec=pltpu.PrefetchScalarGridSpec(
            num_scalar_prefetch=1,
            grid=(columns // tile,),
            in_specs=[
                pl.BlockSpec((rows, half_width), lambda j, info: (0, 0)),
                pl.BlockSpec((rows, half_width), lambda j, info: (0, 0)),
                pl.BlockSpec((half_width, tile), lambda j, info: (info[1], j + skip)),
                pl.BlockSpec((half_width, tile), lambda j, info: (1 - info[1], j + skip)),
                ANY,
            ],
            out_specs=[
                pl.BlockSpec((rows, tile), lambda j, info: (0, j)),
                pl.BlockSpec((8, 128), lambda j, info: (0, 0)),
            ],
        ),
        compiler_params=pltpu.CompilerParams(vmem_limit_bytes=54 * MIB),
        cost_estimate=pl.CostEstimate(
            flops=0,
            bytes_accessed=0,
            transcendentals=0,
        ),
    )(info, latent, other, weight, weight, after)


def up_kernel(info, ids, owners, mine, theirs, left, right, *refs):
    *pieces, out, stack = refs
    fill_stack(info, pieces, stack, 1)
    lowrank = (mine[...] + theirs[...]).astype(jnp.bfloat16).astype(jnp.float32)
    repeated = jnp.concatenate([lowrank] * (CHUNK // lowrank.shape[1]), axis=1)
    columns = left.shape[1]
    for number, base in enumerate((left, right)):
        place = slice(number * columns, (number + 1) * columns)
        delta = jnp.zeros(base.shape, jnp.float32)
        for begin in range(0, stack.shape[0], CHUNK):
            wide = jnp.where(ids[...] == owners[:, begin : begin + CHUNK], repeated, 0.0)
            delta += jnp.dot(
                wide.astype(jnp.bfloat16),
                stack[begin : begin + CHUNK, place],
                preferred_element_type=jnp.float32,
            )
        total = base[...] + delta.astype(jnp.bfloat16).astype(jnp.float32)
        out[:, place] = total.astype(out.dtype)


def on_device(latent, row_adapter_index, shared_weight, adapter_down_weight, adapter_up_weight):
    rows, half_width = latent.shape
    out_width = shared_weight.shape[1]
    local_adapters, _, rank = adapter_down_weight.shape
    shards = lax.axis_size("shard")
    adapters = shards * local_adapters
    columns = adapters * rank
    index = lax.axis_index("shard")
    info = jnp.stack([lax.axis_index("replica"), lax.axis_index("tensor")]).astype(jnp.int32)

    other = swap(latent, "tensor")
    down = jnp.swapaxes(adapter_down_weight, 1, 2).reshape(local_adapters * rank, half_width)
    up = adapter_up_weight.reshape(local_adapters * rank, out_width)
    routed = shards == 8 and local_adapters == 1 and lax.axis_size("replica") == 2
    if routed:
        half = rank // 2
        reach = shards // 2 - 1
        piece = jax.ShapeDtypeStruct((half, half_width), latent.dtype)
        packed = jax.ShapeDtypeStruct((reach * half, half_width), latent.dtype)
        down_half, up_half, both = call(
            halves_kernel,
            [piece, piece, jax.ShapeDtypeStruct((2 * rank, half_width), latent.dtype)],
            [SMEM, VMEM, VMEM],
            4,
        )(info, down, up)
        down_line = [along_line(down_half, shards, step) for step in range(1, reach + 1)]
        up_line = [along_line(up_half, shards, step) for step in range(1, reach + 1)]
        beside = lax.ppermute(both, "shard", [(i, i ^ 1) for i in range(shards)])
        left, left_token = base_half(info, latent, other, shared_weight, down_half, 0)
        pack = call(pack_kernel, packed, [VMEM] * reach + [ANY], 4)
        down_packed = pack(*down_line, left_token)
        down_first = in_plane(down_packed, shards, True)
        down_second = in_plane(down_packed, shards, False)
        right, right_token = base_half(info, latent, other, shared_weight, down_packed, 1)
        down_corner = in_plane(down_first, shards, False)
        up_packed = pack(*up_line, right_token)
        up_first = in_plane(up_packed, shards, True)
        up_second = in_plane(up_packed, shards, False)
        down_pieces = [down, beside, down_packed, down_first, down_second, down_corner]
        owners = routed_owners(shards, index, rank)
        after = up_packed
    else:
        down_pieces = [lax.all_gather(down, "shard", axis=0, tiled=True)]
        up_pieces = [lax.all_gather(up, "shard", axis=0, tiled=True)]
        left, left_token = base_half(info, latent, other, shared_weight, latent, 0)
        right, right_token = base_half(info, latent, other, shared_weight, latent, 1)
        owners = jnp.repeat(jnp.arange(adapters, dtype=jnp.int32), rank)[None, :]
        after = left

    mine = call(
        down_kernel,
        jax.ShapeDtypeStruct((rows, 2 * rank), jnp.float32),
        [SMEM] + [VMEM] * (3 + len(down_pieces)) + [ANY],
        16 if routed else 56,
        [pltpu.VMEM((columns, half_width), jnp.bfloat16)],
        2 * rows * columns * half_width,
        2 * (rows + columns) * half_width,
    )(info, row_adapter_index, owners, latent, *down_pieces, after)
    theirs = swap(mine, "tensor")
    if routed:
        up_corner = in_plane(up_first, shards, False)
        up_pieces = [up, beside, up_packed, up_first, up_second, up_corner]

    return call(
        up_kernel,
        jax.ShapeDtypeStruct((rows, out_width), jnp.bfloat16),
        [SMEM] + [VMEM] * (6 + len(up_pieces)),
        24 if routed else 56,
        [pltpu.VMEM((columns, out_width), jnp.bfloat16)],
        2 * rows * columns * out_width,
        6 * rows * out_width + 2 * columns * out_width,
    )(info, row_adapter_index, owners, mine, theirs, left, right, *up_pieces)


def solution(mesh):
    return jax.shard_map(
        on_device,
        mesh=mesh,
        in_specs=(
            P(("replica", "shard"), "tensor"),
            P(("replica", "shard"), None),
            P(None, "tensor"),
            P("shard", "tensor", None),
            P("shard", None, "tensor"),
        ),
        out_specs=P(("replica", "shard"), "tensor"),
        check_vma=False,
    )
```

```python
import jax
import jax.numpy as jnp
import numpy as np
from jax import lax
from jax.experimental import pallas as pl
from jax.experimental.pallas import tpu as pltpu
from jax.sharding import PartitionSpec as P

MIB = 1024 * 1024
CHUNK = 512
AXES = ("replica", "shard", "tensor")
WAVES = ((1, 3), (2,))
SMEM = pl.BlockSpec(memory_space=pltpu.SMEM)
VMEM = pl.BlockSpec(memory_space=pltpu.VMEM)
ANY = pl.BlockSpec(memory_space=pl.ANY)


def swap(value, axis):
    return lax.ppermute(value, axis, [(0, 1), (1, 0)])


def neighbour(value, shards):
    return lax.ppermute(value, "shard", [(i, i ^ 1) for i in range(shards)])


def along_line(value, shards, step):
    return lax.ppermute(value, "shard", [(i, (i + 2 * step) % shards) for i in range(shards)])


def in_plane(value, shards, first):
    pairs = []
    for r in range(2):
        for s in range(shards):
            for t in range(2):
                to_r, to_s = (r, s ^ 1) if (t == 0) == first else (r ^ 1, s)
                pairs.append(((r * shards + s) * 2 + t, (to_r * shards + to_s) * 2 + t))
    return lax.ppermute(value, AXES, pairs)


def call(kernel, out_shape, in_specs, limit, scratch=(), flops=0, moved=0):
    return pl.pallas_call(
        kernel,
        out_shape=out_shape,
        in_specs=in_specs,
        out_specs=jax.tree.map(lambda _: VMEM, out_shape),
        scratch_shapes=list(scratch),
        compiler_params=pltpu.CompilerParams(vmem_limit_bytes=limit * MIB),
        cost_estimate=pl.CostEstimate(flops=flops, bytes_accessed=moved, transcendentals=0),
    )


def owner_table(shards, rank):
    table = []
    for index in range(shards):
        sources = [(index - 2 * step) % shards for step in range(shards // 2)]
        table.append([a for s in sources for a in (s, s ^ 1) for _ in range(rank)])
    return np.array(table, np.int32)


def pack(pieces, *after):
    rows, width = pieces[0].shape
    count = len(pieces)

    def kernel(*refs):
        for number in range(count):
            refs[-1][number * rows : (number + 1) * rows, :] = refs[number][...]

    return call(
        kernel,
        jax.ShapeDtypeStruct((count * rows, width), pieces[0].dtype),
        [VMEM] * count + [ANY] * len(after),
        4,
    )(*pieces, *after)


def fill_stack(info, which, refs, stack):
    if len(refs) == 1:
        stack[...] = refs[0][...]
        return
    own, beside, *received = refs
    rank = own.shape[0]
    half = rank // 2
    mine = pl.multiple_of(info[0] * half, half)
    rest = pl.multiple_of((1 - info[0]) * half, half)
    stack[0:half, :] = own[pl.ds(mine, half), :]
    stack[half:rank, :] = own[pl.ds(rest, half), :]
    stack[rank : rank + half, :] = beside[pl.ds(which * rank + mine, half), :]
    stack[rank + half : 2 * rank, :] = beside[pl.ds(which * rank + rest, half), :]
    for wave, groups in enumerate(WAVES):
        line, first, second, corner = received[4 * wave : 4 * wave + 4]
        for number, group in enumerate(groups):
            rows = slice((2 * number + which) * half, (2 * number + which + 1) * half)
            top = 2 * rank * group
            stack[top : top + half, :] = line[rows, :]
            place = pl.multiple_of(top + (2 - info[1]) * half, half)
            stack[pl.ds(place, half), :] = first[rows, :]
            place = pl.multiple_of(top + (1 + info[1]) * half, half)
            stack[pl.ds(place, half), :] = second[rows, :]
            stack[top + 3 * half : top + 4 * half, :] = corner[rows, :]


def down_kernel(info, ids, owners, latent, *refs):
    *pieces, _, out, stack = refs
    fill_stack(info, 0, pieces, stack)
    total = jnp.zeros(out.shape, jnp.float32)
    width = out.shape[1]
    for begin in range(0, stack.shape[0], CHUNK):
        part = lax.dot_general(
            latent[...],
            stack[begin : begin + CHUNK, :],
            (((1,), (1,)), ((), ())),
            preferred_element_type=jnp.float32,
        )
        part = jnp.where(ids[...] == owners[:, begin : begin + CHUNK], part, 0.0)
        for lane in range(0, CHUNK, width):
            total += part[:, lane : lane + width]
    out[...] = total


def base_kernel(info, own, other, weight, _, out, token, rows_ref, weight_ref, sems, *, skip):
    width = own.shape[1]
    tiles, _, tile = weight_ref.shape
    copies = [
        pltpu.make_async_copy(own, rows_ref.at[:, pl.ds(0, width)], sems.at[2 * tiles]),
        pltpu.make_async_copy(other, rows_ref.at[:, pl.ds(width, width)], sems.at[2 * tiles + 1]),
    ]
    for number in range(tiles):
        place = pl.ds((skip + number) * tile, tile)
        for part, owner in ((0, info[1]), (1, 1 - info[1])):
            source = pl.ds(pl.multiple_of(owner * width, width), width)
            copies.append(
                pltpu.make_async_copy(
                    weight.at[source, place],
                    weight_ref.at[number, pl.ds(part * width, width), :],
                    sems.at[2 * number + part],
                )
            )
    for copy in copies:
        copy.start()
    token[...] = jnp.zeros_like(token)
    copies[0].wait()
    copies[1].wait()
    for number in range(tiles):
        copies[2 * number + 2].wait()
        copies[2 * number + 3].wait()
        out[:, number * tile : (number + 1) * tile] = jnp.dot(
            rows_ref[...], weight_ref[number], preferred_element_type=jnp.float32
        )


def base(info, latent, other, weight, after, skip, tiles):
    rows, half_width = latent.shape
    tile = CHUNK
    columns = tiles * tile
    return pl.pallas_call(
        lambda *refs: base_kernel(*refs, skip=skip),
        out_shape=[
            jax.ShapeDtypeStruct((rows, columns), jnp.float32),
            jax.ShapeDtypeStruct((8, 128), jnp.float32),
        ],
        in_specs=[SMEM, ANY, ANY, ANY, ANY],
        out_specs=[VMEM, VMEM],
        scratch_shapes=[
            pltpu.VMEM((rows, 2 * half_width), latent.dtype),
            pltpu.VMEM((tiles, 2 * half_width, tile), weight.dtype),
            pltpu.SemaphoreType.DMA((2 * tiles + 2,)),
        ],
        compiler_params=pltpu.CompilerParams(vmem_limit_bytes=50 * MIB),
        cost_estimate=pl.CostEstimate(
            flops=4 * rows * half_width * columns,
            bytes_accessed=4 * half_width * (rows + columns) + 4 * rows * columns,
            transcendentals=0,
        ),
    )(info, latent, other, weight, after)


def up_kernel(info, ids, owners, mine, theirs, left, right, *refs):
    *pieces, out, stack = refs
    fill_stack(info, 1, pieces, stack)
    lowrank = (mine[...] + theirs[...]).astype(jnp.bfloat16).astype(jnp.float32)
    repeated = jnp.concatenate([lowrank] * (CHUNK // lowrank.shape[1]), axis=1)
    split = left.shape[1]
    for begin in range(0, out.shape[1], CHUNK):
        place = slice(begin, begin + CHUNK)
        delta = jnp.zeros((out.shape[0], CHUNK), jnp.float32)
        for depth in range(0, stack.shape[0], CHUNK):
            wide = jnp.where(ids[...] == owners[:, depth : depth + CHUNK], repeated, 0.0)
            delta += jnp.dot(
                wide.astype(jnp.bfloat16),
                stack[depth : depth + CHUNK, place],
                preferred_element_type=jnp.float32,
            )
        part = left[:, place] if begin < split else right[:, begin - split : begin - split + CHUNK]
        total = part + delta.astype(jnp.bfloat16).astype(jnp.float32)
        out[:, place] = total.astype(out.dtype)


def on_device(latent, row_adapter_index, shared_weight, adapter_down_weight, adapter_up_weight):
    rows, half_width = latent.shape
    out_width = shared_weight.shape[1]
    local_adapters, _, rank = adapter_down_weight.shape
    shards = lax.axis_size("shard")
    adapters = shards * local_adapters
    columns = adapters * rank
    index, replica = lax.axis_index("shard"), lax.axis_index("replica")
    info = jnp.stack([replica, lax.axis_index("tensor")]).astype(jnp.int32)
    tiles = out_width // CHUNK
    first_tiles = 2 * tiles // 3

    down = jnp.swapaxes(adapter_down_weight, 1, 2).reshape(local_adapters * rank, half_width)
    up = adapter_up_weight.reshape(local_adapters * rank, out_width)
    routed = shards == 8 and local_adapters == 1 and lax.axis_size("replica") == 2
    if routed:
        half = rank // 2
        piece = jnp.concatenate(
            [
                lax.dynamic_slice_in_dim(down, replica * half, half, axis=0),
                lax.dynamic_slice_in_dim(up, replica * half, half, axis=0),
            ]
        )
        line = {step: along_line(piece, shards, step) for wave in WAVES for step in wave}
        other = swap(latent, "tensor")
        beside = neighbour(jnp.concatenate([down, up]), shards)
        left, token = base(info, latent, other, shared_weight, piece, 0, first_tiles)
        held = pack([line[step] for step in WAVES[0]], token, beside)
        right, token = base(
            info, latent, other, shared_weight, held, first_tiles, tiles - first_tiles
        )
        first, second = in_plane(held, shards, True), in_plane(held, shards, False)
        received = [held, first, second, in_plane(first, shards, False)]
        held = pack([line[step] for step in WAVES[1]], token, first)
        first, second = in_plane(held, shards, True), in_plane(held, shards, False)
        received += [held, first, second, in_plane(first, shards, False)]
        down_pieces = [down, beside, *received]
        up_pieces = [up, beside, *received]
        owners = jnp.asarray(owner_table(shards, rank))[index][None, :]
    else:
        other = swap(latent, "tensor")
        down_pieces = [lax.all_gather(down, "shard", axis=0, tiled=True)]
        up_pieces = [lax.all_gather(up, "shard", axis=0, tiled=True)]
        left, token = base(info, latent, other, shared_weight, latent, 0, first_tiles)
        right, token = base(
            info, latent, other, shared_weight, latent, first_tiles, tiles - first_tiles
        )
        owners = jnp.repeat(jnp.arange(adapters, dtype=jnp.int32), rank)[None, :]

    mine = call(
        down_kernel,
        jax.ShapeDtypeStruct((rows, 2 * rank), jnp.float32),
        [SMEM] + [VMEM] * (3 + len(down_pieces)) + [ANY],
        16 if routed else 56,
        [pltpu.VMEM((columns, half_width), jnp.bfloat16)],
        2 * rows * columns * half_width,
        2 * (rows + columns) * half_width,
    )(info, row_adapter_index, owners, latent, *down_pieces, token)
    theirs = swap(mine, "tensor")

    return call(
        up_kernel,
        jax.ShapeDtypeStruct((rows, out_width), jnp.bfloat16),
        [SMEM] + [VMEM] * (6 + len(up_pieces)),
        24 if routed else 56,
        [pltpu.VMEM((columns, out_width), jnp.bfloat16)],
        2 * rows * columns * out_width,
        6 * rows * out_width + 2 * columns * out_width,
    )(info, row_adapter_index, owners, mine, theirs, left, right, *up_pieces)


def solution(mesh):
    return jax.shard_map(
        on_device,
        mesh=mesh,
        in_specs=(
            P(("replica", "shard"), "tensor"),
            P(("replica", "shard"), None),
            P(None, "tensor"),
            P("shard", "tensor", None),
            P("shard", None, "tensor"),
        ),
        out_specs=P(("replica", "shard"), "tensor"),
        check_vma=False,
    )
```

```python
import jax
import jax.numpy as jnp
import numpy as np
from jax import lax
from jax.experimental import pallas as pl
from jax.experimental.pallas import tpu as pltpu
from jax.sharding import PartitionSpec as P

MIB = 1024 * 1024
CHUNK = 512
AXES = ("replica", "shard", "tensor")
WAVES = ((1, 3), (2,))
BASE_COST = 1000
BASE_LIMIT = 44
LAY_OUT_LIMIT = 56
SMEM = pl.BlockSpec(memory_space=pltpu.SMEM)
VMEM = pl.BlockSpec(memory_space=pltpu.VMEM)
ANY = pl.BlockSpec(memory_space=pl.ANY)
TOKEN = jax.ShapeDtypeStruct((8, 128), jnp.float32)


def swap(value, axis):
    return lax.ppermute(value, axis, [(0, 1), (1, 0)])


def neighbour(value, shards):
    return lax.ppermute(value, "shard", [(i, i ^ 1) for i in range(shards)])


def along_line(value, shards, step):
    return lax.ppermute(value, "shard", [(i, (i + 2 * step) % shards) for i in range(shards)])


def in_plane(value, shards, first):
    pairs = []
    for r in range(2):
        for s in range(shards):
            for t in range(2):
                to_r, to_s = (r, s ^ 1) if (t == 0) == first else (r ^ 1, s)
                pairs.append(((r * shards + s) * 2 + t, (to_r * shards + to_s) * 2 + t))
    return lax.ppermute(value, AXES, pairs)


def call(kernel, out_shape, in_specs, limit, scratch=(), flops=0, moved=0):
    return pl.pallas_call(
        kernel,
        out_shape=out_shape,
        in_specs=in_specs,
        out_specs=jax.tree.map(lambda _: VMEM, out_shape),
        scratch_shapes=list(scratch),
        compiler_params=pltpu.CompilerParams(vmem_limit_bytes=limit * MIB),
        cost_estimate=pl.CostEstimate(flops=flops, bytes_accessed=moved, transcendentals=0),
    )


def owner_table(shards, rank):
    table = []
    for index in range(shards):
        sources = [(index - 2 * step) % shards for step in (0, *WAVES[0], *WAVES[1])]
        table.append([a for s in sources for a in (s, s ^ 1) for _ in range(rank)])
    return np.array(table, np.int32)


def pack(pieces, *after):
    rows, width = pieces[0].shape
    count = len(pieces)

    def kernel(*refs):
        out, token = refs[-2:]
        for number in range(count):
            out[number * rows : (number + 1) * rows, :] = refs[number][...]
        token[...] = jnp.zeros_like(token)

    return call(
        kernel,
        [jax.ShapeDtypeStruct((count * rows, width), pieces[0].dtype), TOKEN],
        [VMEM] * count + [ANY] * len(after),
        4,
    )(*pieces, *after)


def lay_out(down, up, piece, both, sems):
    rank = down.shape[0]
    half = rank // 2
    mine = pl.ds(pl.multiple_of(lax.axis_index("replica") * half, half), half)
    pairs = (
        (down.at[mine, :], piece.at[pl.ds(0, half), :]),
        (up.at[mine, :], piece.at[pl.ds(half, half), :]),
        (down, both.at[pl.ds(0, rank), :]),
        (up, both.at[pl.ds(rank, rank), :]),
    )
    copies = [pltpu.make_async_copy(*pair, sems.at[n]) for n, pair in enumerate(pairs)]
    for copy in copies:
        copy.start()
    for copy in copies:
        copy.wait()


def fill_own(info, which, own, beside, stack):
    rank = own.shape[0]
    half = rank // 2
    mine = pl.multiple_of(info[0] * half, half)
    rest = pl.multiple_of((1 - info[0]) * half, half)
    stack[0:half, :] = own[pl.ds(mine, half), :]
    stack[half:rank, :] = own[pl.ds(rest, half), :]
    stack[rank : rank + half, :] = beside[pl.ds(which * rank + mine, half), :]
    stack[rank + half : 2 * rank, :] = beside[pl.ds(which * rank + rest, half), :]


def fill_wave(info, which, pieces, half, stack, top):
    line, first, second, corner = pieces
    for number in range(line.shape[0] // (2 * half)):
        rows = slice((2 * number + which) * half, (2 * number + which + 1) * half)
        stack[top : top + half, :] = line[rows, :]
        place = pl.multiple_of(top + (2 - info[1]) * half, half)
        stack[pl.ds(place, half), :] = first[rows, :]
        place = pl.multiple_of(top + (1 + info[1]) * half, half)
        stack[pl.ds(place, half), :] = second[rows, :]
        stack[top + 3 * half : top + 4 * half, :] = corner[rows, :]
        top += 4 * half


def masked_products(ids, owners, latent, stack, width):
    total = None
    for begin in range(0, stack.shape[0], CHUNK):
        rows = slice(begin, min(begin + CHUNK, stack.shape[0]))
        part = lax.dot_general(
            latent[...],
            stack[rows, :],
            (((1,), (1,)), ((), ())),
            preferred_element_type=jnp.float32,
        )
        part = jnp.where(ids[...] == owners[:, rows], part, 0.0)
        for lane in range(0, part.shape[1], width):
            fold = part[:, lane : lane + width]
            total = fold if total is None else total + fold
    return total


def down_whole_kernel(ids, owners, latent, stack, out):
    out[...] = masked_products(ids, owners, latent, stack, out.shape[1])


def down_first_kernel(info, ids, owners, latent, own, beside, *refs):
    *pieces, _, out, stack = refs
    half = own.shape[0] // 2
    fill_own(info, 0, own, beside, stack)
    fill_wave(info, 0, pieces, half, stack, 4 * half)
    out[...] = masked_products(ids, owners, latent, stack, out.shape[1])


def down_last_kernel(info, ids, owners, latent, earlier, *refs):
    *pieces, out, stack = refs
    half = stack.shape[0] // 4
    fill_wave(info, 0, pieces, half, stack, 0)
    out[...] = earlier[...] + masked_products(ids, owners, latent, stack, out.shape[1])


def base_kernel(info, own, other, weight, _, out, token, weight_ref, sems, *, skip):
    width = own.shape[1]
    place = pl.ds(skip, out.shape[1])
    copies = []
    for part, owner in ((0, info[1]), (1, 1 - info[1])):
        source = pl.ds(pl.multiple_of(owner * width, width), width)
        copies.append(
            pltpu.make_async_copy(weight.at[source, place], weight_ref.at[part], sems.at[part])
        )
    for copy in copies:
        copy.start()
    token[...] = jnp.zeros_like(token)
    copies[0].wait()
    total = jnp.dot(own[...], weight_ref[0], preferred_element_type=jnp.float32)
    copies[1].wait()
    out[...] = total + jnp.dot(other[...], weight_ref[1], preferred_element_type=jnp.float32)


def base(info, latent, other, weight, after, number):
    rows, half_width = latent.shape
    return pl.pallas_call(
        lambda *refs: base_kernel(*refs, skip=number * CHUNK),
        out_shape=[
            jax.ShapeDtypeStruct((rows, CHUNK), jnp.float32),
            TOKEN,
        ],
        in_specs=[SMEM, VMEM, VMEM, ANY, ANY],
        out_specs=[VMEM, VMEM],
        scratch_shapes=[
            pltpu.VMEM((2, half_width, CHUNK), weight.dtype),
            pltpu.SemaphoreType.DMA((2,)),
        ],
        compiler_params=pltpu.CompilerParams(vmem_limit_bytes=BASE_LIMIT * MIB),
        cost_estimate=pl.CostEstimate(
            flops=BASE_COST, bytes_accessed=BASE_COST, transcendentals=0
        ),
    )(info, latent, other, weight, after)


def up_kernel(info, ids, owners, mine, theirs, *refs):
    tiles = refs[-1].shape[0]
    tile = refs[-1].shape[2]
    parts, pieces = refs[:tiles], refs[tiles:-5]
    out, stack, wide, sems, staged = refs[-5:]
    if len(pieces) == 1:
        stack[...] = pieces[0][...]
    else:
        half = pieces[0].shape[0] // 2
        fill_own(info, 1, pieces[0], pieces[1], stack)
        top = 4 * half
        for wave in range(2):
            fill_wave(info, 1, pieces[4 * wave + 2 : 4 * wave + 6], half, stack, top)
            top += pieces[4 * wave + 2].shape[0] * 2
    lowrank = (mine[...] + theirs[...]).astype(jnp.bfloat16)
    zeros = jnp.zeros_like(lowrank)
    width = lowrank.shape[1]
    for lane in range(0, wide.shape[1], width):
        lanes = slice(lane, lane + width)
        wide[:, lanes] = jnp.where(ids[...] == owners[:, lanes], lowrank, zeros)
    copies = []
    for number in range(tiles):
        place = pl.ds(number * tile, tile)
        delta = jnp.dot(wide[...], stack[:, place], preferred_element_type=jnp.float32)
        total = parts[number][...] + delta.astype(jnp.bfloat16).astype(jnp.float32)
        staged[number] = total.astype(out.dtype)
        copies.append(
            pltpu.make_async_copy(staged.at[number], out.at[:, place], sems.at[number])
        )
        copies[-1].start()
    for copy in copies:
        copy.wait()


def on_device(latent, row_adapter_index, shared_weight, adapter_down_weight, adapter_up_weight):
    rows, half_width = latent.shape
    out_width = shared_weight.shape[1]
    local_adapters, _, rank = adapter_down_weight.shape
    shards = lax.axis_size("shard")
    adapters = shards * local_adapters
    columns = adapters * rank
    index, replica = lax.axis_index("shard"), lax.axis_index("replica")
    info = jnp.stack([replica, lax.axis_index("tensor")]).astype(jnp.int32)
    tiles = out_width // CHUNK
    other = swap(latent, "tensor")
    down = jnp.swapaxes(adapter_down_weight, 1, 2).reshape(local_adapters * rank, half_width)
    up = adapter_up_weight.reshape(local_adapters * rank, out_width)
    ids = row_adapter_index
    routed = shards == 8 and local_adapters == 1 and lax.axis_size("replica") == 2
    lowrank = jax.ShapeDtypeStruct((rows, 2 * rank), jnp.float32)
    if routed:
        half = rank // 2
        piece, both = pl.pallas_call(
            lay_out,
            out_shape=[
                jax.ShapeDtypeStruct((rank, half_width), latent.dtype),
                jax.ShapeDtypeStruct((2 * rank, half_width), latent.dtype),
            ],
            in_specs=[ANY, ANY],
            out_specs=[ANY, ANY],
            scratch_shapes=[pltpu.SemaphoreType.DMA((4,))],
            compiler_params=pltpu.CompilerParams(vmem_limit_bytes=LAY_OUT_LIMIT * MIB),
        )(down, up)
        line = {step: along_line(piece, shards, step) for wave in WAVES for step in wave}
        beside = neighbour(both, shards)
        parts = []
        token = info
        for number in range(tiles - 1):
            part, token = base(info, latent, other, shared_weight, token, number)
            parts.append(part)
        held, token = pack([line[step] for step in WAVES[0]], token, beside)
        part, token = base(info, latent, other, shared_weight, token, tiles - 1)
        parts.append(part)
        first, second = in_plane(held, shards, True), in_plane(held, shards, False)
        wave_one = [held, first, second, in_plane(first, shards, False)]
        held, token = pack([line[step] for step in WAVES[1]], token, first)
        first, second = in_plane(held, shards, True), in_plane(held, shards, False)
        wave_two = [held, first, second, in_plane(first, shards, False)]
        owners = jnp.asarray(owner_table(shards, rank))[index][None, :]
        split = 2 * rank * (1 + len(WAVES[0]))
        mine = call(
            down_first_kernel,
            lowrank,
            [SMEM] + [VMEM] * 9 + [ANY],
            16,
            [pltpu.VMEM((split, half_width), latent.dtype)],
        )(info, ids, owners[:, :split], latent, down, beside, *wave_one, token)
        mine = call(
            down_last_kernel,
            lowrank,
            [SMEM] + [VMEM] * 8,
            16,
            [pltpu.VMEM((columns - split, half_width), latent.dtype)],
        )(info, ids, owners[:, split:], latent, mine, *wave_two)
        up_pieces = [up, beside, *wave_one, *wave_two]
    else:
        parts = []
        token = info
        for number in range(tiles):
            part, token = base(info, latent, other, shared_weight, token, number)
            parts.append(part)
        owners = jnp.repeat(jnp.arange(adapters, dtype=jnp.int32), rank)[None, :]
        mine = call(down_whole_kernel, lowrank, [VMEM] * 4, 48)(
            ids, owners, latent, lax.all_gather(down, "shard", axis=0, tiled=True)
        )
        up_pieces = [lax.all_gather(up, "shard", axis=0, tiled=True)]
    theirs = swap(mine, "tensor")

    return pl.pallas_call(
        up_kernel,
        out_shape=jax.ShapeDtypeStruct((rows, out_width), latent.dtype),
        in_specs=[SMEM] + [VMEM] * (4 + tiles + len(up_pieces)),
        out_specs=ANY,
        scratch_shapes=[
            pltpu.VMEM((columns, out_width), latent.dtype),
            pltpu.VMEM((rows, columns), latent.dtype),
            pltpu.SemaphoreType.DMA((tiles,)),
            pltpu.VMEM((tiles, rows, CHUNK), latent.dtype),
        ],
        compiler_params=pltpu.CompilerParams(vmem_limit_bytes=(24 if routed else 56) * MIB),
    )(info, ids, owners, mine, theirs, *parts, *up_pieces)


def solution(mesh):
    return jax.shard_map(
        on_device,
        mesh=mesh,
        in_specs=(
            P(("replica", "shard"), "tensor"),
            P(("replica", "shard"), None),
            P(None, "tensor"),
            P("shard", "tensor", None),
            P("shard", None, "tensor"),
        ),
        out_specs=P(("replica", "shard"), "tensor"),
        check_vma=False,
    )
```

```python
import jax
import jax.numpy as jnp
import numpy as np
from jax import lax
from jax.experimental import pallas as pl
from jax.experimental.pallas import tpu as pltpu
from jax.sharding import PartitionSpec as P

MIB = 1024 * 1024
CHUNK = 512
AXES = ("replica", "shard", "tensor")
WAVES = ((1, 3), (2,))
FIRST_OWNER = 2
SMEM = pl.BlockSpec(memory_space=pltpu.SMEM)
VMEM = pl.BlockSpec(memory_space=pltpu.VMEM)
ANY = pl.BlockSpec(memory_space=pl.ANY)
TOKEN = jax.ShapeDtypeStruct((8, 128), jnp.float32)


def swap(value, axis):
    return lax.ppermute(value, axis, [(0, 1), (1, 0)])


def neighbour(value, shards):
    return lax.ppermute(value, "shard", [(i, i ^ 1) for i in range(shards)])


def along_line(value, shards, step):
    return lax.ppermute(value, "shard", [(i, (i + 2 * step) % shards) for i in range(shards)])


def in_plane(value, shards, first):
    pairs = []
    for r in range(2):
        for s in range(shards):
            for t in range(2):
                to_r, to_s = (r, s ^ 1) if (t == 0) == first else (r ^ 1, s)
                pairs.append(((r * shards + s) * 2 + t, (to_r * shards + to_s) * 2 + t))
    return lax.ppermute(value, AXES, pairs)


def call(kernel, out_shape, in_specs, limit, scratch=(), flops=0, moved=0):
    return pl.pallas_call(
        kernel,
        out_shape=out_shape,
        in_specs=in_specs,
        out_specs=jax.tree.map(lambda _: VMEM, out_shape),
        scratch_shapes=list(scratch),
        compiler_params=pltpu.CompilerParams(vmem_limit_bytes=limit * MIB),
        cost_estimate=pl.CostEstimate(flops=flops, bytes_accessed=moved, transcendentals=0),
    )


def owner_row(info, begin, count, rank):
    block = (lax.broadcasted_iota(jnp.int32, (1, count), 1) + begin) // rank
    row = jnp.zeros((1, count), jnp.int32)
    for number in range(begin // rank, (begin + count) // rank):
        row = jnp.where(block == number, info[FIRST_OWNER + number], row)
    return row


def pack(pieces, *after):
    rows, width = pieces[0].shape
    count = len(pieces)

    def kernel(*refs):
        out, token = refs[-2:]
        for number in range(count):
            out[number * rows : (number + 1) * rows, :] = refs[number][...]
        token[...] = jnp.zeros_like(token)

    return call(
        kernel,
        [jax.ShapeDtypeStruct((count * rows, width), pieces[0].dtype), TOKEN],
        [VMEM] * count + [ANY] * len(after),
        4,
    )(*pieces, *after)


def fill_wave(info, holds, pieces, stack, top, rank):
    line, first, second, corner = pieces

    def put(here, beside):
        for number in range(line.shape[0] // rank):
            rows = slice(number * rank, (number + 1) * rank)
            place = top + 2 * number * rank
            stack[place : place + rank, :] = here[rows, :]
            stack[place + rank : place + 2 * rank, :] = beside[rows, :]

    for core in range(2):
        next_line, next_replica = (first, second) if core == 0 else (second, first)
        at_core = info[0] == core
        pl.when(at_core & holds)(lambda b=next_line: put(line, b))
        pl.when(at_core & jnp.logical_not(holds))(lambda h=next_replica: put(h, corner))


def masked_products(info, ids, latent, stack, begin, rank):
    total = None
    width = 2 * rank
    for skip in range(0, stack.shape[0], CHUNK):
        count = min(CHUNK, stack.shape[0] - skip)
        part = lax.dot_general(
            latent[...],
            stack[skip : skip + count, :],
            (((1,), (1,)), ((), ())),
            preferred_element_type=jnp.float32,
        )
        mask = ids[...] == owner_row(info, begin + skip, count, rank)
        part = jnp.where(mask, part, 0.0)
        for lane in range(0, count, width):
            fold = part[:, lane : lane + width]
            total = fold if total is None else total + fold
    return total


def down_whole_kernel(info, ids, latent, stack, out):
    out[...] = masked_products(info, ids, latent, stack, 0, out.shape[1] // 2)


def down_first_kernel(info, ids, latent, own, beside, *refs):
    *pieces, _, out, stack = refs
    rank = own.shape[0]
    stack[0:rank, :] = own[...]
    stack[rank : 2 * rank, :] = beside[...]
    fill_wave(info, info[1] == 1, pieces, stack, 2 * rank, rank)
    out[...] = masked_products(info, ids, latent, stack, 0, rank)


def down_last_kernel(info, ids, latent, earlier, *refs, begin):
    *pieces, out, stack = refs
    rank = out.shape[1] // 2
    fill_wave(info, info[1] == 1, pieces, stack, 0, rank)
    out[...] = earlier[...] + masked_products(info, ids, latent, stack, begin, rank)


def base_kernel(info, own, other, weight, _, out, token, *, skip):
    token[...] = jnp.zeros_like(token)
    width = own.shape[1]
    mine = pl.ds(pl.multiple_of(info[0] * width, width), width)
    rest = pl.ds(pl.multiple_of((1 - info[0]) * width, width), width)
    for begin in range(0, out.shape[1], CHUNK):
        place = slice(begin, begin + CHUNK)
        source = slice(skip + begin, skip + begin + CHUNK)
        out[:, place] = jnp.dot(
            own[...], weight[mine, source], preferred_element_type=jnp.float32
        ) + jnp.dot(other[...], weight[rest, source], preferred_element_type=jnp.float32)


def base(info, latent, other, weight, after, skip, columns):
    rows, half_width = latent.shape
    return pl.pallas_call(
        lambda *refs: base_kernel(*refs, skip=skip),
        out_shape=[jax.ShapeDtypeStruct((rows, columns), jnp.float32), TOKEN],
        in_specs=[SMEM, VMEM, VMEM, VMEM, ANY],
        out_specs=[VMEM, VMEM],
        compiler_params=pltpu.CompilerParams(vmem_limit_bytes=24 * MIB),
        cost_estimate=pl.CostEstimate(flops=1000, bytes_accessed=1000, transcendentals=0),
    )(info, latent, other, weight, after)


def up_kernel(info, ids, mine, theirs, left, right, *refs):
    *pieces, out, stack, wide, sems, staged = refs
    rank = mine.shape[1] // 2
    if len(pieces) == 1:
        stack[...] = pieces[0][...]
    else:
        stack[0:rank, :] = pieces[0][...]
        stack[rank : 2 * rank, :] = pieces[1][...]
        top = 2 * rank
        for wave in range(2):
            received = pieces[4 * wave + 2 : 4 * wave + 6]
            fill_wave(info, info[1] == 0, received, stack, top, rank)
            top += received[0].shape[0] * 2
    lowrank = (mine[...] + theirs[...]).astype(jnp.bfloat16)
    zeros = jnp.zeros_like(lowrank)
    width = 2 * rank
    for lane in range(0, wide.shape[1], width):
        mask = ids[...] == owner_row(info, lane, width, rank)
        wide[:, lane : lane + width] = jnp.where(mask, lowrank, zeros)
    copies = []
    tiles, _, tile = staged.shape
    for number in range(tiles):
        place = pl.ds(number * tile, tile)
        delta = jnp.dot(wide[...], stack[:, place], preferred_element_type=jnp.float32)
        begin = number * tile
        if begin < left.shape[1]:
            part = left[:, begin : begin + tile]
        else:
            begin -= left.shape[1]
            part = right[:, begin : begin + tile]
        total = part + delta.astype(jnp.bfloat16).astype(jnp.float32)
        staged[number] = total.astype(out.dtype)
        copies.append(
            pltpu.make_async_copy(staged.at[number], out.at[:, place], sems.at[number])
        )
        copies[-1].start()
    for copy in copies:
        copy.wait()


def on_device(latent, row_adapter_index, shared_weight, adapter_down_weight, adapter_up_weight):
    rows, half_width = latent.shape
    out_width = shared_weight.shape[1]
    local_adapters, _, rank = adapter_down_weight.shape
    shards = lax.axis_size("shard")
    adapters = shards * local_adapters
    columns = adapters * rank
    index, core = lax.axis_index("shard"), lax.axis_index("tensor")
    holds_down = core == lax.axis_index("replica")
    tiles = out_width // CHUNK
    cut = 2 * tiles // 3 * CHUNK
    down = jnp.swapaxes(adapter_down_weight, 1, 2).reshape(local_adapters * rank, half_width)
    up = adapter_up_weight.reshape(local_adapters * rank, out_width)
    ids = row_adapter_index
    routed = shards == 8 and local_adapters == 1 and lax.axis_size("replica") == 2
    routed = routed and half_width == out_width
    lowrank = jax.ShapeDtypeStruct((rows, 2 * rank), jnp.float32)
    if routed:
        sources = [(index - 2 * step) % shards for step in (0, *WAVES[0], *WAVES[1])]
        owners = [a for source in sources for a in (source, source ^ 1)]
    else:
        owners = list(range(adapters))
    info = jnp.stack([jnp.asarray(v, jnp.int32) for v in (core, holds_down, *owners)])
    if routed:
        piece = jnp.where(holds_down, down, up)
        line = {step: along_line(piece, shards, step) for wave in WAVES for step in wave}
        other = swap(latent, "tensor")
        down_beside, up_beside = neighbour(down, shards), neighbour(up, shards)
        left, token = base(info, latent, other, shared_weight, info, 0, cut)
        held, token = pack([line[step] for step in WAVES[0]], token, down_beside, up_beside)
        right, token = base(info, latent, other, shared_weight, token, cut, out_width - cut)
        first, second = in_plane(held, shards, True), in_plane(held, shards, False)
        wave_one = [held, first, second, in_plane(first, shards, False)]
        held, token = pack([line[step] for step in WAVES[1]], token, first)
        first, second = in_plane(held, shards, True), in_plane(held, shards, False)
        wave_two = [held, first, second, in_plane(first, shards, False)]
        split = 2 * rank * (1 + len(WAVES[0]))
        mine = call(
            down_first_kernel,
            lowrank,
            [SMEM] + [VMEM] * 8 + [ANY],
            16,
            [pltpu.VMEM((split, half_width), latent.dtype)],
        )(info, ids, latent, down, down_beside, *wave_one, token)
        mine = call(
            lambda *refs: down_last_kernel(*refs, begin=split),
            lowrank,
            [SMEM] + [VMEM] * 7,
            16,
            [pltpu.VMEM((columns - split, half_width), latent.dtype)],
        )(info, ids, latent, mine, *wave_two)
        up_pieces = [up, up_beside, *wave_one, *wave_two]
    else:
        other = swap(latent, "tensor")
        left, token = base(info, latent, other, shared_weight, info, 0, cut)
        right, token = base(info, latent, other, shared_weight, token, cut, out_width - cut)
        mine = call(down_whole_kernel, lowrank, [SMEM] + [VMEM] * 3, 48)(
            info, ids, latent, lax.all_gather(down, "shard", axis=0, tiled=True)
        )
        up_pieces = [lax.all_gather(up, "shard", axis=0, tiled=True)]
    theirs = swap(mine, "tensor")

    return pl.pallas_call(
        up_kernel,
        out_shape=jax.ShapeDtypeStruct((rows, out_width), latent.dtype),
        in_specs=[SMEM] + [VMEM] * (5 + len(up_pieces)),
        out_specs=ANY,
        scratch_shapes=[
            pltpu.VMEM((columns, out_width), latent.dtype),
            pltpu.VMEM((rows, columns), latent.dtype),
            pltpu.SemaphoreType.DMA((tiles,)),
            pltpu.VMEM((tiles, rows, CHUNK), latent.dtype),
        ],
        compiler_params=pltpu.CompilerParams(vmem_limit_bytes=(24 if routed else 56) * MIB),
    )(info, ids, mine, theirs, left, right, *up_pieces)


def solution(mesh):
    return jax.shard_map(
        on_device,
        mesh=mesh,
        in_specs=(
            P(("replica", "shard"), "tensor"),
            P(("replica", "shard"), None),
            P(None, "tensor"),
            P("shard", "tensor", None),
            P("shard", None, "tensor"),
        ),
        out_specs=P(("replica", "shard"), "tensor"),
        check_vma=False,
    )
```

```python
import jax
import jax.numpy as jnp
import numpy as np
from jax import lax
from jax.experimental import pallas as pl
from jax.experimental.pallas import tpu as pltpu
from jax.sharding import PartitionSpec as P

MIB = 1024 * 1024
CHUNK = 512
AXES = ("replica", "shard", "tensor")
WAVES = ((1, 3), (2,))
FIRST_OWNER = 2
SMEM = pl.BlockSpec(memory_space=pltpu.SMEM)
VMEM = pl.BlockSpec(memory_space=pltpu.VMEM)
ANY = pl.BlockSpec(memory_space=pl.ANY)
TOKEN = jax.ShapeDtypeStruct((8, 128), jnp.float32)


def swap(value, axis):
    return lax.ppermute(value, axis, [(0, 1), (1, 0)])


def neighbour(value, shards):
    return lax.ppermute(value, "shard", [(i, i ^ 1) for i in range(shards)])


def along_line(value, shards, step):
    return lax.ppermute(value, "shard", [(i, (i + 2 * step) % shards) for i in range(shards)])


def in_plane(value, shards, first):
    pairs = []
    for r in range(2):
        for s in range(shards):
            for t in range(2):
                to_r, to_s = (r, s ^ 1) if (t == 0) == first else (r ^ 1, s)
                pairs.append(((r * shards + s) * 2 + t, (to_r * shards + to_s) * 2 + t))
    return lax.ppermute(value, AXES, pairs)


def call(kernel, out_shape, in_specs, limit, scratch=(), flops=0, moved=0):
    return pl.pallas_call(
        kernel,
        out_shape=out_shape,
        in_specs=in_specs,
        out_specs=jax.tree.map(lambda _: VMEM, out_shape),
        scratch_shapes=list(scratch),
        compiler_params=pltpu.CompilerParams(vmem_limit_bytes=limit * MIB),
        cost_estimate=pl.CostEstimate(flops=flops, bytes_accessed=moved, transcendentals=0),
    )


def owner_row(info, begin, count, rank):
    block = (lax.broadcasted_iota(jnp.int32, (1, count), 1) + begin) // rank
    row = jnp.zeros((1, count), jnp.int32)
    for number in range(begin // rank, (begin + count) // rank):
        row = jnp.where(block == number, info[FIRST_OWNER + number], row)
    return row


def pack(pieces, *after):
    rows, width = pieces[0].shape
    count = len(pieces)

    def kernel(*refs):
        out, token = refs[-2:]
        for number in range(count):
            out[number * rows : (number + 1) * rows, :] = refs[number][...]
        token[...] = jnp.zeros_like(token)

    return call(
        kernel,
        [jax.ShapeDtypeStruct((count * rows, width), pieces[0].dtype), TOKEN],
        [VMEM] * count + [ANY] * len(after),
        4,
    )(*pieces, *after)


def fill_wave(info, holds, pieces, stack, top, rank):
    line, first, second, corner = pieces

    def put(here, beside):
        for number in range(line.shape[0] // rank):
            rows = slice(number * rank, (number + 1) * rank)
            place = top + 2 * number * rank
            stack[place : place + rank, :] = here[rows, :]
            stack[place + rank : place + 2 * rank, :] = beside[rows, :]

    for core in range(2):
        next_line, next_replica = (first, second) if core == 0 else (second, first)
        at_core = info[0] == core
        pl.when(at_core & holds)(lambda b=next_line: put(line, b))
        pl.when(at_core & jnp.logical_not(holds))(lambda h=next_replica: put(h, corner))


def masked_products(info, ids, latent, stack, begin, rank):
    total = None
    width = 2 * rank
    for skip in range(0, stack.shape[0], CHUNK):
        count = min(CHUNK, stack.shape[0] - skip)
        part = lax.dot_general(
            latent[...],
            stack[skip : skip + count, :],
            (((1,), (1,)), ((), ())),
            preferred_element_type=jnp.float32,
        )
        mask = ids[...] == owner_row(info, begin + skip, count, rank)
        part = jnp.where(mask, part, 0.0)
        for lane in range(0, count, width):
            fold = part[:, lane : lane + width]
            total = fold if total is None else total + fold
    return total


def down_whole_kernel(info, ids, latent, stack, out):
    out[...] = masked_products(info, ids, latent, stack, 0, out.shape[1] // 2)


def down_first_kernel(info, ids, latent, own, beside, *refs):
    *pieces, _, out, stack = refs
    rank = own.shape[0]
    stack[0:rank, :] = own[...]
    stack[rank : 2 * rank, :] = beside[...]
    fill_wave(info, info[1] == 1, pieces, stack, 2 * rank, rank)
    out[...] = masked_products(info, ids, latent, stack, 0, rank)


def down_last_kernel(info, ids, latent, earlier, *refs, begin):
    *pieces, out, stack = refs
    rank = out.shape[1] // 2
    fill_wave(info, info[1] == 1, pieces, stack, 0, rank)
    out[...] = earlier[...] + masked_products(info, ids, latent, stack, begin, rank)


def base_kernel(info, own, other, weight, *refs, skip):
    out, token = refs[-2:]
    token[...] = jnp.zeros_like(token)
    width = own.shape[1]
    mine = pl.ds(pl.multiple_of(info[0] * width, width), width)
    rest = pl.ds(pl.multiple_of((1 - info[0]) * width, width), width)
    for begin in range(0, out.shape[1], CHUNK):
        place = slice(begin, begin + CHUNK)
        source = slice(skip + begin, skip + begin + CHUNK)
        out[:, place] = jnp.dot(
            own[...], weight[mine, source], preferred_element_type=jnp.float32
        ) + jnp.dot(other[...], weight[rest, source], preferred_element_type=jnp.float32)


def base(info, latent, other, weight, after, skip, columns):
    rows, half_width = latent.shape
    return pl.pallas_call(
        lambda *refs: base_kernel(*refs, skip=skip),
        out_shape=[jax.ShapeDtypeStruct((rows, columns), jnp.float32), TOKEN],
        in_specs=[SMEM, VMEM, VMEM, VMEM] + [ANY] * len(after),
        out_specs=[VMEM, VMEM],
        compiler_params=pltpu.CompilerParams(vmem_limit_bytes=24 * MIB),
        cost_estimate=pl.CostEstimate(flops=1000, bytes_accessed=1000, transcendentals=0),
    )(info, latent, other, weight, *after)


def up_kernel(info, ids, mine, theirs, left, right, *refs):
    *pieces, out, stack, wide, sems, staged = refs
    rank = mine.shape[1] // 2
    if len(pieces) == 1:
        stack[...] = pieces[0][...]
    else:
        stack[0:rank, :] = pieces[0][...]
        stack[rank : 2 * rank, :] = pieces[1][...]
        top = 2 * rank
        for wave in range(2):
            received = pieces[4 * wave + 2 : 4 * wave + 6]
            fill_wave(info, info[1] == 0, received, stack, top, rank)
            top += received[0].shape[0] * 2
    lowrank = (mine[...] + theirs[...]).astype(jnp.bfloat16)
    zeros = jnp.zeros_like(lowrank)
    width = 2 * rank
    for lane in range(0, wide.shape[1], width):
        mask = ids[...] == owner_row(info, lane, width, rank)
        wide[:, lane : lane + width] = jnp.where(mask, lowrank, zeros)
    copies = []
    tiles, _, tile = staged.shape
    for number in range(tiles):
        place = pl.ds(number * tile, tile)
        delta = jnp.dot(wide[...], stack[:, place], preferred_element_type=jnp.float32)
        begin = number * tile
        if begin < left.shape[1]:
            part = left[:, begin : begin + tile]
        else:
            begin -= left.shape[1]
            part = right[:, begin : begin + tile]
        total = part + delta.astype(jnp.bfloat16).astype(jnp.float32)
        staged[number] = total.astype(out.dtype)
        copies.append(
            pltpu.make_async_copy(staged.at[number], out.at[:, place], sems.at[number])
        )
        copies[-1].start()
    for copy in copies:
        copy.wait()


def on_device(latent, row_adapter_index, shared_weight, adapter_down_weight, adapter_up_weight):
    rows, half_width = latent.shape
    out_width = shared_weight.shape[1]
    local_adapters, _, rank = adapter_down_weight.shape
    shards = lax.axis_size("shard")
    adapters = shards * local_adapters
    columns = adapters * rank
    index, core = lax.axis_index("shard"), lax.axis_index("tensor")
    holds_down = core == lax.axis_index("replica")
    tiles = out_width // CHUNK
    cut = tiles // 3 * CHUNK
    down = jnp.swapaxes(adapter_down_weight, 1, 2).reshape(local_adapters * rank, half_width)
    up = adapter_up_weight.reshape(local_adapters * rank, out_width)
    ids = row_adapter_index
    routed = shards == 8 and local_adapters == 1 and lax.axis_size("replica") == 2
    routed = routed and half_width == out_width
    lowrank = jax.ShapeDtypeStruct((rows, 2 * rank), jnp.float32)
    if routed:
        sources = [(index - 2 * step) % shards for step in (0, *WAVES[0], *WAVES[1])]
        owners = [a for source in sources for a in (source, source ^ 1)]
    else:
        owners = list(range(adapters))
    info = jnp.stack([jnp.asarray(v, jnp.int32) for v in (core, holds_down, *owners)])
    if routed:
        piece = jnp.where(holds_down, down, up)
        line = {step: along_line(piece, shards, step) for wave in WAVES for step in wave}
        other = swap(latent, "tensor")
        down_beside, up_beside = neighbour(down, shards), neighbour(up, shards)
        left, token = base(info, latent, other, shared_weight, [ids], 0, cut)
        held, token = pack([line[step] for step in WAVES[0]], token, down_beside, up_beside)
        right, token = base(info, latent, other, shared_weight, [token], cut, out_width - cut)
        first, second = in_plane(held, shards, True), in_plane(held, shards, False)
        wave_one = [held, first, second, in_plane(first, shards, False)]
        held, token = pack([line[step] for step in WAVES[1]], token, first)
        first, second = in_plane(held, shards, True), in_plane(held, shards, False)
        wave_two = [held, first, second, in_plane(first, shards, False)]
        split = 2 * rank * (1 + len(WAVES[0]))
        mine = call(
            down_first_kernel,
            lowrank,
            [SMEM] + [VMEM] * 8 + [ANY],
            16,
            [pltpu.VMEM((split, half_width), latent.dtype)],
        )(info, ids, latent, down, down_beside, *wave_one, token)
        mine = call(
            lambda *refs: down_last_kernel(*refs, begin=split),
            lowrank,
            [SMEM] + [VMEM] * 7,
            16,
            [pltpu.VMEM((columns - split, half_width), latent.dtype)],
        )(info, ids, latent, mine, *wave_two)
        up_pieces = [up, up_beside, *wave_one, *wave_two]
    else:
        other = swap(latent, "tensor")
        left, token = base(info, latent, other, shared_weight, [ids], 0, cut)
        right, token = base(info, latent, other, shared_weight, [token], cut, out_width - cut)
        mine = call(down_whole_kernel, lowrank, [SMEM] + [VMEM] * 3, 48)(
            info, ids, latent, lax.all_gather(down, "shard", axis=0, tiled=True)
        )
        up_pieces = [lax.all_gather(up, "shard", axis=0, tiled=True)]
    theirs = swap(mine, "tensor")

    return pl.pallas_call(
        up_kernel,
        out_shape=jax.ShapeDtypeStruct((rows, out_width), latent.dtype),
        in_specs=[SMEM] + [VMEM] * (5 + len(up_pieces)),
        out_specs=ANY,
        scratch_shapes=[
            pltpu.VMEM((columns, out_width), latent.dtype),
            pltpu.VMEM((rows, columns), latent.dtype),
            pltpu.SemaphoreType.DMA((tiles,)),
            pltpu.VMEM((tiles, rows, CHUNK), latent.dtype),
        ],
        compiler_params=pltpu.CompilerParams(vmem_limit_bytes=(24 if routed else 56) * MIB),
    )(info, ids, mine, theirs, left, right, *up_pieces)


def solution(mesh):
    return jax.shard_map(
        on_device,
        mesh=mesh,
        in_specs=(
            P(("replica", "shard"), "tensor"),
            P(("replica", "shard"), None),
            P(None, "tensor"),
            P("shard", "tensor", None),
            P("shard", None, "tensor"),
        ),
        out_specs=P(("replica", "shard"), "tensor"),
        check_vma=False,
    )
```

```python
import jax
import jax.numpy as jnp
import numpy as np
from jax import lax
from jax.experimental import pallas as pl
from jax.experimental.pallas import tpu as pltpu
from jax.sharding import PartitionSpec as P

MIB = 1024 * 1024
CHUNK = 512
AXES = ("replica", "shard", "tensor")
FIRST_OWNER = 2
SMEM = pl.BlockSpec(memory_space=pltpu.SMEM)
VMEM = pl.BlockSpec(memory_space=pltpu.VMEM)
ANY = pl.BlockSpec(memory_space=pl.ANY)
TOKEN = jax.ShapeDtypeStruct((8, 128), jnp.float32)


def swap(value, axis):
    return lax.ppermute(value, axis, [(0, 1), (1, 0)])


def neighbour(value, shards):
    return lax.ppermute(value, "shard", [(i, i ^ 1) for i in range(shards)])


def along_line(value, shards, step):
    return lax.ppermute(value, "shard", [(i, (i + 2 * step) % shards) for i in range(shards)])


def in_plane(value, shards, first):
    pairs = []
    for r in range(2):
        for s in range(shards):
            for t in range(2):
                to_r, to_s = (r, s ^ 1) if (t == 0) == first else (r ^ 1, s)
                pairs.append(((r * shards + s) * 2 + t, (to_r * shards + to_s) * 2 + t))
    return lax.ppermute(value, AXES, pairs)


def call(kernel, out_shape, in_specs, limit, scratch=(), flops=0, moved=0):
    return pl.pallas_call(
        kernel,
        out_shape=out_shape,
        in_specs=in_specs,
        out_specs=jax.tree.map(lambda _: VMEM, out_shape),
        scratch_shapes=list(scratch),
        compiler_params=pltpu.CompilerParams(vmem_limit_bytes=limit * MIB),
        cost_estimate=pl.CostEstimate(flops=flops, bytes_accessed=moved, transcendentals=0),
    )


def owner_row(info, blocks, rank):
    place = lax.broadcasted_iota(jnp.int32, (1, len(blocks) * rank), 1) // rank
    row = jnp.full(place.shape, -1, jnp.int32)
    for number, block in enumerate(blocks):
        if block is not None:
            row = jnp.where(place == number, info[FIRST_OWNER + block], row)
    return row


def pack(pieces, *after):
    count = len(pieces)
    total = sum(rows for _, _, rows in pieces)
    width, dtype = pieces[0][0].shape[1], pieces[0][0].dtype

    def kernel(*refs):
        out, token = refs[-2:]
        top = 0
        for ref, (_, begin, rows) in zip(refs, pieces):
            out[top : top + rows, :] = ref[begin : begin + rows, :]
            top += rows
        token[...] = jnp.zeros_like(token)

    return call(
        kernel,
        [jax.ShapeDtypeStruct((total, width), dtype), TOKEN],
        [VMEM] * count + [ANY] * len(after),
        4,
    )(*[array for array, _, _ in pieces], *after)


def put(blocks, stack, top, rank):
    for number, parts in enumerate(blocks):
        place = top + 2 * number * rank
        for ref, begin, rows in parts:
            stack[place : place + rows, :] = ref[begin : begin + rows, :]
            place += rows


def fill_here(info, holds, received, stack, top, rank):
    early, early_first, early_second, late, late_first, late_second, _, _ = received

    def blocks(pair, single):
        return [[(pair, 0, rank)], [(pair, rank, rank)], [(single, 0, rank)]]

    swapped = ((early_second, late_second), (early_first, late_first))
    pl.when(holds)(lambda: put(blocks(early, late), stack, top, rank))
    for core in range(2):
        away = jnp.logical_not(holds) & (info[0] == core)
        pl.when(away)(lambda refs=swapped[core]: put(blocks(*refs), stack, top, rank))


def fill_beside(info, holds, received, stack, top, rank, direct=True, corner=True):
    _, early_first, early_second, _, late_first, late_second, corner_one, corner_two = received
    half = rank // 2
    swapped = ((early_first, late_first), (early_second, late_second))
    if direct:
        for core in range(2):

            def straight(refs=swapped[core]):
                pair, single = refs
                blocks = [[(pair, 0, rank)], [(pair, rank, rank)], [(single, 0, rank)]]
                put(blocks, stack, top, rank)

            pl.when(holds & (info[0] == core))(straight)
    if corner:

        def turned():
            last = [(corner_one, rank, half), (corner_two, rank, half)]
            put([[(corner_one, 0, rank)], [(corner_two, 0, rank)], last], stack, top, rank)

        pl.when(jnp.logical_not(holds))(turned)


def clear(stack, top, rank, count):
    for number in range(count):
        place = top + 2 * number * rank
        stack[place : place + rank, :] = jnp.zeros((rank, stack.shape[1]), stack.dtype)


def masked_products(info, ids, latent, stack, blocks, rank):
    total = None
    width = 2 * rank
    for skip in range(0, stack.shape[0], CHUNK):
        count = min(CHUNK, stack.shape[0] - skip)
        part = lax.dot_general(
            latent[...],
            stack[skip : skip + count, :],
            (((1,), (1,)), ((), ())),
            preferred_element_type=jnp.float32,
        )
        owners = owner_row(info, blocks[skip // rank : (skip + count) // rank], rank)
        part = jnp.where(ids[...] == owners, part, 0.0)
        for lane in range(0, count, width):
            fold = part[:, lane : lane + width]
            total = fold if total is None else total + fold
    return total


def down_whole_kernel(info, ids, latent, stack, out):
    rank = out.shape[1] // 2
    blocks = range(stack.shape[0] // rank)
    out[...] = masked_products(info, ids, latent, stack, blocks, rank)


def down_first_kernel(info, ids, latent, own, beside, *refs):
    *received, _, out, stack = refs
    rank = own.shape[0]
    holds = info[1] == 1
    stack[0:rank, :] = own[...]
    stack[rank : 2 * rank, :] = beside[...]
    fill_here(info, holds, (*received, None, None), stack, 2 * rank, rank)
    fill_beside(info, holds, (*received, None, None), stack, 3 * rank, rank, corner=False)
    pl.when(jnp.logical_not(holds))(lambda: clear(stack, 3 * rank, rank, 3))
    out[...] = masked_products(info, ids, latent, stack, range(stack.shape[0] // rank), rank)


def down_last_kernel(info, ids, latent, earlier, corner_one, corner_two, out, stack):
    rank = out.shape[1] // 2
    half = rank // 2
    holds = info[1] == 1

    @pl.when(holds)
    def _():
        out[...] = earlier[...]

    @pl.when(jnp.logical_not(holds))
    def _():
        stack[0:rank, :] = corner_one[0:rank, :]
        stack[rank : 2 * rank, :] = corner_two[0:rank, :]
        stack[2 * rank : 2 * rank + half, :] = corner_one[rank : rank + half, :]
        stack[2 * rank + half : 3 * rank, :] = corner_two[rank : rank + half, :]
        stack[3 * rank : 4 * rank, :] = jnp.zeros((rank, stack.shape[1]), stack.dtype)
        pair = masked_products(info, ids, latent, stack, (3, 5, 7, None), rank)
        fold = pair[:, :rank] + pair[:, rank:]
        out[...] = earlier[...] + jnp.concatenate([jnp.zeros_like(fold), fold], axis=1)


def base_kernel(info, own, other, weight, *refs, skip):
    out, token = refs[-2:]
    token[...] = jnp.zeros_like(token)
    width = own.shape[1]
    mine = pl.ds(pl.multiple_of(info[0] * width, width), width)
    rest = pl.ds(pl.multiple_of((1 - info[0]) * width, width), width)
    for begin in range(0, out.shape[1], CHUNK):
        place = slice(begin, begin + CHUNK)
        source = slice(skip + begin, skip + begin + CHUNK)
        out[:, place] = jnp.dot(
            own[...], weight[mine, source], preferred_element_type=jnp.float32
        ) + jnp.dot(other[...], weight[rest, source], preferred_element_type=jnp.float32)


def base(info, latent, other, weight, after, skip, end):
    rows, columns = latent.shape[0], end - skip
    return pl.pallas_call(
        lambda *refs: base_kernel(*refs, skip=skip),
        out_shape=[jax.ShapeDtypeStruct((rows, columns), jnp.float32), TOKEN],
        in_specs=[SMEM, VMEM, VMEM, VMEM] + [ANY] * len(after),
        out_specs=[VMEM, VMEM],
        compiler_params=pltpu.CompilerParams(vmem_limit_bytes=24 * MIB),
        cost_estimate=pl.CostEstimate(flops=1000, bytes_accessed=1000, transcendentals=0),
    )(info, latent, other, weight, *after)


def up_kernel(info, ids, mine, theirs, *refs, base_parts):
    *pieces, out, stack, wide, sems, staged = refs[base_parts:]
    bases = [
        part.at[:, pl.ds(begin, CHUNK)]
        for part in refs[:base_parts]
        for begin in range(0, part.shape[1], CHUNK)
    ]
    rank = mine.shape[1] // 2
    if len(pieces) == 1:
        stack[...] = pieces[0][...]
    else:
        own, beside, *received = pieces
        holds = info[1] == 0
        stack[0:rank, :] = own[...]
        stack[rank : 2 * rank, :] = beside[...]
        fill_here(info, holds, received, stack, 2 * rank, rank)
        fill_beside(info, holds, received, stack, 3 * rank, rank)
    lowrank = (mine[...] + theirs[...]).astype(jnp.bfloat16)
    zeros = jnp.zeros_like(lowrank)
    width = 2 * rank
    for lane in range(0, wide.shape[1], width):
        mask = ids[...] == owner_row(info, (lane // rank, lane // rank + 1), rank)
        wide[:, lane : lane + width] = jnp.where(mask, lowrank, zeros)
    copies = []
    tiles, _, tile = staged.shape
    for number in range(tiles):
        place = pl.ds(number * tile, tile)
        delta = jnp.dot(wide[...], stack[:, place], preferred_element_type=jnp.float32)
        total = bases[number][...] + delta.astype(jnp.bfloat16).astype(jnp.float32)
        staged[number] = total.astype(out.dtype)
        copies.append(
            pltpu.make_async_copy(staged.at[number], out.at[:, place], sems.at[number])
        )
        copies[-1].start()
    for copy in copies:
        copy.wait()


def on_device(latent, row_adapter_index, shared_weight, adapter_down_weight, adapter_up_weight):
    rows, half_width = latent.shape
    out_width = shared_weight.shape[1]
    local_adapters, _, rank = adapter_down_weight.shape
    shards = lax.axis_size("shard")
    adapters = shards * local_adapters
    columns = adapters * rank
    index, core = lax.axis_index("shard"), lax.axis_index("tensor")
    holds_down = core == lax.axis_index("replica")
    tiles = out_width // CHUNK
    cuts = [tiles * number // 3 * CHUNK for number in range(4)]
    down = jnp.swapaxes(adapter_down_weight, 1, 2).reshape(local_adapters * rank, half_width)
    up = adapter_up_weight.reshape(local_adapters * rank, out_width)
    ids = row_adapter_index
    routed = shards == 8 and local_adapters == 1 and lax.axis_size("replica") == 2
    routed = routed and half_width == out_width and tiles % 3 == 0
    lowrank = jax.ShapeDtypeStruct((rows, 2 * rank), jnp.float32)
    if routed:
        sources = [(index - 2 * step) % shards for step in (0, 1, 3, 2)]
        owners = [a for source in sources for a in (source, source ^ 1)]
    else:
        owners = list(range(adapters))
    info = jnp.stack([jnp.asarray(v, jnp.int32) for v in (core, holds_down, *owners)])
    if routed:
        piece = jnp.where(holds_down, down, up)
        line = {step: along_line(piece, shards, step) for step in (1, 3)}
        other = swap(latent, "tensor")
        down_beside, up_beside = neighbour(down, shards), neighbour(up, shards)
        parts = []
        part, token = base(info, latent, other, shared_weight, [ids], cuts[0], cuts[1])
        parts.append(part)
        relay, token = pack([(line[1], 0, rank)], token)
        line[2] = along_line(relay, shards, 1)
        early, token = pack([(line[1], 0, rank), (line[3], 0, rank)], token, down_beside, up_beside)
        part, token = base(info, latent, other, shared_weight, [token], cuts[1], cuts[2])
        parts.append(part)
        early_first, early_second = in_plane(early, shards, True), in_plane(early, shards, False)
        late, token = pack([(line[2], 0, rank)], token)
        part, token = base(info, latent, other, shared_weight, [token], cuts[2], cuts[3])
        parts.append(part)
        late_first, late_second = in_plane(late, shards, True), in_plane(late, shards, False)
        half = rank // 2
        turn_one, token = pack([(early_first, 0, rank), (late_first, 0, half)], token)
        turn_two, token = pack([(early_second, rank, rank), (late_second, half, half)], token)
        corner_one = in_plane(turn_one, shards, False)
        corner_two = in_plane(turn_two, shards, True)
        received = [early, early_first, early_second, late, late_first, late_second]
        mine = call(
            down_first_kernel,
            lowrank,
            [SMEM] + [VMEM] * 10 + [ANY],
            16,
            [pltpu.VMEM((columns, half_width), latent.dtype)],
        )(info, ids, latent, down, down_beside, *received, token)
        mine = call(
            down_last_kernel,
            lowrank,
            [SMEM] + [VMEM] * 5,
            16,
            [pltpu.VMEM((4 * rank, half_width), latent.dtype)],
        )(info, ids, latent, mine, corner_one, corner_two)
        up_pieces = [up, up_beside, *received, corner_one, corner_two]
    else:
        other = swap(latent, "tensor")
        parts, token = [], ids
        for begin, end in zip(cuts[:-1], cuts[1:]):
            part, token = base(info, latent, other, shared_weight, [token], begin, end)
            parts.append(part)
        mine = call(down_whole_kernel, lowrank, [SMEM] + [VMEM] * 3, 48)(
            info, ids, latent, lax.all_gather(down, "shard", axis=0, tiled=True)
        )
        up_pieces = [lax.all_gather(up, "shard", axis=0, tiled=True)]
    theirs = swap(mine, "tensor")

    return pl.pallas_call(
        lambda *refs: up_kernel(*refs, base_parts=len(parts)),
        out_shape=jax.ShapeDtypeStruct((rows, out_width), latent.dtype),
        in_specs=[SMEM] + [VMEM] * (3 + len(parts) + len(up_pieces)),
        out_specs=ANY,
        scratch_shapes=[
            pltpu.VMEM((columns, out_width), latent.dtype),
            pltpu.VMEM((rows, columns), latent.dtype),
            pltpu.SemaphoreType.DMA((tiles,)),
            pltpu.VMEM((tiles, rows, CHUNK), latent.dtype),
        ],
        compiler_params=pltpu.CompilerParams(vmem_limit_bytes=(24 if routed else 56) * MIB),
    )(info, ids, mine, theirs, *parts, *up_pieces)


def solution(mesh):
    return jax.shard_map(
        on_device,
        mesh=mesh,
        in_specs=(
            P(("replica", "shard"), "tensor"),
            P(("replica", "shard"), None),
            P(None, "tensor"),
            P("shard", "tensor", None),
            P("shard", None, "tensor"),
        ),
        out_specs=P(("replica", "shard"), "tensor"),
        check_vma=False,
    )
```

```python
import jax
import jax.numpy as jnp
import numpy as np
from jax import lax
from jax.experimental import pallas as pl
from jax.experimental.pallas import tpu as pltpu
from jax.sharding import PartitionSpec as P

MIB = 1024 * 1024
CHUNK = 512
TILE = 256
AXES = ("replica", "shard", "tensor")
FIRST_OWNER = 2
SMEM = pl.BlockSpec(memory_space=pltpu.SMEM)
VMEM = pl.BlockSpec(memory_space=pltpu.VMEM)
ANY = pl.BlockSpec(memory_space=pl.ANY)
TOKEN = jax.ShapeDtypeStruct((8, 128), jnp.float32)


def swap(value, axis):
    return lax.ppermute(value, axis, [(0, 1), (1, 0)])


def neighbour(value, shards):
    return lax.ppermute(value, "shard", [(i, i ^ 1) for i in range(shards)])


def along_line(value, shards, step):
    return lax.ppermute(value, "shard", [(i, (i + 2 * step) % shards) for i in range(shards)])


def in_plane(value, shards, first):
    pairs = []
    for r in range(2):
        for s in range(shards):
            for t in range(2):
                to_r, to_s = (r, s ^ 1) if (t == 0) == first else (r ^ 1, s)
                pairs.append(((r * shards + s) * 2 + t, (to_r * shards + to_s) * 2 + t))
    return lax.ppermute(value, AXES, pairs)


def call(kernel, out_shape, in_specs, limit, scratch=(), flops=0, moved=0):
    return pl.pallas_call(
        kernel,
        out_shape=out_shape,
        in_specs=in_specs,
        out_specs=jax.tree.map(lambda _: VMEM, out_shape),
        scratch_shapes=list(scratch),
        compiler_params=pltpu.CompilerParams(vmem_limit_bytes=limit * MIB),
        cost_estimate=pl.CostEstimate(flops=flops, bytes_accessed=moved, transcendentals=0),
    )


def owner_row(info, blocks, rank):
    place = lax.broadcasted_iota(jnp.int32, (1, len(blocks) * rank), 1) // rank
    row = jnp.full(place.shape, -1, jnp.int32)
    for number, block in enumerate(blocks):
        if block is not None:
            row = jnp.where(place == number, info[FIRST_OWNER + block], row)
    return row


def pack(pieces, *after):
    count = len(pieces)
    total = sum(rows for _, _, rows in pieces)
    width, dtype = pieces[0][0].shape[1], pieces[0][0].dtype

    def kernel(*refs):
        out, token = refs[-2:]
        top = 0
        for ref, (_, begin, rows) in zip(refs, pieces):
            out[top : top + rows, :] = ref[begin : begin + rows, :]
            top += rows
        token[...] = jnp.zeros_like(token)

    return call(
        kernel,
        [jax.ShapeDtypeStruct((total, width), dtype), TOKEN],
        [VMEM] * count + [ANY] * len(after),
        4,
    )(*[array for array, _, _ in pieces], *after)


def put(blocks, stack, top, rank):
    for number, parts in enumerate(blocks):
        place = top + 2 * number * rank
        for ref, begin, rows in parts:
            stack[place : place + rows, :] = ref[begin : begin + rows, :]
            place += rows


def fill_here(info, holds, received, stack, top, rank):
    early, early_first, early_second, late, late_first, late_second, _, _ = received

    def blocks(pair, single):
        return [[(pair, 0, rank)], [(pair, rank, rank)], [(single, 0, rank)]]

    swapped = ((early_second, late_second), (early_first, late_first))
    pl.when(holds)(lambda: put(blocks(early, late), stack, top, rank))
    for core in range(2):
        away = jnp.logical_not(holds) & (info[0] == core)
        pl.when(away)(lambda refs=swapped[core]: put(blocks(*refs), stack, top, rank))


def fill_beside(info, holds, received, stack, top, rank, direct=True, corner=True):
    _, early_first, early_second, _, late_first, late_second, corner_one, corner_two = received
    half = rank // 2
    swapped = ((early_first, late_first), (early_second, late_second))
    if direct:
        for core in range(2):

            def straight(refs=swapped[core]):
                pair, single = refs
                blocks = [[(pair, 0, rank)], [(pair, rank, rank)], [(single, 0, rank)]]
                put(blocks, stack, top, rank)

            pl.when(holds & (info[0] == core))(straight)
    if corner:

        def turned():
            last = [(corner_one, rank, half), (corner_two, rank, half)]
            put([[(corner_one, 0, rank)], [(corner_two, 0, rank)], last], stack, top, rank)

        pl.when(jnp.logical_not(holds))(turned)


def clear(stack, top, rank, count):
    for number in range(count):
        place = top + 2 * number * rank
        stack[place : place + rank, :] = jnp.zeros((rank, stack.shape[1]), stack.dtype)


def masked_products(info, ids, latent, stack, blocks, rank):
    total = None
    width = 2 * rank
    for skip in range(0, stack.shape[0], CHUNK):
        count = min(CHUNK, stack.shape[0] - skip)
        part = lax.dot_general(
            latent[...],
            stack[skip : skip + count, :],
            (((1,), (1,)), ((), ())),
            preferred_element_type=jnp.float32,
        )
        owners = owner_row(info, blocks[skip // rank : (skip + count) // rank], rank)
        part = jnp.where(ids[...] == owners, part, 0.0)
        for lane in range(0, count, width):
            fold = part[:, lane : lane + width]
            total = fold if total is None else total + fold
    return total


def down_whole_kernel(info, ids, latent, stack, out):
    rank = out.shape[1] // 2
    blocks = range(stack.shape[0] // rank)
    out[...] = masked_products(info, ids, latent, stack, blocks, rank)


def down_first_kernel(info, ids, latent, own, beside, *refs):
    *received, _, out, stack = refs
    rank = own.shape[0]
    holds = info[1] == 1
    stack[0:rank, :] = own[...]
    stack[rank : 2 * rank, :] = beside[...]
    fill_here(info, holds, (*received, None, None), stack, 2 * rank, rank)
    fill_beside(info, holds, (*received, None, None), stack, 3 * rank, rank, corner=False)
    pl.when(jnp.logical_not(holds))(lambda: clear(stack, 3 * rank, rank, 3))
    out[...] = masked_products(info, ids, latent, stack, range(stack.shape[0] // rank), rank)


def down_last_kernel(info, ids, latent, earlier, corner_one, corner_two, out, stack):
    rank = out.shape[1] // 2
    half = rank // 2
    holds = info[1] == 1

    @pl.when(holds)
    def _():
        out[...] = earlier[...]

    @pl.when(jnp.logical_not(holds))
    def _():
        stack[0:rank, :] = corner_one[0:rank, :]
        stack[rank : 2 * rank, :] = corner_two[0:rank, :]
        stack[2 * rank : 2 * rank + half, :] = corner_one[rank : rank + half, :]
        stack[2 * rank + half : 3 * rank, :] = corner_two[rank : rank + half, :]
        stack[3 * rank : 4 * rank, :] = jnp.zeros((rank, stack.shape[1]), stack.dtype)
        pair = masked_products(info, ids, latent, stack, (3, 5, 7, None), rank)
        fold = pair[:, :rank] + pair[:, rank:]
        out[...] = earlier[...] + jnp.concatenate([jnp.zeros_like(fold), fold], axis=1)


def base_kernel(info, own, other, weight, *refs, skip):
    out, token = refs[-2:]
    token[...] = jnp.zeros_like(token)
    width = own.shape[1]
    mine = pl.ds(pl.multiple_of(info[0] * width, width), width)
    rest = pl.ds(pl.multiple_of((1 - info[0]) * width, width), width)
    step = min(CHUNK, out.shape[1])
    for begin in range(0, out.shape[1], step):
        place = slice(begin, min(begin + step, out.shape[1]))
        source = slice(skip + begin, skip + place.stop)
        out[:, place] = jnp.dot(
            own[...], weight[mine, source], preferred_element_type=jnp.float32
        ) + jnp.dot(other[...], weight[rest, source], preferred_element_type=jnp.float32)


def base(info, latent, other, weight, after, skip, end):
    rows, columns = latent.shape[0], end - skip
    return pl.pallas_call(
        lambda *refs: base_kernel(*refs, skip=skip),
        out_shape=[jax.ShapeDtypeStruct((rows, columns), jnp.float32), TOKEN],
        in_specs=[SMEM, VMEM, VMEM, VMEM] + [ANY] * len(after),
        out_specs=[VMEM, VMEM],
        compiler_params=pltpu.CompilerParams(vmem_limit_bytes=24 * MIB),
        cost_estimate=pl.CostEstimate(flops=1000, bytes_accessed=1000, transcendentals=0),
    )(info, latent, other, weight, *after)


def up_kernel(info, ids, mine, theirs, *refs, base_parts):
    *pieces, out, stack, wide, sems, staged = refs[base_parts:]
    bases = [
        part.at[:, pl.ds(begin, TILE)]
        for part in refs[:base_parts]
        for begin in range(0, part.shape[1], TILE)
    ]
    rank = mine.shape[1] // 2
    if len(pieces) == 1:
        stack[...] = pieces[0][...]
    else:
        own, beside, *received = pieces
        holds = info[1] == 0
        stack[0:rank, :] = own[...]
        stack[rank : 2 * rank, :] = beside[...]
        fill_here(info, holds, received, stack, 2 * rank, rank)
        fill_beside(info, holds, received, stack, 3 * rank, rank)
    lowrank = (mine[...] + theirs[...]).astype(jnp.bfloat16)
    zeros = jnp.zeros_like(lowrank)
    width = 2 * rank
    for lane in range(0, wide.shape[1], width):
        mask = ids[...] == owner_row(info, (lane // rank, lane // rank + 1), rank)
        wide[:, lane : lane + width] = jnp.where(mask, lowrank, zeros)
    copies = []
    tiles, _, tile = staged.shape
    for number in range(tiles):
        place = pl.ds(number * tile, tile)
        delta = jnp.dot(wide[...], stack[:, place], preferred_element_type=jnp.float32)
        total = bases[number][...] + delta.astype(jnp.bfloat16).astype(jnp.float32)
        staged[number] = total.astype(out.dtype)
        copies.append(
            pltpu.make_async_copy(staged.at[number], out.at[:, place], sems.at[number])
        )
        copies[-1].start()
    for copy in copies:
        copy.wait()


def on_device(latent, row_adapter_index, shared_weight, adapter_down_weight, adapter_up_weight):
    rows, half_width = latent.shape
    out_width = shared_weight.shape[1]
    local_adapters, _, rank = adapter_down_weight.shape
    shards = lax.axis_size("shard")
    adapters = shards * local_adapters
    columns = adapters * rank
    index, core = lax.axis_index("shard"), lax.axis_index("tensor")
    holds_down = core == lax.axis_index("replica")
    tiles = out_width // TILE
    cuts = [0, out_width // 6, out_width * 2 // 3, out_width]
    down = jnp.swapaxes(adapter_down_weight, 1, 2).reshape(local_adapters * rank, half_width)
    up = adapter_up_weight.reshape(local_adapters * rank, out_width)
    ids = row_adapter_index
    routed = shards == 8 and local_adapters == 1 and lax.axis_size("replica") == 2
    routed = routed and half_width == out_width and tiles % 6 == 0
    lowrank = jax.ShapeDtypeStruct((rows, 2 * rank), jnp.float32)
    if routed:
        sources = [(index - 2 * step) % shards for step in (0, 1, 3, 2)]
        owners = [a for source in sources for a in (source, source ^ 1)]
    else:
        owners = list(range(adapters))
    info = jnp.stack([jnp.asarray(v, jnp.int32) for v in (core, holds_down, *owners)])
    if routed:
        piece = jnp.where(holds_down, down, up)
        line = {step: along_line(piece, shards, step) for step in (1, 3)}
        other = swap(latent, "tensor")
        down_beside, up_beside = neighbour(down, shards), neighbour(up, shards)
        parts = []
        part, token = base(info, latent, other, shared_weight, [ids], cuts[0], cuts[1])
        parts.append(part)
        relay, token = pack([(line[1], 0, rank)], token)
        line[2] = along_line(relay, shards, 1)
        early, token = pack([(line[1], 0, rank), (line[3], 0, rank)], token, down_beside)
        part, token = base(info, latent, other, shared_weight, [token, up_beside], cuts[1], cuts[2])
        parts.append(part)
        early_first, early_second = in_plane(early, shards, True), in_plane(early, shards, False)
        late, token = pack([(line[2], 0, rank)], token)
        part, token = base(info, latent, other, shared_weight, [token], cuts[2], cuts[3])
        parts.append(part)
        late_first, late_second = in_plane(late, shards, True), in_plane(late, shards, False)
        half = rank // 2
        turn_one, token = pack([(early_first, 0, rank), (late_first, 0, half)], token)
        turn_two, token = pack([(early_second, rank, rank), (late_second, half, half)], token)
        corner_one = in_plane(turn_one, shards, False)
        corner_two = in_plane(turn_two, shards, True)
        received = [early, early_first, early_second, late, late_first, late_second]
        mine = call(
            down_first_kernel,
            lowrank,
            [SMEM] + [VMEM] * 10 + [ANY],
            16,
            [pltpu.VMEM((columns, half_width), latent.dtype)],
        )(info, ids, latent, down, down_beside, *received, token)
        mine = call(
            down_last_kernel,
            lowrank,
            [SMEM] + [VMEM] * 5,
            16,
            [pltpu.VMEM((4 * rank, half_width), latent.dtype)],
        )(info, ids, latent, mine, corner_one, corner_two)
        up_pieces = [up, up_beside, *received, corner_one, corner_two]
    else:
        other = swap(latent, "tensor")
        parts, token = [], ids
        for begin, end in zip(cuts[:-1], cuts[1:]):
            part, token = base(info, latent, other, shared_weight, [token], begin, end)
            parts.append(part)
        mine = call(down_whole_kernel, lowrank, [SMEM] + [VMEM] * 3, 48)(
            info, ids, latent, lax.all_gather(down, "shard", axis=0, tiled=True)
        )
        up_pieces = [lax.all_gather(up, "shard", axis=0, tiled=True)]
    theirs = swap(mine, "tensor")

    return pl.pallas_call(
        lambda *refs: up_kernel(*refs, base_parts=len(parts)),
        out_shape=jax.ShapeDtypeStruct((rows, out_width), latent.dtype),
        in_specs=[SMEM] + [VMEM] * (3 + len(parts) + len(up_pieces)),
        out_specs=ANY,
        scratch_shapes=[
            pltpu.VMEM((columns, out_width), latent.dtype),
            pltpu.VMEM((rows, columns), latent.dtype),
            pltpu.SemaphoreType.DMA((tiles,)),
            pltpu.VMEM((tiles, rows, TILE), latent.dtype),
        ],
        compiler_params=pltpu.CompilerParams(vmem_limit_bytes=(24 if routed else 56) * MIB),
    )(info, ids, mine, theirs, *parts, *up_pieces)


def solution(mesh):
    return jax.shard_map(
        on_device,
        mesh=mesh,
        in_specs=(
            P(("replica", "shard"), "tensor"),
            P(("replica", "shard"), None),
            P(None, "tensor"),
            P("shard", "tensor", None),
            P("shard", None, "tensor"),
        ),
        out_specs=P(("replica", "shard"), "tensor"),
        check_vma=False,
    )
```

```python
import jax
import jax.numpy as jnp
import numpy as np
from jax import lax
from jax.experimental import pallas as pl
from jax.experimental.pallas import tpu as pltpu
from jax.sharding import PartitionSpec as P

MIB = 1024 * 1024
CHUNK = 512
TILE = 256
AXES = ("replica", "shard", "tensor")
FIRST_OWNER = 2
SMEM = pl.BlockSpec(memory_space=pltpu.SMEM)
VMEM = pl.BlockSpec(memory_space=pltpu.VMEM)
ANY = pl.BlockSpec(memory_space=pl.ANY)
TOKEN = jax.ShapeDtypeStruct((8, 128), jnp.float32)


def swap(value, axis):
    return lax.ppermute(value, axis, [(0, 1), (1, 0)])


def neighbour(value, shards):
    return lax.ppermute(value, "shard", [(i, i ^ 1) for i in range(shards)])


def along_line(value, shards, step):
    return lax.ppermute(value, "shard", [(i, (i + 2 * step) % shards) for i in range(shards)])


def in_plane(value, shards, first):
    pairs = []
    for r in range(2):
        for s in range(shards):
            for t in range(2):
                to_r, to_s = (r, s ^ 1) if (t == 0) == first else (r ^ 1, s)
                pairs.append(((r * shards + s) * 2 + t, (to_r * shards + to_s) * 2 + t))
    return lax.ppermute(value, AXES, pairs)


def call(kernel, out_shape, in_specs, limit, scratch=(), flops=0, moved=0):
    return pl.pallas_call(
        kernel,
        out_shape=out_shape,
        in_specs=in_specs,
        out_specs=jax.tree.map(lambda _: VMEM, out_shape),
        scratch_shapes=list(scratch),
        compiler_params=pltpu.CompilerParams(vmem_limit_bytes=limit * MIB),
        cost_estimate=pl.CostEstimate(flops=flops, bytes_accessed=moved, transcendentals=0),
    )


def owner_row(info, blocks, rank):
    place = lax.broadcasted_iota(jnp.int32, (1, len(blocks) * rank), 1) // rank
    row = jnp.full(place.shape, -1, jnp.int32)
    for number, block in enumerate(blocks):
        if block is not None:
            row = jnp.where(place == number, info[FIRST_OWNER + block], row)
    return row


def pack(pieces, *after):
    count = len(pieces)
    total = sum(rows for _, _, rows in pieces)
    width, dtype = pieces[0][0].shape[1], pieces[0][0].dtype

    def kernel(*refs):
        out, token = refs[-2:]
        top = 0
        for ref, (_, begin, rows) in zip(refs, pieces):
            out[top : top + rows, :] = ref[begin : begin + rows, :]
            top += rows
        token[...] = jnp.zeros_like(token)

    return call(
        kernel,
        [jax.ShapeDtypeStruct((total, width), dtype), TOKEN],
        [VMEM] * count + [ANY] * len(after),
        4,
    )(*[array for array, _, _ in pieces], *after)


def put(blocks, stack, top, rank):
    for number, parts in enumerate(blocks):
        place = top + 2 * number * rank
        for ref, begin, rows in parts:
            stack[place : place + rows, :] = ref[begin : begin + rows, :]
            place += rows


def fill_here(info, holds, received, stack, top, rank):
    early, early_first, early_second, late, late_first, late_second, *_ = received

    def blocks(pair, single):
        return [[(pair, 0, rank)], [(pair, rank, rank)], [(single, 0, rank)]]

    swapped = ((early_second, late_second), (early_first, late_first))
    pl.when(holds)(lambda: put(blocks(early, late), stack, top, rank))
    for core in range(2):
        away = jnp.logical_not(holds) & (info[0] == core)
        pl.when(away)(lambda refs=swapped[core]: put(blocks(*refs), stack, top, rank))


def fill_beside(info, holds, received, stack, top, rank, direct=True, corner=True):
    _, early_first, early_second, _, late_first, late_second, *corners = received
    swapped = ((early_first, late_first), (early_second, late_second))
    if direct:
        for core in range(2):

            def straight(refs=swapped[core]):
                pair, single = refs
                blocks = [[(pair, 0, rank)], [(pair, rank, rank)], [(single, 0, rank)]]
                put(blocks, stack, top, rank)

            pl.when(holds & (info[0] == core))(straight)
    if corner:
        blocks = [[(ref, 0, rank)] for ref in corners]
        pl.when(jnp.logical_not(holds))(lambda: put(blocks, stack, top, rank))


def clear(stack, top, rank, count):
    for number in range(count):
        place = top + 2 * number * rank
        stack[place : place + rank, :] = jnp.zeros((rank, stack.shape[1]), stack.dtype)


def masked_products(info, ids, latent, stack, blocks, rank):
    total = None
    width = 2 * rank
    for skip in range(0, stack.shape[0], CHUNK):
        count = min(CHUNK, stack.shape[0] - skip)
        part = lax.dot_general(
            latent[...],
            stack[skip : skip + count, :],
            (((1,), (1,)), ((), ())),
            preferred_element_type=jnp.float32,
        )
        owners = owner_row(info, blocks[skip // rank : (skip + count) // rank], rank)
        part = jnp.where(ids[...] == owners, part, 0.0)
        for lane in range(0, count, width):
            fold = part[:, lane : lane + width]
            total = fold if total is None else total + fold
    return total


def down_whole_kernel(info, ids, latent, stack, out):
    rank = out.shape[1] // 2
    blocks = range(stack.shape[0] // rank)
    out[...] = masked_products(info, ids, latent, stack, blocks, rank)


def down_first_kernel(info, ids, latent, own, beside, *refs):
    *received, _, out, stack = refs
    rank = own.shape[0]
    holds = info[1] == 1
    stack[0:rank, :] = own[...]
    stack[rank : 2 * rank, :] = beside[...]
    fill_here(info, holds, received, stack, 2 * rank, rank)
    fill_beside(info, holds, received, stack, 3 * rank, rank, corner=False)
    pl.when(jnp.logical_not(holds))(lambda: clear(stack, 3 * rank, rank, 3))
    out[...] = masked_products(info, ids, latent, stack, range(stack.shape[0] // rank), rank)


def down_last_kernel(info, ids, latent, earlier, *refs):
    *corners, out, stack = refs
    rank = out.shape[1] // 2
    holds = info[1] == 1

    @pl.when(holds)
    def _():
        out[...] = earlier[...]

    @pl.when(jnp.logical_not(holds))
    def _():
        for number, corner in enumerate(corners):
            stack[number * rank : (number + 1) * rank, :] = corner[...]
        stack[3 * rank : 4 * rank, :] = jnp.zeros((rank, stack.shape[1]), stack.dtype)
        pair = masked_products(info, ids, latent, stack, (3, 5, 7, None), rank)
        fold = pair[:, :rank] + pair[:, rank:]
        out[...] = earlier[...] + jnp.concatenate([jnp.zeros_like(fold), fold], axis=1)


def base_kernel(info, own, other, weight, *refs, skip):
    out, token = refs[-2:]
    token[...] = jnp.zeros_like(token)
    width = own.shape[1]
    mine = pl.ds(pl.multiple_of(info[0] * width, width), width)
    rest = pl.ds(pl.multiple_of((1 - info[0]) * width, width), width)
    step = min(CHUNK, out.shape[1])
    for begin in range(0, out.shape[1], step):
        place = slice(begin, min(begin + step, out.shape[1]))
        source = slice(skip + begin, skip + place.stop)
        out[:, place] = jnp.dot(
            own[...], weight[mine, source], preferred_element_type=jnp.float32
        ) + jnp.dot(other[...], weight[rest, source], preferred_element_type=jnp.float32)


def base(info, latent, other, weight, after, skip, end):
    rows, columns = latent.shape[0], end - skip
    return pl.pallas_call(
        lambda *refs: base_kernel(*refs, skip=skip),
        out_shape=[jax.ShapeDtypeStruct((rows, columns), jnp.float32), TOKEN],
        in_specs=[SMEM, VMEM, VMEM, VMEM] + [ANY] * len(after),
        out_specs=[VMEM, VMEM],
        compiler_params=pltpu.CompilerParams(vmem_limit_bytes=24 * MIB),
        cost_estimate=pl.CostEstimate(flops=1000, bytes_accessed=1000, transcendentals=0),
    )(info, latent, other, weight, *after)


def up_kernel(info, ids, mine, theirs, *refs, base_parts):
    *pieces, out, stack, wide, sems, staged = refs[base_parts:]
    bases = [
        part.at[:, pl.ds(begin, TILE)]
        for part in refs[:base_parts]
        for begin in range(0, part.shape[1], TILE)
    ]
    rank = mine.shape[1] // 2
    if len(pieces) == 1:
        stack[...] = pieces[0][...]
    else:
        own, beside, *received = pieces
        holds = info[1] == 0
        stack[0:rank, :] = own[...]
        stack[rank : 2 * rank, :] = beside[...]
        fill_here(info, holds, received, stack, 2 * rank, rank)
        fill_beside(info, holds, received, stack, 3 * rank, rank)
    lowrank = (mine[...] + theirs[...]).astype(jnp.bfloat16)
    zeros = jnp.zeros_like(lowrank)
    width = 2 * rank
    for lane in range(0, wide.shape[1], width):
        mask = ids[...] == owner_row(info, (lane // rank, lane // rank + 1), rank)
        wide[:, lane : lane + width] = jnp.where(mask, lowrank, zeros)
    copies = []
    tiles, _, tile = staged.shape
    for number in range(tiles):
        place = pl.ds(number * tile, tile)
        delta = jnp.dot(wide[...], stack[:, place], preferred_element_type=jnp.float32)
        total = bases[number][...] + delta.astype(jnp.bfloat16).astype(jnp.float32)
        staged[number] = total.astype(out.dtype)
        copies.append(
            pltpu.make_async_copy(staged.at[number], out.at[:, place], sems.at[number])
        )
        copies[-1].start()
    for copy in copies:
        copy.wait()


def on_device(latent, row_adapter_index, shared_weight, adapter_down_weight, adapter_up_weight):
    rows, half_width = latent.shape
    out_width = shared_weight.shape[1]
    local_adapters, _, rank = adapter_down_weight.shape
    shards = lax.axis_size("shard")
    adapters = shards * local_adapters
    columns = adapters * rank
    index, core = lax.axis_index("shard"), lax.axis_index("tensor")
    holds_down = core == lax.axis_index("replica")
    tiles = out_width // TILE
    cuts = [0, out_width // 6, out_width * 2 // 3, out_width]
    down = jnp.swapaxes(adapter_down_weight, 1, 2).reshape(local_adapters * rank, half_width)
    up = adapter_up_weight.reshape(local_adapters * rank, out_width)
    ids = row_adapter_index
    routed = shards == 8 and local_adapters == 1 and lax.axis_size("replica") == 2
    routed = routed and half_width == out_width and tiles % 6 == 0
    lowrank = jax.ShapeDtypeStruct((rows, 2 * rank), jnp.float32)
    if routed:
        sources = [(index - 2 * step) % shards for step in (0, 1, 3, 2)]
        owners = [a for source in sources for a in (source, source ^ 1)]
    else:
        owners = list(range(adapters))
    info = jnp.stack([jnp.asarray(v, jnp.int32) for v in (core, holds_down, *owners)])
    if routed:
        piece = jnp.where(holds_down, down, up)
        line = {step: along_line(piece, shards, step) for step in (1, 3)}
        other = swap(latent, "tensor")
        down_beside, up_beside = neighbour(down, shards), neighbour(up, shards)
        parts = []
        part, token = base(info, latent, other, shared_weight, [ids], cuts[0], cuts[1])
        parts.append(part)
        line[2] = along_line(line[1], shards, 1)
        early, token = pack([(line[1], 0, rank), (line[3], 0, rank)], token, down_beside, up_beside)
        part, token = base(info, latent, other, shared_weight, [token], cuts[1], cuts[2])
        parts.append(part)
        early_first, early_second = in_plane(early, shards, True), in_plane(early, shards, False)
        late, token = pack([(line[2], 0, rank)], token)
        part, token = base(info, latent, other, shared_weight, [token], cuts[2], cuts[3])
        parts.append(part)
        late_second = in_plane(late, shards, False)
        turn, token = pack([(early_first, 0, rank)], token)
        corner_one = in_plane(turn, shards, False)
        late_first = along_line(turn, shards, 1)
        turn, token = pack([(early_second, rank, rank)], token)
        corner_two = in_plane(turn, shards, True)
        turn, token = pack([(late_second, 0, rank)], token)
        corner_three = in_plane(turn, shards, True)
        corners = [corner_one, corner_two, corner_three]
        received = [early, early_first, early_second, late, late_first, late_second]
        mine = call(
            down_first_kernel,
            lowrank,
            [SMEM] + [VMEM] * 10 + [ANY],
            16,
            [pltpu.VMEM((columns, half_width), latent.dtype)],
        )(info, ids, latent, down, down_beside, *received, token)
        mine = call(
            down_last_kernel,
            lowrank,
            [SMEM] + [VMEM] * 6,
            16,
            [pltpu.VMEM((4 * rank, half_width), latent.dtype)],
        )(info, ids, latent, mine, *corners)
        up_pieces = [up, up_beside, *received, *corners]
    else:
        other = swap(latent, "tensor")
        parts, token = [], ids
        for begin, end in zip(cuts[:-1], cuts[1:]):
            part, token = base(info, latent, other, shared_weight, [token], begin, end)
            parts.append(part)
        mine = call(down_whole_kernel, lowrank, [SMEM] + [VMEM] * 3, 48)(
            info, ids, latent, lax.all_gather(down, "shard", axis=0, tiled=True)
        )
        up_pieces = [lax.all_gather(up, "shard", axis=0, tiled=True)]
    theirs = swap(mine, "tensor")

    return pl.pallas_call(
        lambda *refs: up_kernel(*refs, base_parts=len(parts)),
        out_shape=jax.ShapeDtypeStruct((rows, out_width), latent.dtype),
        in_specs=[SMEM] + [VMEM] * (3 + len(parts) + len(up_pieces)),
        out_specs=ANY,
        scratch_shapes=[
            pltpu.VMEM((columns, out_width), latent.dtype),
            pltpu.VMEM((rows, columns), latent.dtype),
            pltpu.SemaphoreType.DMA((tiles,)),
            pltpu.VMEM((tiles, rows, TILE), latent.dtype),
        ],
        compiler_params=pltpu.CompilerParams(vmem_limit_bytes=(24 if routed else 56) * MIB),
    )(info, ids, mine, theirs, *parts, *up_pieces)


def solution(mesh):
    return jax.shard_map(
        on_device,
        mesh=mesh,
        in_specs=(
            P(("replica", "shard"), "tensor"),
            P(("replica", "shard"), None),
            P(None, "tensor"),
            P("shard", "tensor", None),
            P("shard", None, "tensor"),
        ),
        out_specs=P(("replica", "shard"), "tensor"),
        check_vma=False,
    )
```

```python
import jax
import jax.numpy as jnp
import numpy as np
from jax import lax
from jax.experimental import pallas as pl
from jax.experimental.pallas import tpu as pltpu
from jax.sharding import PartitionSpec as P

MIB = 1024 * 1024
CHUNK = 512
TILE = 256
AXES = ("replica", "shard", "tensor")
FIRST_OWNER = 2
SMEM = pl.BlockSpec(memory_space=pltpu.SMEM)
VMEM = pl.BlockSpec(memory_space=pltpu.VMEM)
ANY = pl.BlockSpec(memory_space=pl.ANY)
TOKEN = jax.ShapeDtypeStruct((8, 128), jnp.float32)


def swap(value, axis):
    return lax.ppermute(value, axis, [(0, 1), (1, 0)])


def neighbour(value, shards):
    return lax.ppermute(value, "shard", [(i, i ^ 1) for i in range(shards)])


def ring_step(index, step):
    plane = index >> 1
    place = ((plane ^ (plane >> 1)) + step) & 3
    return ((place ^ (place >> 1)) << 1) | (index & 1)


def along_line(value, shards, step):
    return lax.ppermute(value, "shard", [(i, ring_step(i, step)) for i in range(shards)])


def in_plane(value, shards, first):
    pairs = []
    for r in range(2):
        for s in range(shards):
            for t in range(2):
                to_r, to_s = (r, s ^ 1) if (t == 0) == first else (r ^ 1, s)
                pairs.append(((r * shards + s) * 2 + t, (to_r * shards + to_s) * 2 + t))
    return lax.ppermute(value, AXES, pairs)


def call(kernel, out_shape, in_specs, limit, scratch=(), flops=0, moved=0):
    return pl.pallas_call(
        kernel,
        out_shape=out_shape,
        in_specs=in_specs,
        out_specs=jax.tree.map(lambda _: VMEM, out_shape),
        scratch_shapes=list(scratch),
        compiler_params=pltpu.CompilerParams(vmem_limit_bytes=limit * MIB),
        cost_estimate=pl.CostEstimate(flops=flops, bytes_accessed=moved, transcendentals=0),
    )


def owner_row(info, blocks, rank):
    place = lax.broadcasted_iota(jnp.int32, (1, len(blocks) * rank), 1) // rank
    row = jnp.full(place.shape, -1, jnp.int32)
    for number, block in enumerate(blocks):
        if block is not None:
            row = jnp.where(place == number, info[FIRST_OWNER + block], row)
    return row


def pack(pieces, *after):
    count = len(pieces)
    total = sum(rows for _, _, rows in pieces)
    width, dtype = pieces[0][0].shape[1], pieces[0][0].dtype

    def kernel(*refs):
        out, token = refs[-2:]
        top = 0
        for ref, (_, begin, rows) in zip(refs, pieces):
            out[top : top + rows, :] = ref[begin : begin + rows, :]
            top += rows
        token[...] = jnp.zeros_like(token)

    return call(
        kernel,
        [jax.ShapeDtypeStruct((total, width), dtype), TOKEN],
        [VMEM] * count + [ANY] * len(after),
        4,
    )(*[array for array, _, _ in pieces], *after)


def put(blocks, stack, top, rank):
    for number, parts in enumerate(blocks):
        place = top + 2 * number * rank
        for ref, begin, rows in parts:
            stack[place : place + rows, :] = ref[begin : begin + rows, :]
            place += rows


def fill_here(info, holds, received, stack, top, rank):
    early, early_first, early_second, late, late_first, late_second, *_ = received

    def blocks(pair, single):
        return [[(pair, 0, rank)], [(pair, rank, rank)], [(single, 0, rank)]]

    swapped = ((early_second, late_second), (early_first, late_first))
    pl.when(holds)(lambda: put(blocks(early, late), stack, top, rank))
    for core in range(2):
        away = jnp.logical_not(holds) & (info[0] == core)
        pl.when(away)(lambda refs=swapped[core]: put(blocks(*refs), stack, top, rank))


def fill_beside(info, holds, received, stack, top, rank, direct=True, corner=True):
    _, early_first, early_second, _, late_first, late_second, *corners = received
    swapped = ((early_first, late_first), (early_second, late_second))
    if direct:
        for core in range(2):

            def straight(refs=swapped[core]):
                pair, single = refs
                blocks = [[(pair, 0, rank)], [(pair, rank, rank)], [(single, 0, rank)]]
                put(blocks, stack, top, rank)

            pl.when(holds & (info[0] == core))(straight)
    if corner:
        blocks = [[(ref, 0, rank)] for ref in corners]
        pl.when(jnp.logical_not(holds))(lambda: put(blocks, stack, top, rank))


def clear(stack, top, rank, count):
    for number in range(count):
        place = top + 2 * number * rank
        stack[place : place + rank, :] = jnp.zeros((rank, stack.shape[1]), stack.dtype)


def masked_products(info, ids, latent, stack, blocks, rank):
    total = None
    width = 2 * rank
    for skip in range(0, stack.shape[0], CHUNK):
        count = min(CHUNK, stack.shape[0] - skip)
        part = lax.dot_general(
            latent[...],
            stack[skip : skip + count, :],
            (((1,), (1,)), ((), ())),
            preferred_element_type=jnp.float32,
        )
        owners = owner_row(info, blocks[skip // rank : (skip + count) // rank], rank)
        part = jnp.where(ids[...] == owners, part, 0.0)
        for lane in range(0, count, width):
            fold = part[:, lane : lane + width]
            total = fold if total is None else total + fold
    return total


def down_whole_kernel(info, ids, latent, stack, out):
    rank = out.shape[1] // 2
    blocks = range(stack.shape[0] // rank)
    out[...] = masked_products(info, ids, latent, stack, blocks, rank)


def down_first_kernel(info, ids, latent, own, beside, *refs):
    *received, _, out, stack = refs
    rank = own.shape[0]
    holds = info[1] == 1
    stack[0:rank, :] = own[...]
    stack[rank : 2 * rank, :] = beside[...]
    fill_here(info, holds, received, stack, 2 * rank, rank)
    fill_beside(info, holds, received, stack, 3 * rank, rank, corner=False)
    pl.when(jnp.logical_not(holds))(lambda: clear(stack, 3 * rank, rank, 3))
    out[...] = masked_products(info, ids, latent, stack, range(stack.shape[0] // rank), rank)


def down_last_kernel(info, ids, latent, earlier, *refs):
    *corners, out, stack = refs
    rank = out.shape[1] // 2
    holds = info[1] == 1

    @pl.when(holds)
    def _():
        out[...] = earlier[...]

    @pl.when(jnp.logical_not(holds))
    def _():
        for number, corner in enumerate(corners):
            stack[number * rank : (number + 1) * rank, :] = corner[...]
        stack[3 * rank : 4 * rank, :] = jnp.zeros((rank, stack.shape[1]), stack.dtype)
        pair = masked_products(info, ids, latent, stack, (3, 5, 7, None), rank)
        fold = pair[:, :rank] + pair[:, rank:]
        out[...] = earlier[...] + jnp.concatenate([jnp.zeros_like(fold), fold], axis=1)


def base_kernel(info, own, other, weight, *refs, skip):
    out, token = refs[-2:]
    token[...] = jnp.zeros_like(token)
    width = own.shape[1]
    mine = pl.ds(pl.multiple_of(info[0] * width, width), width)
    rest = pl.ds(pl.multiple_of((1 - info[0]) * width, width), width)
    step = min(CHUNK, out.shape[1])
    for begin in range(0, out.shape[1], step):
        place = slice(begin, min(begin + step, out.shape[1]))
        source = slice(skip + begin, skip + place.stop)
        out[:, place] = jnp.dot(
            own[...], weight[mine, source], preferred_element_type=jnp.float32
        ) + jnp.dot(other[...], weight[rest, source], preferred_element_type=jnp.float32)


def base(info, latent, other, weight, after, skip, end):
    rows, columns = latent.shape[0], end - skip
    return pl.pallas_call(
        lambda *refs: base_kernel(*refs, skip=skip),
        out_shape=[jax.ShapeDtypeStruct((rows, columns), jnp.float32), TOKEN],
        in_specs=[SMEM, VMEM, VMEM, VMEM] + [ANY] * len(after),
        out_specs=[VMEM, VMEM],
        compiler_params=pltpu.CompilerParams(vmem_limit_bytes=24 * MIB),
        cost_estimate=pl.CostEstimate(flops=1000, bytes_accessed=1000, transcendentals=0),
    )(info, latent, other, weight, *after)


def up_kernel(info, ids, mine, theirs, *refs, base_parts):
    *pieces, out, stack, wide, sems, staged = refs[base_parts:]
    bases = [
        part.at[:, pl.ds(begin, TILE)]
        for part in refs[:base_parts]
        for begin in range(0, part.shape[1], TILE)
    ]
    rank = mine.shape[1] // 2
    if len(pieces) == 1:
        stack[...] = pieces[0][...]
    else:
        own, beside, *received = pieces
        holds = info[1] == 0
        stack[0:rank, :] = own[...]
        stack[rank : 2 * rank, :] = beside[...]
        fill_here(info, holds, received, stack, 2 * rank, rank)
        fill_beside(info, holds, received, stack, 3 * rank, rank)
    lowrank = (mine[...] + theirs[...]).astype(jnp.bfloat16)
    zeros = jnp.zeros_like(lowrank)
    width = 2 * rank
    for lane in range(0, wide.shape[1], width):
        mask = ids[...] == owner_row(info, (lane // rank, lane // rank + 1), rank)
        wide[:, lane : lane + width] = jnp.where(mask, lowrank, zeros)
    copies = []
    tiles, _, tile = staged.shape
    for number in range(tiles):
        place = pl.ds(number * tile, tile)
        delta = jnp.dot(wide[...], stack[:, place], preferred_element_type=jnp.float32)
        total = bases[number][...] + delta.astype(jnp.bfloat16).astype(jnp.float32)
        staged[number] = total.astype(out.dtype)
        copies.append(
            pltpu.make_async_copy(staged.at[number], out.at[:, place], sems.at[number])
        )
        copies[-1].start()
    for copy in copies:
        copy.wait()


def on_device(latent, row_adapter_index, shared_weight, adapter_down_weight, adapter_up_weight):
    rows, half_width = latent.shape
    out_width = shared_weight.shape[1]
    local_adapters, _, rank = adapter_down_weight.shape
    shards = lax.axis_size("shard")
    adapters = shards * local_adapters
    columns = adapters * rank
    index, core = lax.axis_index("shard"), lax.axis_index("tensor")
    holds_down = core == lax.axis_index("replica")
    tiles = out_width // TILE
    cuts = [0, out_width // 6, out_width * 2 // 3, out_width]
    down = jnp.swapaxes(adapter_down_weight, 1, 2).reshape(local_adapters * rank, half_width)
    up = adapter_up_weight.reshape(local_adapters * rank, out_width)
    ids = row_adapter_index
    routed = shards == 8 and local_adapters == 1 and lax.axis_size("replica") == 2
    routed = routed and half_width == out_width and tiles % 6 == 0
    lowrank = jax.ShapeDtypeStruct((rows, 2 * rank), jnp.float32)
    if routed:
        sources = [ring_step(index, -step) for step in (0, 1, 3, 2)]
        owners = [a for source in sources for a in (source, source ^ 1)]
    else:
        owners = list(range(adapters))
    info = jnp.stack([jnp.asarray(v, jnp.int32) for v in (core, holds_down, *owners)])
    if routed:
        piece = jnp.where(holds_down, down, up)
        line = {step: along_line(piece, shards, step) for step in (1, 3)}
        other = swap(latent, "tensor")
        down_beside, up_beside = neighbour(down, shards), neighbour(up, shards)
        parts = []
        part, token = base(info, latent, other, shared_weight, [ids], cuts[0], cuts[1])
        parts.append(part)
        line[2] = along_line(line[1], shards, 1)
        early, token = pack([(line[1], 0, rank), (line[3], 0, rank)], token, down_beside, up_beside)
        part, token = base(info, latent, other, shared_weight, [token], cuts[1], cuts[2])
        parts.append(part)
        early_first, early_second = in_plane(early, shards, True), in_plane(early, shards, False)
        late, token = pack([(line[2], 0, rank)], token)
        part, token = base(info, latent, other, shared_weight, [token], cuts[2], cuts[3])
        parts.append(part)
        late_second = in_plane(late, shards, False)
        turn, token = pack([(early_first, 0, rank)], token)
        corner_one = in_plane(turn, shards, False)
        late_first = along_line(turn, shards, 1)
        turn, token = pack([(early_second, rank, rank)], token)
        corner_two = in_plane(turn, shards, True)
        turn, token = pack([(late_second, 0, rank)], token)
        corner_three = in_plane(turn, shards, True)
        corners = [corner_one, corner_two, corner_three]
        received = [early, early_first, early_second, late, late_first, late_second]
        mine = call(
            down_first_kernel,
            lowrank,
            [SMEM] + [VMEM] * 10 + [ANY],
            16,
            [pltpu.VMEM((columns, half_width), latent.dtype)],
        )(info, ids, latent, down, down_beside, *received, token)
        mine = call(
            down_last_kernel,
            lowrank,
            [SMEM] + [VMEM] * 6,
            16,
            [pltpu.VMEM((4 * rank, half_width), latent.dtype)],
        )(info, ids, latent, mine, *corners)
        up_pieces = [up, up_beside, *received, *corners]
    else:
        other = swap(latent, "tensor")
        parts, token = [], ids
        for begin, end in zip(cuts[:-1], cuts[1:]):
            part, token = base(info, latent, other, shared_weight, [token], begin, end)
            parts.append(part)
        mine = call(down_whole_kernel, lowrank, [SMEM] + [VMEM] * 3, 48)(
            info, ids, latent, lax.all_gather(down, "shard", axis=0, tiled=True)
        )
        up_pieces = [lax.all_gather(up, "shard", axis=0, tiled=True)]
    theirs = swap(mine, "tensor")

    return pl.pallas_call(
        lambda *refs: up_kernel(*refs, base_parts=len(parts)),
        out_shape=jax.ShapeDtypeStruct((rows, out_width), latent.dtype),
        in_specs=[SMEM] + [VMEM] * (3 + len(parts) + len(up_pieces)),
        out_specs=ANY,
        scratch_shapes=[
            pltpu.VMEM((columns, out_width), latent.dtype),
            pltpu.VMEM((rows, columns), latent.dtype),
            pltpu.SemaphoreType.DMA((tiles,)),
            pltpu.VMEM((tiles, rows, TILE), latent.dtype),
        ],
        compiler_params=pltpu.CompilerParams(vmem_limit_bytes=(24 if routed else 56) * MIB),
    )(info, ids, mine, theirs, *parts, *up_pieces)


def solution(mesh):
    return jax.shard_map(
        on_device,
        mesh=mesh,
        in_specs=(
            P(("replica", "shard"), "tensor"),
            P(("replica", "shard"), None),
            P(None, "tensor"),
            P("shard", "tensor", None),
            P("shard", None, "tensor"),
        ),
        out_specs=P(("replica", "shard"), "tensor"),
        check_vma=False,
    )
```

```python
import jax
import jax.numpy as jnp
import numpy as np
from jax import lax
from jax.experimental import pallas as pl
from jax.experimental.pallas import tpu as pltpu
from jax.sharding import PartitionSpec as P

MIB = 1024 * 1024
CHUNK = 512
TILE = 256
AXES = ("replica", "shard", "tensor")
FIRST_OWNER = 2
SMEM = pl.BlockSpec(memory_space=pltpu.SMEM)
VMEM = pl.BlockSpec(memory_space=pltpu.VMEM)
ANY = pl.BlockSpec(memory_space=pl.ANY)
TOKEN = jax.ShapeDtypeStruct((8, 128), jnp.float32)


def swap(value, axis):
    return lax.ppermute(value, axis, [(0, 1), (1, 0)])


def neighbour(value, shards):
    return lax.ppermute(value, "shard", [(i, i ^ 1) for i in range(shards)])


def ring_step(index, step):
    plane = index >> 1
    place = ((plane ^ (plane >> 1)) + step) & 3
    return ((place ^ (place >> 1)) << 1) | (index & 1)


def along_line(value, shards, step):
    return lax.ppermute(value, "shard", [(i, ring_step(i, step)) for i in range(shards)])


def in_plane(value, shards, first):
    pairs = []
    for r in range(2):
        for s in range(shards):
            for t in range(2):
                to_r, to_s = (r, s ^ 1) if (t == 0) == first else (r ^ 1, s)
                pairs.append(((r * shards + s) * 2 + t, (to_r * shards + to_s) * 2 + t))
    return lax.ppermute(value, AXES, pairs)


def call(kernel, out_shape, in_specs, limit, scratch=(), flops=0, moved=0):
    return pl.pallas_call(
        kernel,
        out_shape=out_shape,
        in_specs=in_specs,
        out_specs=jax.tree.map(lambda _: VMEM, out_shape),
        scratch_shapes=list(scratch),
        compiler_params=pltpu.CompilerParams(vmem_limit_bytes=limit * MIB),
        cost_estimate=pl.CostEstimate(flops=flops, bytes_accessed=moved, transcendentals=0),
    )


def owner_row(info, blocks, rank):
    place = lax.broadcasted_iota(jnp.int32, (1, len(blocks) * rank), 1) // rank
    row = jnp.full(place.shape, -1, jnp.int32)
    for number, block in enumerate(blocks):
        if block is not None:
            row = jnp.where(place == number, info[FIRST_OWNER + block], row)
    return row


def pack(pieces, *after):
    count = len(pieces)
    total = sum(rows for _, _, rows in pieces)
    width, dtype = pieces[0][0].shape[1], pieces[0][0].dtype

    def kernel(*refs):
        out, token = refs[-2:]
        top = 0
        for ref, (_, begin, rows) in zip(refs, pieces):
            out[top : top + rows, :] = ref[begin : begin + rows, :]
            top += rows
        token[...] = jnp.zeros_like(token)

    return call(
        kernel,
        [jax.ShapeDtypeStruct((total, width), dtype), TOKEN],
        [VMEM] * count + [ANY] * len(after),
        4,
    )(*[array for array, _, _ in pieces], *after)


def put(blocks, stack, top, rank):
    for number, parts in enumerate(blocks):
        place = top + 2 * number * rank
        for ref, begin, rows in parts:
            stack[place : place + rows, :] = ref[begin : begin + rows, :]
            place += rows


def fill_here(info, holds, received, stack, top, rank):
    early, early_first, early_second, late, late_first, late_second, *_ = received

    def blocks(pair, single):
        return [[(pair, 0, rank)], [(pair, rank, rank)], [(single, 0, rank)]]

    swapped = ((early_second, late_second), (early_first, late_first))
    pl.when(holds)(lambda: put(blocks(early, late), stack, top, rank))
    for core in range(2):
        away = jnp.logical_not(holds) & (info[0] == core)
        pl.when(away)(lambda refs=swapped[core]: put(blocks(*refs), stack, top, rank))


def fill_beside(info, holds, received, stack, top, rank, direct=True, corner=True):
    _, early_first, early_second, _, late_first, late_second, *corners = received
    swapped = ((early_first, late_first), (early_second, late_second))
    if direct:
        for core in range(2):

            def straight(refs=swapped[core]):
                pair, single = refs
                blocks = [[(pair, 0, rank)], [(pair, rank, rank)], [(single, 0, rank)]]
                put(blocks, stack, top, rank)

            pl.when(holds & (info[0] == core))(straight)
    if corner:
        blocks = [[(ref, 0, rank)] for ref in corners]
        pl.when(jnp.logical_not(holds))(lambda: put(blocks, stack, top, rank))


def clear(stack, top, rank, count):
    for number in range(count):
        place = top + 2 * number * rank
        stack[place : place + rank, :] = jnp.zeros((rank, stack.shape[1]), stack.dtype)


def masked_products(info, ids, latent, stack, blocks, rank):
    total = None
    width = 2 * rank
    for skip in range(0, stack.shape[0], CHUNK):
        count = min(CHUNK, stack.shape[0] - skip)
        part = lax.dot_general(
            latent[...],
            stack[skip : skip + count, :],
            (((1,), (1,)), ((), ())),
            preferred_element_type=jnp.float32,
        )
        owners = owner_row(info, blocks[skip // rank : (skip + count) // rank], rank)
        part = jnp.where(ids[...] == owners, part, 0.0)
        for lane in range(0, count, width):
            fold = part[:, lane : lane + width]
            total = fold if total is None else total + fold
    return total


def down_whole_kernel(info, ids, latent, stack, out):
    rank = out.shape[1] // 2
    blocks = range(stack.shape[0] // rank)
    out[...] = masked_products(info, ids, latent, stack, blocks, rank)


def down_first_kernel(info, ids, latent, own, beside, *refs):
    *received, _, out, stack = refs
    rank = own.shape[0]
    holds = info[1] == 1
    stack[0:rank, :] = own[...]
    stack[rank : 2 * rank, :] = beside[...]
    fill_here(info, holds, received, stack, 2 * rank, rank)
    fill_beside(info, holds, received, stack, 3 * rank, rank, corner=False)
    pl.when(jnp.logical_not(holds))(lambda: clear(stack, 3 * rank, rank, 3))
    out[...] = masked_products(info, ids, latent, stack, range(stack.shape[0] // rank), rank)


def down_last_kernel(info, ids, latent, earlier, *refs):
    *corners, out, stack = refs
    rank = out.shape[1] // 2
    holds = info[1] == 1

    @pl.when(holds)
    def _():
        out[...] = earlier[...]

    @pl.when(jnp.logical_not(holds))
    def _():
        for number, corner in enumerate(corners):
            stack[number * rank : (number + 1) * rank, :] = corner[...]
        stack[3 * rank : 4 * rank, :] = jnp.zeros((rank, stack.shape[1]), stack.dtype)
        pair = masked_products(info, ids, latent, stack, (3, 5, 7, None), rank)
        fold = pair[:, :rank] + pair[:, rank:]
        out[...] = earlier[...] + jnp.concatenate([jnp.zeros_like(fold), fold], axis=1)


def base_kernel(info, own, other, weight, *refs, skip):
    out, token = refs[-2:]
    token[...] = jnp.zeros_like(token)
    width = own.shape[1]
    mine = pl.ds(pl.multiple_of(info[0] * width, width), width)
    rest = pl.ds(pl.multiple_of((1 - info[0]) * width, width), width)
    step = min(CHUNK, out.shape[1])
    for begin in range(0, out.shape[1], step):
        place = slice(begin, min(begin + step, out.shape[1]))
        source = slice(skip + begin, skip + place.stop)
        out[:, place] = jnp.dot(
            own[...], weight[mine, source], preferred_element_type=jnp.float32
        ) + jnp.dot(other[...], weight[rest, source], preferred_element_type=jnp.float32)


def base(info, latent, other, weight, after, skip, end):
    rows, columns = latent.shape[0], end - skip
    return pl.pallas_call(
        lambda *refs: base_kernel(*refs, skip=skip),
        out_shape=[jax.ShapeDtypeStruct((rows, columns), jnp.float32), TOKEN],
        in_specs=[SMEM, VMEM, VMEM, VMEM] + [ANY] * len(after),
        out_specs=[VMEM, VMEM],
        compiler_params=pltpu.CompilerParams(vmem_limit_bytes=24 * MIB),
        cost_estimate=pl.CostEstimate(flops=1000, bytes_accessed=1000, transcendentals=0),
    )(info, latent, other, weight, *after)


def up_kernel(info, ids, mine, theirs, *refs, base_parts):
    *pieces, out, stack, wide, sems, staged = refs[base_parts:]
    bases = [
        part.at[:, pl.ds(begin, TILE)]
        for part in refs[:base_parts]
        for begin in range(0, part.shape[1], TILE)
    ]
    rank = mine.shape[1] // 2
    if len(pieces) == 1:
        stack[...] = pieces[0][...]
    else:
        own, beside, *received = pieces
        holds = info[1] == 0
        stack[0:rank, :] = own[...]
        stack[rank : 2 * rank, :] = beside[...]
        fill_here(info, holds, received, stack, 2 * rank, rank)
        fill_beside(info, holds, received, stack, 3 * rank, rank)
    lowrank = (mine[...] + theirs[...]).astype(jnp.bfloat16)
    zeros = jnp.zeros_like(lowrank)
    width = 2 * rank
    for lane in range(0, wide.shape[1], width):
        mask = ids[...] == owner_row(info, (lane // rank, lane // rank + 1), rank)
        wide[:, lane : lane + width] = jnp.where(mask, lowrank, zeros)
    copies = []
    tiles, _, tile = staged.shape
    for number in range(tiles):
        place = pl.ds(number * tile, tile)
        delta = jnp.dot(wide[...], stack[:, place], preferred_element_type=jnp.float32)
        total = bases[number][...] + delta.astype(jnp.bfloat16).astype(jnp.float32)
        staged[number] = total.astype(out.dtype)
        copies.append(
            pltpu.make_async_copy(staged.at[number], out.at[:, place], sems.at[number])
        )
        copies[-1].start()
    for copy in copies:
        copy.wait()


def on_device(latent, row_adapter_index, shared_weight, adapter_down_weight, adapter_up_weight):
    rows, half_width = latent.shape
    out_width = shared_weight.shape[1]
    local_adapters, _, rank = adapter_down_weight.shape
    shards = lax.axis_size("shard")
    adapters = shards * local_adapters
    columns = adapters * rank
    index, core = lax.axis_index("shard"), lax.axis_index("tensor")
    holds_down = core == lax.axis_index("replica")
    tiles = out_width // TILE
    cuts = [0, out_width // 6, out_width * 2 // 3, out_width]
    down = jnp.swapaxes(adapter_down_weight, 1, 2).reshape(local_adapters * rank, half_width)
    up = adapter_up_weight.reshape(local_adapters * rank, out_width)
    ids = row_adapter_index
    routed = shards == 8 and local_adapters == 1 and lax.axis_size("replica") == 2
    routed = routed and half_width == out_width and tiles % 6 == 0
    lowrank = jax.ShapeDtypeStruct((rows, 2 * rank), jnp.float32)
    if routed:
        sources = [ring_step(index, -step) for step in (0, 1, 3, 2)]
        owners = [a for source in sources for a in (source, source ^ 1)]
    else:
        owners = list(range(adapters))
    info = jnp.stack([jnp.asarray(v, jnp.int32) for v in (core, holds_down, *owners)])
    if routed:
        piece = jnp.where(holds_down, down, up)
        line = {step: along_line(piece, shards, step) for step in (1, 3)}
        other = swap(latent, "tensor")
        down_beside, up_beside = neighbour(down, shards), neighbour(up, shards)
        parts = []
        part, token = base(info, latent, other, shared_weight, [ids], cuts[0], cuts[1])
        parts.append(part)
        line[2] = along_line(line[1], shards, 1)
        early, token = pack([(line[1], 0, rank), (line[3], 0, rank)], token, down_beside, up_beside)
        part, token = base(info, latent, other, shared_weight, [token], cuts[1], cuts[2])
        parts.append(part)
        early_first, early_second = in_plane(early, shards, True), in_plane(early, shards, False)
        late, token = pack([(line[2], 0, rank)], token)
        late_second = in_plane(late, shards, False)
        turn, token = pack([(early_first, 0, rank)], token)
        corner_one = in_plane(turn, shards, False)
        late_first = along_line(turn, shards, 1)
        turn, token = pack([(early_second, rank, rank)], token)
        corner_two = in_plane(turn, shards, True)
        turn, token = pack([(late_second, 0, rank)], token)
        corner_three = in_plane(turn, shards, True)
        part, token = base(info, latent, other, shared_weight, [token], cuts[2], cuts[3])
        parts.append(part)
        corners = [corner_one, corner_two, corner_three]
        received = [early, early_first, early_second, late, late_first, late_second]
        mine = call(
            down_first_kernel,
            lowrank,
            [SMEM] + [VMEM] * 10 + [ANY],
            16,
            [pltpu.VMEM((columns, half_width), latent.dtype)],
        )(info, ids, latent, down, down_beside, *received, token)
        mine = call(
            down_last_kernel,
            lowrank,
            [SMEM] + [VMEM] * 6,
            16,
            [pltpu.VMEM((4 * rank, half_width), latent.dtype)],
        )(info, ids, latent, mine, *corners)
        up_pieces = [up, up_beside, *received, *corners]
    else:
        other = swap(latent, "tensor")
        parts, token = [], ids
        for begin, end in zip(cuts[:-1], cuts[1:]):
            part, token = base(info, latent, other, shared_weight, [token], begin, end)
            parts.append(part)
        mine = call(down_whole_kernel, lowrank, [SMEM] + [VMEM] * 3, 48)(
            info, ids, latent, lax.all_gather(down, "shard", axis=0, tiled=True)
        )
        up_pieces = [lax.all_gather(up, "shard", axis=0, tiled=True)]
    theirs = swap(mine, "tensor")

    return pl.pallas_call(
        lambda *refs: up_kernel(*refs, base_parts=len(parts)),
        out_shape=jax.ShapeDtypeStruct((rows, out_width), latent.dtype),
        in_specs=[SMEM] + [VMEM] * (3 + len(parts) + len(up_pieces)),
        out_specs=ANY,
        scratch_shapes=[
            pltpu.VMEM((columns, out_width), latent.dtype),
            pltpu.VMEM((rows, columns), latent.dtype),
            pltpu.SemaphoreType.DMA((tiles,)),
            pltpu.VMEM((tiles, rows, TILE), latent.dtype),
        ],
        compiler_params=pltpu.CompilerParams(vmem_limit_bytes=(24 if routed else 56) * MIB),
    )(info, ids, mine, theirs, *parts, *up_pieces)


def solution(mesh):
    return jax.shard_map(
        on_device,
        mesh=mesh,
        in_specs=(
            P(("replica", "shard"), "tensor"),
            P(("replica", "shard"), None),
            P(None, "tensor"),
            P("shard", "tensor", None),
            P("shard", None, "tensor"),
        ),
        out_specs=P(("replica", "shard"), "tensor"),
        check_vma=False,
    )
```

```python
import jax
import jax.numpy as jnp
import numpy as np
from jax import lax
from jax.experimental import pallas as pl
from jax.experimental.pallas import tpu as pltpu
from jax.sharding import PartitionSpec as P

MIB = 1024 * 1024
CHUNK = 512
TILE = 256
AXES = ("replica", "shard", "tensor")
FIRST_OWNER = 2
SMEM = pl.BlockSpec(memory_space=pltpu.SMEM)
VMEM = pl.BlockSpec(memory_space=pltpu.VMEM)
ANY = pl.BlockSpec(memory_space=pl.ANY)
TOKEN = jax.ShapeDtypeStruct((8, 128), jnp.float32)


def swap(value, axis):
    return lax.ppermute(value, axis, [(0, 1), (1, 0)])


def neighbour(value, shards):
    return lax.ppermute(value, "shard", [(i, i ^ 1) for i in range(shards)])


def ring_step(index, step):
    plane = index >> 1
    place = ((plane ^ (plane >> 1)) + step) & 3
    return ((place ^ (place >> 1)) << 1) | (index & 1)


def along_line(value, shards, step):
    return lax.ppermute(value, "shard", [(i, ring_step(i, step)) for i in range(shards)])


def in_plane(value, shards, first):
    pairs = []
    for r in range(2):
        for s in range(shards):
            for t in range(2):
                to_r, to_s = (r, s ^ 1) if (t == 0) == first else (r ^ 1, s)
                pairs.append(((r * shards + s) * 2 + t, (to_r * shards + to_s) * 2 + t))
    return lax.ppermute(value, AXES, pairs)


def call(kernel, out_shape, in_specs, limit, scratch=(), flops=0, moved=0):
    return pl.pallas_call(
        kernel,
        out_shape=out_shape,
        in_specs=in_specs,
        out_specs=jax.tree.map(lambda _: VMEM, out_shape),
        scratch_shapes=list(scratch),
        compiler_params=pltpu.CompilerParams(vmem_limit_bytes=limit * MIB),
        cost_estimate=pl.CostEstimate(flops=flops, bytes_accessed=moved, transcendentals=0),
    )


def owner_row(info, blocks, rank):
    place = lax.broadcasted_iota(jnp.int32, (1, len(blocks) * rank), 1) // rank
    row = jnp.full(place.shape, -1, jnp.int32)
    for number, block in enumerate(blocks):
        if block is not None:
            row = jnp.where(place == number, info[FIRST_OWNER + block], row)
    return row


def pack(pieces, *after):
    count = len(pieces)
    total = sum(rows for _, _, rows in pieces)
    width, dtype = pieces[0][0].shape[1], pieces[0][0].dtype

    def kernel(*refs):
        out, token = refs[-2:]
        top = 0
        for ref, (_, begin, rows) in zip(refs, pieces):
            out[top : top + rows, :] = ref[begin : begin + rows, :]
            top += rows
        token[...] = jnp.zeros_like(token)

    return call(
        kernel,
        [jax.ShapeDtypeStruct((total, width), dtype), TOKEN],
        [VMEM] * count + [ANY] * len(after),
        4,
    )(*[array for array, _, _ in pieces], *after)


def put(blocks, stack, top, rank):
    for number, block in enumerate(blocks):
        place = top + 2 * number * rank
        stack[place : place + rank, :] = block[...]


def fill_here(info, holds, received, stack, top, rank):
    here, first, second = received[0:3], received[3:6], received[6:9]
    pl.when(holds)(lambda: put(here, stack, top, rank))
    for core, refs in enumerate((second, first)):
        away = jnp.logical_not(holds) & (info[0] == core)
        pl.when(away)(lambda refs=refs: put(refs, stack, top, rank))


def fill_beside(info, holds, received, stack, top, rank, direct=True, corner=True):
    if direct:
        for core, refs in enumerate((received[3:6], received[6:9])):
            pl.when(holds & (info[0] == core))(lambda refs=refs: put(refs, stack, top, rank))
    if corner:
        corners = received[9:12]
        pl.when(jnp.logical_not(holds))(lambda: put(corners, stack, top, rank))


def clear(stack, top, rank, count):
    for number in range(count):
        place = top + 2 * number * rank
        stack[place : place + rank, :] = jnp.zeros((rank, stack.shape[1]), stack.dtype)


def masked_products(info, ids, latent, stack, blocks, rank):
    total = None
    width = 2 * rank
    for skip in range(0, stack.shape[0], CHUNK):
        count = min(CHUNK, stack.shape[0] - skip)
        part = lax.dot_general(
            latent[...],
            stack[skip : skip + count, :],
            (((1,), (1,)), ((), ())),
            preferred_element_type=jnp.float32,
        )
        owners = owner_row(info, blocks[skip // rank : (skip + count) // rank], rank)
        part = jnp.where(ids[...] == owners, part, 0.0)
        for lane in range(0, count, width):
            fold = part[:, lane : lane + width]
            total = fold if total is None else total + fold
    return total


def down_whole_kernel(info, ids, latent, stack, out):
    rank = out.shape[1] // 2
    blocks = range(stack.shape[0] // rank)
    out[...] = masked_products(info, ids, latent, stack, blocks, rank)


def down_first_kernel(info, ids, latent, own, beside, *refs):
    *received, _, out, stack = refs
    rank = own.shape[0]
    holds = info[1] == 1
    stack[0:rank, :] = own[...]
    stack[rank : 2 * rank, :] = beside[...]
    fill_here(info, holds, received, stack, 2 * rank, rank)
    fill_beside(info, holds, received, stack, 3 * rank, rank, corner=False)
    pl.when(jnp.logical_not(holds))(lambda: clear(stack, 3 * rank, rank, 3))
    out[...] = masked_products(info, ids, latent, stack, range(stack.shape[0] // rank), rank)


def down_last_kernel(info, ids, latent, earlier, *refs):
    *corners, out, stack = refs
    rank = out.shape[1] // 2
    holds = info[1] == 1

    @pl.when(holds)
    def _():
        out[...] = earlier[...]

    @pl.when(jnp.logical_not(holds))
    def _():
        for number, corner in enumerate(corners):
            stack[number * rank : (number + 1) * rank, :] = corner[...]
        stack[3 * rank : 4 * rank, :] = jnp.zeros((rank, stack.shape[1]), stack.dtype)
        pair = masked_products(info, ids, latent, stack, (3, 5, 7, None), rank)
        fold = pair[:, :rank] + pair[:, rank:]
        out[...] = earlier[...] + jnp.concatenate([jnp.zeros_like(fold), fold], axis=1)


def base_kernel(info, own, other, weight, *refs, skip):
    out, token = refs[-2:]
    token[...] = jnp.zeros_like(token)
    width = own.shape[1]
    mine = pl.ds(pl.multiple_of(info[0] * width, width), width)
    rest = pl.ds(pl.multiple_of((1 - info[0]) * width, width), width)
    step = min(CHUNK, out.shape[1])
    for begin in range(0, out.shape[1], step):
        place = slice(begin, min(begin + step, out.shape[1]))
        source = slice(skip + begin, skip + place.stop)
        out[:, place] = jnp.dot(
            own[...], weight[mine, source], preferred_element_type=jnp.float32
        ) + jnp.dot(other[...], weight[rest, source], preferred_element_type=jnp.float32)


def base(info, latent, other, weight, after, skip, end):
    rows, columns = latent.shape[0], end - skip
    return pl.pallas_call(
        lambda *refs: base_kernel(*refs, skip=skip),
        out_shape=[jax.ShapeDtypeStruct((rows, columns), jnp.float32), TOKEN],
        in_specs=[SMEM, VMEM, VMEM, VMEM] + [ANY] * len(after),
        out_specs=[VMEM, VMEM],
        compiler_params=pltpu.CompilerParams(vmem_limit_bytes=24 * MIB),
        cost_estimate=pl.CostEstimate(flops=1000, bytes_accessed=1000, transcendentals=0),
    )(info, latent, other, weight, *after)


def up_kernel(info, ids, mine, theirs, *refs, base_parts):
    *pieces, out, stack, wide, sems, staged = refs[base_parts:]
    bases = [
        part.at[:, pl.ds(begin, TILE)]
        for part in refs[:base_parts]
        for begin in range(0, part.shape[1], TILE)
    ]
    rank = mine.shape[1] // 2
    if len(pieces) == 1:
        stack[...] = pieces[0][...]
    else:
        own, beside, *received = pieces
        holds = info[1] == 0
        stack[0:rank, :] = own[...]
        stack[rank : 2 * rank, :] = beside[...]
        fill_here(info, holds, received, stack, 2 * rank, rank)
        fill_beside(info, holds, received, stack, 3 * rank, rank)
    lowrank = (mine[...] + theirs[...]).astype(jnp.bfloat16)
    zeros = jnp.zeros_like(lowrank)
    width = 2 * rank
    for lane in range(0, wide.shape[1], width):
        mask = ids[...] == owner_row(info, (lane // rank, lane // rank + 1), rank)
        wide[:, lane : lane + width] = jnp.where(mask, lowrank, zeros)
    copies = []
    tiles, _, tile = staged.shape
    for number in range(tiles):
        place = pl.ds(number * tile, tile)
        delta = jnp.dot(wide[...], stack[:, place], preferred_element_type=jnp.float32)
        total = bases[number][...] + delta.astype(jnp.bfloat16).astype(jnp.float32)
        staged[number] = total.astype(out.dtype)
        copies.append(
            pltpu.make_async_copy(staged.at[number], out.at[:, place], sems.at[number])
        )
        copies[-1].start()
    for copy in copies:
        copy.wait()


def on_device(latent, row_adapter_index, shared_weight, adapter_down_weight, adapter_up_weight):
    rows, half_width = latent.shape
    out_width = shared_weight.shape[1]
    local_adapters, _, rank = adapter_down_weight.shape
    shards = lax.axis_size("shard")
    adapters = shards * local_adapters
    columns = adapters * rank
    index, core = lax.axis_index("shard"), lax.axis_index("tensor")
    holds_down = core == lax.axis_index("replica")
    tiles = out_width // TILE
    cuts = [0, out_width // 6, out_width * 2 // 3, out_width]
    down = jnp.swapaxes(adapter_down_weight, 1, 2).reshape(local_adapters * rank, half_width)
    up = adapter_up_weight.reshape(local_adapters * rank, out_width)
    ids = row_adapter_index
    routed = shards == 8 and local_adapters == 1 and lax.axis_size("replica") == 2
    routed = routed and half_width == out_width and tiles % 6 == 0
    lowrank = jax.ShapeDtypeStruct((rows, 2 * rank), jnp.float32)
    if routed:
        sources = [ring_step(index, -step) for step in (0, 1, 3, 2)]
        owners = [a for source in sources for a in (source, source ^ 1)]
    else:
        owners = list(range(adapters))
    info = jnp.stack([jnp.asarray(v, jnp.int32) for v in (core, holds_down, *owners)])
    if routed:
        piece = jnp.where(holds_down, down, up)
        line = {step: along_line(piece, shards, step) for step in (1, 3)}
        other = swap(latent, "tensor")
        down_beside, up_beside = neighbour(down, shards), neighbour(up, shards)
        parts = []
        part, token = base(info, latent, other, shared_weight, [ids], cuts[0], cuts[1])
        parts.append(part)
        one, token = pack([(line[1], 0, rank)], token, down_beside)
        line[2] = along_line(one, shards, 1)
        one_first, one_second = in_plane(one, shards, True), in_plane(one, shards, False)
        three, token = pack([(line[3], 0, rank)], token, up_beside)
        three_first, three_second = in_plane(three, shards, True), in_plane(three, shards, False)
        part, token = base(info, latent, other, shared_weight, [token], cuts[1], cuts[2])
        parts.append(part)
        two, token = pack([(line[2], 0, rank)], token)
        two_second = in_plane(two, shards, False)
        turn, token = pack([(one_first, 0, rank)], token, one_second)
        corner_one = in_plane(turn, shards, False)
        two_first = along_line(turn, shards, 1)
        turn, token = pack([(three_second, 0, rank)], token, three_first)
        corner_three = in_plane(turn, shards, True)
        turn, token = pack([(two_second, 0, rank)], token)
        corner_two = in_plane(turn, shards, True)
        part, token = base(info, latent, other, shared_weight, [token], cuts[2], cuts[3])
        parts.append(part)
        corners = [corner_one, corner_three, corner_two]
        received = [one, three, two, one_first, three_first, two_first]
        received += [one_second, three_second, two_second]
        mine = call(
            down_first_kernel,
            lowrank,
            [SMEM] + [VMEM] * 13 + [ANY],
            16,
            [pltpu.VMEM((columns, half_width), latent.dtype)],
        )(info, ids, latent, down, down_beside, *received, token)
        mine = call(
            down_last_kernel,
            lowrank,
            [SMEM] + [VMEM] * 6,
            16,
            [pltpu.VMEM((4 * rank, half_width), latent.dtype)],
        )(info, ids, latent, mine, *corners)
        up_pieces = [up, up_beside, *received, *corners]
    else:
        other = swap(latent, "tensor")
        parts, token = [], ids
        for begin, end in zip(cuts[:-1], cuts[1:]):
            part, token = base(info, latent, other, shared_weight, [token], begin, end)
            parts.append(part)
        mine = call(down_whole_kernel, lowrank, [SMEM] + [VMEM] * 3, 48)(
            info, ids, latent, lax.all_gather(down, "shard", axis=0, tiled=True)
        )
        up_pieces = [lax.all_gather(up, "shard", axis=0, tiled=True)]
    theirs = swap(mine, "tensor")

    return pl.pallas_call(
        lambda *refs: up_kernel(*refs, base_parts=len(parts)),
        out_shape=jax.ShapeDtypeStruct((rows, out_width), latent.dtype),
        in_specs=[SMEM] + [VMEM] * (3 + len(parts) + len(up_pieces)),
        out_specs=ANY,
        scratch_shapes=[
            pltpu.VMEM((columns, out_width), latent.dtype),
            pltpu.VMEM((rows, columns), latent.dtype),
            pltpu.SemaphoreType.DMA((tiles,)),
            pltpu.VMEM((tiles, rows, TILE), latent.dtype),
        ],
        compiler_params=pltpu.CompilerParams(vmem_limit_bytes=(24 if routed else 56) * MIB),
    )(info, ids, mine, theirs, *parts, *up_pieces)


def solution(mesh):
    return jax.shard_map(
        on_device,
        mesh=mesh,
        in_specs=(
            P(("replica", "shard"), "tensor"),
            P(("replica", "shard"), None),
            P(None, "tensor"),
            P("shard", "tensor", None),
            P("shard", None, "tensor"),
        ),
        out_specs=P(("replica", "shard"), "tensor"),
        check_vma=False,
    )
```

```python
import jax
import jax.numpy as jnp
import numpy as np
from jax import lax
from jax.experimental import pallas as pl
from jax.experimental.pallas import tpu as pltpu
from jax.sharding import PartitionSpec as P

MIB = 1024 * 1024
CHUNK = 512
TILE = 256
AXES = ("replica", "shard", "tensor")
FIRST_OWNER = 2
SMEM = pl.BlockSpec(memory_space=pltpu.SMEM)
VMEM = pl.BlockSpec(memory_space=pltpu.VMEM)
ANY = pl.BlockSpec(memory_space=pl.ANY)
TOKEN = jax.ShapeDtypeStruct((8, 128), jnp.float32)


def swap(value, axis):
    return lax.ppermute(value, axis, [(0, 1), (1, 0)])


def neighbour(value, shards):
    return lax.ppermute(value, "shard", [(i, i ^ 1) for i in range(shards)])


def ring_step(index, step):
    plane = index >> 1
    place = ((plane ^ (plane >> 1)) + step) & 3
    return ((place ^ (place >> 1)) << 1) | (index & 1)


def along_line(value, shards, step):
    return lax.ppermute(value, "shard", [(i, ring_step(i, step)) for i in range(shards)])


def in_plane(value, shards, first):
    pairs = []
    for r in range(2):
        for s in range(shards):
            for t in range(2):
                to_r, to_s = (r, s ^ 1) if (t == 0) == first else (r ^ 1, s)
                pairs.append(((r * shards + s) * 2 + t, (to_r * shards + to_s) * 2 + t))
    return lax.ppermute(value, AXES, pairs)


def call(kernel, out_shape, in_specs, limit, scratch=(), flops=0, moved=0):
    return pl.pallas_call(
        kernel,
        out_shape=out_shape,
        in_specs=in_specs,
        out_specs=jax.tree.map(lambda _: VMEM, out_shape),
        scratch_shapes=list(scratch),
        compiler_params=pltpu.CompilerParams(vmem_limit_bytes=limit * MIB),
        cost_estimate=pl.CostEstimate(flops=flops, bytes_accessed=moved, transcendentals=0),
    )


def owner_row(info, blocks, rank):
    place = lax.broadcasted_iota(jnp.int32, (1, len(blocks) * rank), 1) // rank
    row = jnp.full(place.shape, -1, jnp.int32)
    for number, block in enumerate(blocks):
        if block is not None:
            row = jnp.where(place == number, info[FIRST_OWNER + block], row)
    return row


def pack(pieces, *after):
    count = len(pieces)
    total = sum(rows for _, _, rows in pieces)
    width, dtype = pieces[0][0].shape[1], pieces[0][0].dtype

    def kernel(*refs):
        out, token = refs[-2:]
        top = 0
        for ref, (_, begin, rows) in zip(refs, pieces):
            out[top : top + rows, :] = ref[begin : begin + rows, :]
            top += rows
        token[...] = jnp.zeros_like(token)

    return call(
        kernel,
        [jax.ShapeDtypeStruct((total, width), dtype), TOKEN],
        [VMEM] * count + [ANY] * len(after),
        4,
    )(*[array for array, _, _ in pieces], *after)


def put(blocks, stack, top, rank):
    for number, block in enumerate(blocks):
        place = top + 2 * number * rank
        stack[place : place + rank, :] = block[...]


def fill_here(info, holds, received, stack, top, rank):
    here, first, second = received[0:3], received[3:6], received[6:9]
    pl.when(holds)(lambda: put(here, stack, top, rank))
    for core, refs in enumerate((second, first)):
        away = jnp.logical_not(holds) & (info[0] == core)
        pl.when(away)(lambda refs=refs: put(refs, stack, top, rank))


def fill_beside(info, holds, received, stack, top, rank, direct=True, corner=True):
    if direct:
        for core, refs in enumerate((received[3:6], received[6:9])):
            pl.when(holds & (info[0] == core))(lambda refs=refs: put(refs, stack, top, rank))
    if corner:
        corners = received[9:12]
        pl.when(jnp.logical_not(holds))(lambda: put(corners, stack, top, rank))


def clear(stack, top, rank, count):
    for number in range(count):
        place = top + 2 * number * rank
        stack[place : place + rank, :] = jnp.zeros((rank, stack.shape[1]), stack.dtype)


def masked_products(info, ids, latent, stack, blocks, rank):
    total = None
    width = 2 * rank
    for skip in range(0, stack.shape[0], CHUNK):
        count = min(CHUNK, stack.shape[0] - skip)
        part = lax.dot_general(
            latent[...],
            stack[skip : skip + count, :],
            (((1,), (1,)), ((), ())),
            preferred_element_type=jnp.float32,
        )
        owners = owner_row(info, blocks[skip // rank : (skip + count) // rank], rank)
        part = jnp.where(ids[...] == owners, part, 0.0)
        for lane in range(0, count, width):
            fold = part[:, lane : lane + width]
            total = fold if total is None else total + fold
    return total


def down_whole_kernel(info, ids, latent, stack, out):
    rank = out.shape[1] // 2
    blocks = range(stack.shape[0] // rank)
    out[...] = masked_products(info, ids, latent, stack, blocks, rank)


def down_first_kernel(info, ids, latent, own, beside, *refs):
    *received, _, out, stack = refs
    rank = own.shape[0]
    holds = info[1] == 1
    stack[0:rank, :] = own[...]
    stack[rank : 2 * rank, :] = beside[...]
    fill_here(info, holds, received, stack, 2 * rank, rank)
    fill_beside(info, holds, received, stack, 3 * rank, rank, corner=False)
    pl.when(jnp.logical_not(holds))(lambda: clear(stack, 3 * rank, rank, 3))
    out[...] = masked_products(info, ids, latent, stack, range(stack.shape[0] // rank), rank)


def down_last_kernel(info, ids, latent, earlier, *refs):
    *corners, out, stack = refs
    rank = out.shape[1] // 2
    holds = info[1] == 1

    @pl.when(holds)
    def _():
        out[...] = earlier[...]

    @pl.when(jnp.logical_not(holds))
    def _():
        for number, corner in enumerate(corners):
            stack[number * rank : (number + 1) * rank, :] = corner[...]
        stack[3 * rank : 4 * rank, :] = jnp.zeros((rank, stack.shape[1]), stack.dtype)
        pair = masked_products(info, ids, latent, stack, (3, 5, 7, None), rank)
        fold = pair[:, :rank] + pair[:, rank:]
        out[...] = earlier[...] + jnp.concatenate([jnp.zeros_like(fold), fold], axis=1)


def base_kernel(info, own, other, weight, *refs, skip):
    out, token = refs[-2:]
    token[...] = jnp.zeros_like(token)
    width = own.shape[1]
    mine = pl.ds(pl.multiple_of(info[0] * width, width), width)
    rest = pl.ds(pl.multiple_of((1 - info[0]) * width, width), width)
    step = min(CHUNK, out.shape[1])
    for begin in range(0, out.shape[1], step):
        place = slice(begin, min(begin + step, out.shape[1]))
        source = slice(skip + begin, skip + place.stop)
        out[:, place] = jnp.dot(
            own[...], weight[mine, source], preferred_element_type=jnp.float32
        ) + jnp.dot(other[...], weight[rest, source], preferred_element_type=jnp.float32)


def base(info, latent, other, weight, after, skip, end):
    rows, columns = latent.shape[0], end - skip
    return pl.pallas_call(
        lambda *refs: base_kernel(*refs, skip=skip),
        out_shape=[jax.ShapeDtypeStruct((rows, columns), jnp.float32), TOKEN],
        in_specs=[SMEM, VMEM, VMEM, VMEM] + [ANY] * len(after),
        out_specs=[VMEM, VMEM],
        compiler_params=pltpu.CompilerParams(vmem_limit_bytes=24 * MIB),
        cost_estimate=pl.CostEstimate(flops=1000, bytes_accessed=1000, transcendentals=0),
    )(info, latent, other, weight, *after)


def up_kernel(info, ids, mine, theirs, *refs, base_parts):
    *pieces, out, stack, wide, sems, staged = refs[base_parts:]
    bases = [
        part.at[:, pl.ds(begin, TILE)]
        for part in refs[:base_parts]
        for begin in range(0, part.shape[1], TILE)
    ]
    rank = mine.shape[1] // 2
    if len(pieces) == 1:
        stack[...] = pieces[0][...]
    else:
        own, beside, *received = pieces
        holds = info[1] == 0
        stack[0:rank, :] = own[...]
        stack[rank : 2 * rank, :] = beside[...]
        fill_here(info, holds, received, stack, 2 * rank, rank)
        fill_beside(info, holds, received, stack, 3 * rank, rank)
    lowrank = (mine[...] + theirs[...]).astype(jnp.bfloat16)
    zeros = jnp.zeros_like(lowrank)
    width = 2 * rank
    for lane in range(0, wide.shape[1], width):
        mask = ids[...] == owner_row(info, (lane // rank, lane // rank + 1), rank)
        wide[:, lane : lane + width] = jnp.where(mask, lowrank, zeros)
    copies = []
    tiles, _, tile = staged.shape
    for number in range(tiles):
        place = pl.ds(number * tile, tile)
        delta = jnp.dot(wide[...], stack[:, place], preferred_element_type=jnp.float32)
        total = bases[number][...] + delta.astype(jnp.bfloat16).astype(jnp.float32)
        staged[number] = total.astype(out.dtype)
        copies.append(
            pltpu.make_async_copy(staged.at[number], out.at[:, place], sems.at[number])
        )
        copies[-1].start()
    for copy in copies:
        copy.wait()


def on_device(latent, row_adapter_index, shared_weight, adapter_down_weight, adapter_up_weight):
    rows, half_width = latent.shape
    out_width = shared_weight.shape[1]
    local_adapters, _, rank = adapter_down_weight.shape
    shards = lax.axis_size("shard")
    adapters = shards * local_adapters
    columns = adapters * rank
    index, core = lax.axis_index("shard"), lax.axis_index("tensor")
    holds_down = core == lax.axis_index("replica")
    tiles = out_width // TILE
    cuts = [0, out_width // 6, out_width * 2 // 3, out_width]
    down = jnp.swapaxes(adapter_down_weight, 1, 2).reshape(local_adapters * rank, half_width)
    up = adapter_up_weight.reshape(local_adapters * rank, out_width)
    ids = row_adapter_index
    routed = shards == 8 and local_adapters == 1 and lax.axis_size("replica") == 2
    routed = routed and half_width == out_width and tiles % 6 == 0
    lowrank = jax.ShapeDtypeStruct((rows, 2 * rank), jnp.float32)
    if routed:
        sources = [ring_step(index, -step) for step in (0, 1, 3, 2)]
        owners = [a for source in sources for a in (source, source ^ 1)]
    else:
        owners = list(range(adapters))
    info = jnp.stack([jnp.asarray(v, jnp.int32) for v in (core, holds_down, *owners)])
    if routed:
        piece = jnp.where(holds_down, down, up)
        line = {step: along_line(piece, shards, step) for step in (1, 3)}
        other = swap(latent, "tensor")
        down_beside, up_beside = neighbour(down, shards), neighbour(up, shards)
        parts = []
        one, token = pack([(line[1], 0, rank)], ids, info, down_beside)
        line[2] = along_line(one, shards, 1)
        one_first, one_second = in_plane(one, shards, True), in_plane(one, shards, False)
        part, token = base(info, latent, other, shared_weight, [token], cuts[0], cuts[1])
        parts.append(part)
        three, token = pack([(line[3], 0, rank)], token, up_beside)
        three_first, three_second = in_plane(three, shards, True), in_plane(three, shards, False)
        part, token = base(info, latent, other, shared_weight, [token], cuts[1], cuts[2])
        parts.append(part)
        two, token = pack([(line[2], 0, rank)], token)
        two_second = in_plane(two, shards, False)
        turn, token = pack([(one_first, 0, rank)], token, one_second)
        corner_one = in_plane(turn, shards, False)
        two_first = along_line(turn, shards, 1)
        turn, token = pack([(three_second, 0, rank)], token, three_first)
        corner_three = in_plane(turn, shards, True)
        turn, token = pack([(two_second, 0, rank)], token)
        corner_two = in_plane(turn, shards, True)
        part, token = base(info, latent, other, shared_weight, [token], cuts[2], cuts[3])
        parts.append(part)
        corners = [corner_one, corner_three, corner_two]
        received = [one, three, two, one_first, three_first, two_first]
        received += [one_second, three_second, two_second]
        mine = call(
            down_first_kernel,
            lowrank,
            [SMEM] + [VMEM] * 13 + [ANY],
            16,
            [pltpu.VMEM((columns, half_width), latent.dtype)],
        )(info, ids, latent, down, down_beside, *received, token)
        mine = call(
            down_last_kernel,
            lowrank,
            [SMEM] + [VMEM] * 6,
            16,
            [pltpu.VMEM((4 * rank, half_width), latent.dtype)],
        )(info, ids, latent, mine, *corners)
        up_pieces = [up, up_beside, *received, *corners]
    else:
        other = swap(latent, "tensor")
        parts, token = [], ids
        for begin, end in zip(cuts[:-1], cuts[1:]):
            part, token = base(info, latent, other, shared_weight, [token], begin, end)
            parts.append(part)
        mine = call(down_whole_kernel, lowrank, [SMEM] + [VMEM] * 3, 48)(
            info, ids, latent, lax.all_gather(down, "shard", axis=0, tiled=True)
        )
        up_pieces = [lax.all_gather(up, "shard", axis=0, tiled=True)]
    theirs = swap(mine, "tensor")

    return pl.pallas_call(
        lambda *refs: up_kernel(*refs, base_parts=len(parts)),
        out_shape=jax.ShapeDtypeStruct((rows, out_width), latent.dtype),
        in_specs=[SMEM] + [VMEM] * (3 + len(parts) + len(up_pieces)),
        out_specs=ANY,
        scratch_shapes=[
            pltpu.VMEM((columns, out_width), latent.dtype),
            pltpu.VMEM((rows, columns), latent.dtype),
            pltpu.SemaphoreType.DMA((tiles,)),
            pltpu.VMEM((tiles, rows, TILE), latent.dtype),
        ],
        compiler_params=pltpu.CompilerParams(vmem_limit_bytes=(24 if routed else 56) * MIB),
    )(info, ids, mine, theirs, *parts, *up_pieces)


def solution(mesh):
    return jax.shard_map(
        on_device,
        mesh=mesh,
        in_specs=(
            P(("replica", "shard"), "tensor"),
            P(("replica", "shard"), None),
            P(None, "tensor"),
            P("shard", "tensor", None),
            P("shard", None, "tensor"),
        ),
        out_specs=P(("replica", "shard"), "tensor"),
        check_vma=False,
    )
```

```python
import jax
import jax.numpy as jnp
import numpy as np
from jax import lax
from jax.experimental import pallas as pl
from jax.experimental.pallas import tpu as pltpu
from jax.sharding import PartitionSpec as P

MIB = 1024 * 1024
CHUNK = 512
TILE = 256
AXES = ("replica", "shard", "tensor")
FIRST_OWNER = 2
SMEM = pl.BlockSpec(memory_space=pltpu.SMEM)
VMEM = pl.BlockSpec(memory_space=pltpu.VMEM)
ANY = pl.BlockSpec(memory_space=pl.ANY)
TOKEN = jax.ShapeDtypeStruct((8, 128), jnp.float32)


def swap(value, axis):
    return lax.ppermute(value, axis, [(0, 1), (1, 0)])


def neighbour(value, shards):
    return lax.ppermute(value, "shard", [(i, i ^ 1) for i in range(shards)])


def ring_step(index, step):
    plane = index >> 1
    place = ((plane ^ (plane >> 1)) + step) & 3
    return ((place ^ (place >> 1)) << 1) | (index & 1)


def along_line(value, shards, step):
    return lax.ppermute(value, "shard", [(i, ring_step(i, step)) for i in range(shards)])


def in_plane(value, shards, first):
    pairs = []
    for r in range(2):
        for s in range(shards):
            for t in range(2):
                to_r, to_s = (r, s ^ 1) if (t == 0) == first else (r ^ 1, s)
                pairs.append(((r * shards + s) * 2 + t, (to_r * shards + to_s) * 2 + t))
    return lax.ppermute(value, AXES, pairs)


def call(kernel, out_shape, in_specs, limit, scratch=(), flops=0, moved=0):
    return pl.pallas_call(
        kernel,
        out_shape=out_shape,
        in_specs=in_specs,
        out_specs=jax.tree.map(lambda _: VMEM, out_shape),
        scratch_shapes=list(scratch),
        compiler_params=pltpu.CompilerParams(vmem_limit_bytes=limit * MIB),
        cost_estimate=pl.CostEstimate(flops=flops, bytes_accessed=moved, transcendentals=0),
    )


def owner_row(info, blocks, rank):
    place = lax.broadcasted_iota(jnp.int32, (1, len(blocks) * rank), 1) // rank
    row = jnp.full(place.shape, -1, jnp.int32)
    for number, block in enumerate(blocks):
        if block is not None:
            row = jnp.where(place == number, info[FIRST_OWNER + block], row)
    return row


def pack(pieces, *after):
    count = len(pieces)
    total = sum(rows for _, _, rows in pieces)
    width, dtype = pieces[0][0].shape[1], pieces[0][0].dtype

    def kernel(*refs):
        out, token = refs[-2:]
        top = 0
        for ref, (_, begin, rows) in zip(refs, pieces):
            out[top : top + rows, :] = ref[begin : begin + rows, :]
            top += rows
        token[...] = jnp.zeros_like(token)

    return call(
        kernel,
        [jax.ShapeDtypeStruct((total, width), dtype), TOKEN],
        [VMEM] * count + [ANY] * len(after),
        4,
    )(*[array for array, _, _ in pieces], *after)


def put(blocks, stack, top, rank):
    for number, block in enumerate(blocks):
        place = top + 2 * number * rank
        stack[place : place + rank, :] = block[...]


def fill_here(info, holds, received, stack, top, rank):
    here, first, second = received[0:3], received[3:6], received[6:9]
    pl.when(holds)(lambda: put(here, stack, top, rank))
    for core, refs in enumerate((second, first)):
        away = jnp.logical_not(holds) & (info[0] == core)
        pl.when(away)(lambda refs=refs: put(refs, stack, top, rank))


def fill_beside(info, holds, received, stack, top, rank, direct=True, corner=True):
    if direct:
        for core, refs in enumerate((received[3:6], received[6:9])):
            pl.when(holds & (info[0] == core))(lambda refs=refs: put(refs, stack, top, rank))
    if corner:
        corners = received[9:12]
        pl.when(jnp.logical_not(holds))(lambda: put(corners, stack, top, rank))


def clear(stack, top, rank, count):
    for number in range(count):
        place = top + 2 * number * rank
        stack[place : place + rank, :] = jnp.zeros((rank, stack.shape[1]), stack.dtype)


def prepare_kernel(weight, row_ids, *refs):
    spread, token = refs[-2:]
    wide = jnp.broadcast_to(row_ids[...].astype(jnp.float32), (128, row_ids.shape[1]))
    spread[...] = wide.T.astype(jnp.int32)
    token[...] = weight[0:8, 0:128].astype(jnp.float32)


def masked_products(info, ids, latent, stack, blocks, rank):
    total = None
    width = 2 * rank
    for skip in range(0, stack.shape[0], CHUNK):
        count = min(CHUNK, stack.shape[0] - skip)
        part = lax.dot_general(
            latent[...],
            stack[skip : skip + count, :],
            (((1,), (1,)), ((), ())),
            preferred_element_type=jnp.float32,
        )
        owners = owner_row(info, blocks[skip // rank : (skip + count) // rank], rank)
        for lane in range(0, count, width):
            lanes = slice(lane, lane + width)
            fold = jnp.where(ids[...] == owners[:, lanes], part[:, lanes], 0.0)
            total = fold if total is None else total + fold
    return total


def down_whole_kernel(info, ids, latent, stack, out):
    rank = out.shape[1] // 2
    blocks = range(stack.shape[0] // rank)
    out[...] = masked_products(info, ids, latent, stack, blocks, rank)


def down_first_kernel(info, ids, latent, own, beside, *refs):
    *received, _, out, stack = refs
    rank = own.shape[0]
    holds = info[1] == 1
    stack[0:rank, :] = own[...]
    stack[rank : 2 * rank, :] = beside[...]
    fill_here(info, holds, received, stack, 2 * rank, rank)
    fill_beside(info, holds, received, stack, 3 * rank, rank, corner=False)
    pl.when(jnp.logical_not(holds))(lambda: clear(stack, 3 * rank, rank, 3))
    out[...] = masked_products(info, ids, latent, stack, range(stack.shape[0] // rank), rank)


def down_last_kernel(info, ids, latent, earlier, *refs):
    *corners, out, stack = refs
    rank = out.shape[1] // 2
    holds = info[1] == 1

    @pl.when(holds)
    def _():
        out[...] = earlier[...]

    @pl.when(jnp.logical_not(holds))
    def _():
        for number, corner in enumerate(corners):
            stack[number * rank : (number + 1) * rank, :] = corner[...]
        stack[3 * rank : 4 * rank, :] = jnp.zeros((rank, stack.shape[1]), stack.dtype)
        pair = masked_products(info, ids, latent, stack, (3, 5, 7, None), rank)
        fold = pair[:, :rank] + pair[:, rank:]
        out[...] = earlier[...] + jnp.concatenate([jnp.zeros_like(fold), fold], axis=1)


def base_kernel(info, own, other, weight, *refs, skip):
    out, token = refs[-2:]
    token[...] = jnp.zeros_like(token)
    width = own.shape[1]
    mine = pl.ds(pl.multiple_of(info[0] * width, width), width)
    rest = pl.ds(pl.multiple_of((1 - info[0]) * width, width), width)
    step = min(CHUNK, out.shape[1])
    for begin in range(0, out.shape[1], step):
        place = slice(begin, min(begin + step, out.shape[1]))
        source = slice(skip + begin, skip + place.stop)
        out[:, place] = jnp.dot(
            own[...], weight[mine, source], preferred_element_type=jnp.float32
        ) + jnp.dot(other[...], weight[rest, source], preferred_element_type=jnp.float32)


def base(info, latent, other, weight, after, skip, end):
    rows, columns = latent.shape[0], end - skip
    return pl.pallas_call(
        lambda *refs: base_kernel(*refs, skip=skip),
        out_shape=[jax.ShapeDtypeStruct((rows, columns), jnp.float32), TOKEN],
        in_specs=[SMEM, VMEM, VMEM, VMEM] + [ANY] * len(after),
        out_specs=[VMEM, VMEM],
        compiler_params=pltpu.CompilerParams(vmem_limit_bytes=24 * MIB),
        cost_estimate=pl.CostEstimate(flops=1000, bytes_accessed=1000, transcendentals=0),
    )(info, latent, other, weight, *after)


def up_kernel(info, ids, mine, theirs, *refs, base_parts):
    *pieces, out, stack, wide, sems, staged = refs[base_parts:]
    bases = [
        part.at[:, pl.ds(begin, TILE)]
        for part in refs[:base_parts]
        for begin in range(0, part.shape[1], TILE)
    ]
    rank = mine.shape[1] // 2
    if len(pieces) == 1:
        stack[...] = pieces[0][...]
    else:
        own, beside, *received = pieces
        holds = info[1] == 0
        stack[0:rank, :] = own[...]
        stack[rank : 2 * rank, :] = beside[...]
        fill_here(info, holds, received, stack, 2 * rank, rank)
        fill_beside(info, holds, received, stack, 3 * rank, rank)
    lowrank = (mine[...] + theirs[...]).astype(jnp.bfloat16)
    zeros = jnp.zeros_like(lowrank)
    width = 2 * rank
    for lane in range(0, wide.shape[1], width):
        mask = ids[...] == owner_row(info, (lane // rank, lane // rank + 1), rank)
        wide[:, lane : lane + width] = jnp.where(mask, lowrank, zeros)
    copies = []
    tiles, _, tile = staged.shape
    for number in range(tiles):
        place = pl.ds(number * tile, tile)
        delta = jnp.dot(wide[...], stack[:, place], preferred_element_type=jnp.float32)
        total = bases[number][...] + delta.astype(jnp.bfloat16).astype(jnp.float32)
        staged[number] = total.astype(out.dtype)
        copies.append(
            pltpu.make_async_copy(staged.at[number], out.at[:, place], sems.at[number])
        )
        copies[-1].start()
    for copy in copies:
        copy.wait()


def on_device(latent, row_adapter_index, shared_weight, adapter_down_weight, adapter_up_weight):
    rows, half_width = latent.shape
    out_width = shared_weight.shape[1]
    local_adapters, _, rank = adapter_down_weight.shape
    shards = lax.axis_size("shard")
    adapters = shards * local_adapters
    columns = adapters * rank
    index, core = lax.axis_index("shard"), lax.axis_index("tensor")
    holds_down = core == lax.axis_index("replica")
    tiles = out_width // TILE
    cuts = [0, out_width // 6, out_width // 2, out_width]
    down = jnp.swapaxes(adapter_down_weight, 1, 2).reshape(local_adapters * rank, half_width)
    up = adapter_up_weight.reshape(local_adapters * rank, out_width)
    row_ids = row_adapter_index.reshape(1, rows)
    routed = shards == 8 and local_adapters == 1 and lax.axis_size("replica") == 2
    routed = routed and half_width == out_width and tiles % 6 == 0
    lowrank = jax.ShapeDtypeStruct((rows, 2 * rank), jnp.float32)
    if routed:
        sources = [ring_step(index, -step) for step in (0, 1, 3, 2)]
        owners = [a for source in sources for a in (source, source ^ 1)]
    else:
        owners = list(range(adapters))
    info = jnp.stack([jnp.asarray(v, jnp.int32) for v in (core, holds_down, *owners)])
    ids, token = call(
        prepare_kernel,
        [jax.ShapeDtypeStruct((rows, 2 * rank), jnp.int32), TOKEN],
        [VMEM, VMEM, ANY],
        16,
    )(shared_weight, row_ids, info)
    if routed:
        piece = jnp.where(holds_down, down, up)
        line = {step: along_line(piece, shards, step) for step in (1, 3)}
        other = swap(latent, "tensor")
        down_beside, up_beside = neighbour(down, shards), neighbour(up, shards)
        one, token = pack([(line[1], 0, rank)], token, down_beside)
        line[2] = along_line(one, shards, 1)
        one_first, one_second = in_plane(one, shards, True), in_plane(one, shards, False)
        part_one, token = base(info, latent, other, shared_weight, [token], cuts[0], cuts[1])
        three, token = pack([(line[3], 0, rank)], token, up_beside)
        three_first, three_second = in_plane(three, shards, True), in_plane(three, shards, False)
        two, token = pack([(line[2], 0, rank)], token)
        two_second = in_plane(two, shards, False)
        turn, token = pack([(one_first, 0, rank)], token, one_second)
        corner_one = in_plane(turn, shards, False)
        two_first = along_line(turn, shards, 1)
        part_two, token = base(info, latent, other, shared_weight, [token], cuts[1], cuts[2])
        turn, token = pack([(three_second, 0, rank)], token, three_first)
        corner_three = in_plane(turn, shards, True)
        turn, token = pack([(two_second, 0, rank)], token)
        corner_two = in_plane(turn, shards, True)
        part_three, token = base(info, latent, other, shared_weight, [token], cuts[2], cuts[3])
        parts = [part_one, part_two, part_three]
        corners = [corner_one, corner_three, corner_two]
        received = [one, three, two, one_first, three_first, two_first]
        received += [one_second, three_second, two_second]
        mine = call(
            down_first_kernel,
            lowrank,
            [SMEM] + [VMEM] * 13 + [ANY],
            16,
            [pltpu.VMEM((columns, half_width), latent.dtype)],
        )(info, ids, latent, down, down_beside, *received, token)
        mine = call(
            down_last_kernel,
            lowrank,
            [SMEM] + [VMEM] * 6,
            16,
            [pltpu.VMEM((4 * rank, half_width), latent.dtype)],
        )(info, ids, latent, mine, *corners)
        up_pieces = [up, up_beside, *received, *corners]
    else:
        other = swap(latent, "tensor")
        parts = []
        for begin, end in zip(cuts[:-1], cuts[1:]):
            part, token = base(info, latent, other, shared_weight, [token], begin, end)
            parts.append(part)
        mine = call(down_whole_kernel, lowrank, [SMEM] + [VMEM] * 3, 48)(
            info, ids, latent, lax.all_gather(down, "shard", axis=0, tiled=True)
        )
        up_pieces = [lax.all_gather(up, "shard", axis=0, tiled=True)]
    theirs = swap(mine, "tensor")

    return pl.pallas_call(
        lambda *refs: up_kernel(*refs, base_parts=len(parts)),
        out_shape=jax.ShapeDtypeStruct((rows, out_width), latent.dtype),
        in_specs=[SMEM] + [VMEM] * (3 + len(parts) + len(up_pieces)),
        out_specs=ANY,
        scratch_shapes=[
            pltpu.VMEM((columns, out_width), latent.dtype),
            pltpu.VMEM((rows, columns), latent.dtype),
            pltpu.SemaphoreType.DMA((tiles,)),
            pltpu.VMEM((tiles, rows, TILE), latent.dtype),
        ],
        compiler_params=pltpu.CompilerParams(vmem_limit_bytes=(24 if routed else 56) * MIB),
    )(info, ids, mine, theirs, *parts, *up_pieces)


def solution(mesh):
    return jax.shard_map(
        on_device,
        mesh=mesh,
        in_specs=(
            P(("replica", "shard"), "tensor"),
            P(("replica", "shard"), None),
            P(None, "tensor"),
            P("shard", "tensor", None),
            P("shard", None, "tensor"),
        ),
        out_specs=P(("replica", "shard"), "tensor"),
        check_vma=False,
    )
```

```python
import jax
import jax.numpy as jnp
import numpy as np
from jax import lax
from jax.experimental import pallas as pl
from jax.experimental.pallas import tpu as pltpu
from jax.sharding import PartitionSpec as P

MIB = 1024 * 1024
CHUNK = 512
TILE = 256
AXES = ("replica", "shard", "tensor")
FIRST_OWNER = 2
SMEM = pl.BlockSpec(memory_space=pltpu.SMEM)
VMEM = pl.BlockSpec(memory_space=pltpu.VMEM)
ANY = pl.BlockSpec(memory_space=pl.ANY)
TOKEN = jax.ShapeDtypeStruct((8, 128), jnp.float32)


def swap(value, axis):
    return lax.ppermute(value, axis, [(0, 1), (1, 0)])


def neighbour(value, shards):
    return lax.ppermute(value, "shard", [(i, i ^ 1) for i in range(shards)])


def ring_step(index, step):
    plane = index >> 1
    place = ((plane ^ (plane >> 1)) + step) & 3
    return ((place ^ (place >> 1)) << 1) | (index & 1)


def along_line(value, shards, step):
    return lax.ppermute(value, "shard", [(i, ring_step(i, step)) for i in range(shards)])


def in_plane(value, shards, first):
    pairs = []
    for r in range(2):
        for s in range(shards):
            for t in range(2):
                to_r, to_s = (r, s ^ 1) if (t == 0) == first else (r ^ 1, s)
                pairs.append(((r * shards + s) * 2 + t, (to_r * shards + to_s) * 2 + t))
    return lax.ppermute(value, AXES, pairs)


def call(kernel, out_shape, in_specs, limit, scratch=(), flops=0, moved=0):
    return pl.pallas_call(
        kernel,
        out_shape=out_shape,
        in_specs=in_specs,
        out_specs=jax.tree.map(lambda _: VMEM, out_shape),
        scratch_shapes=list(scratch),
        compiler_params=pltpu.CompilerParams(vmem_limit_bytes=limit * MIB),
        cost_estimate=pl.CostEstimate(flops=flops, bytes_accessed=moved, transcendentals=0),
    )


def owner_row(info, blocks, rank):
    place = lax.broadcasted_iota(jnp.int32, (1, len(blocks) * rank), 1) // rank
    row = jnp.full(place.shape, -1, jnp.int32)
    for number, block in enumerate(blocks):
        if block is not None:
            row = jnp.where(place == number, info[FIRST_OWNER + block], row)
    return row


def pack(pieces, *after):
    count = len(pieces)
    total = sum(rows for _, _, rows in pieces)
    width, dtype = pieces[0][0].shape[1], pieces[0][0].dtype

    def kernel(*refs):
        out, token = refs[-2:]
        top = 0
        for ref, (_, begin, rows) in zip(refs, pieces):
            out[top : top + rows, :] = ref[begin : begin + rows, :]
            top += rows
        token[...] = jnp.zeros_like(token)

    return call(
        kernel,
        [jax.ShapeDtypeStruct((total, width), dtype), TOKEN],
        [VMEM] * count + [ANY] * len(after),
        4,
    )(*[array for array, _, _ in pieces], *after)


def put(blocks, stack, top, rank):
    for number, block in enumerate(blocks):
        place = top + 2 * number * rank
        stack[place : place + rank, :] = block[...]


def fill_here(info, holds, received, stack, top, rank):
    here, first, second = received[0:3], received[3:6], received[6:9]
    pl.when(holds)(lambda: put(here, stack, top, rank))
    for core, refs in enumerate((second, first)):
        away = jnp.logical_not(holds) & (info[0] == core)
        pl.when(away)(lambda refs=refs: put(refs, stack, top, rank))


def fill_beside(info, holds, received, stack, top, rank, direct=True, corner=True):
    if direct:
        for core, refs in enumerate((received[3:6], received[6:9])):
            pl.when(holds & (info[0] == core))(lambda refs=refs: put(refs, stack, top, rank))
    if corner:
        corners = received[9:12]
        pl.when(jnp.logical_not(holds))(lambda: put(corners, stack, top, rank))


def clear(stack, top, rank, count):
    for number in range(count):
        place = top + 2 * number * rank
        stack[place : place + rank, :] = jnp.zeros((rank, stack.shape[1]), stack.dtype)


def prepare_kernel(weight, row_ids, *refs):
    spread, token = refs[-2:]
    wide = jnp.broadcast_to(row_ids[...].astype(jnp.float32), (128, row_ids.shape[1]))
    spread[...] = wide.T.astype(jnp.int32)
    token[...] = weight[0:8, 0:128].astype(jnp.float32)


def masked_products(info, ids, latent, stack, blocks, rank):
    total = None
    width = 2 * rank
    for skip in range(0, stack.shape[0], CHUNK):
        count = min(CHUNK, stack.shape[0] - skip)
        part = lax.dot_general(
            latent[...],
            stack[skip : skip + count, :],
            (((1,), (1,)), ((), ())),
            preferred_element_type=jnp.float32,
        )
        owners = owner_row(info, blocks[skip // rank : (skip + count) // rank], rank)
        for lane in range(0, count, width):
            lanes = slice(lane, lane + width)
            fold = jnp.where(ids[...] == owners[:, lanes], part[:, lanes], 0.0)
            total = fold if total is None else total + fold
    return total


def down_whole_kernel(info, ids, latent, stack, out):
    rank = out.shape[1] // 2
    blocks = range(stack.shape[0] // rank)
    out[...] = masked_products(info, ids, latent, stack, blocks, rank)


def down_first_kernel(info, ids, latent, own, beside, *refs):
    *received, _, out, stack = refs
    rank = own.shape[0]
    holds = info[1] == 1
    stack[0:rank, :] = own[...]
    stack[rank : 2 * rank, :] = beside[...]
    fill_here(info, holds, received, stack, 2 * rank, rank)
    fill_beside(info, holds, received, stack, 3 * rank, rank, corner=False)
    pl.when(jnp.logical_not(holds))(lambda: clear(stack, 3 * rank, rank, 3))
    out[...] = masked_products(info, ids, latent, stack, range(stack.shape[0] // rank), rank)


def down_last_kernel(info, ids, latent, earlier, *refs):
    *corners, out, stack = refs
    rank = out.shape[1] // 2
    holds = info[1] == 1

    @pl.when(holds)
    def _():
        out[...] = earlier[...]

    @pl.when(jnp.logical_not(holds))
    def _():
        for number, corner in enumerate(corners):
            stack[number * rank : (number + 1) * rank, :] = corner[...]
        stack[3 * rank : 4 * rank, :] = jnp.zeros((rank, stack.shape[1]), stack.dtype)
        pair = masked_products(info, ids, latent, stack, (3, 5, 7, None), rank)
        fold = pair[:, :rank] + pair[:, rank:]
        out[...] = earlier[...] + jnp.concatenate([jnp.zeros_like(fold), fold], axis=1)


def base_kernel(info, own, other, weight, *refs, skip):
    out, token = refs[-2:]
    token[...] = jnp.zeros_like(token)
    width = own.shape[1]
    mine = pl.ds(pl.multiple_of(info[0] * width, width), width)
    rest = pl.ds(pl.multiple_of((1 - info[0]) * width, width), width)
    step = min(CHUNK, out.shape[1])
    for begin in range(0, out.shape[1], step):
        place = slice(begin, min(begin + step, out.shape[1]))
        source = slice(skip + begin, skip + place.stop)
        out[:, place] = jnp.dot(
            own[...], weight[mine, source], preferred_element_type=jnp.float32
        ) + jnp.dot(other[...], weight[rest, source], preferred_element_type=jnp.float32)


def base(info, latent, other, weight, after, skip, end):
    rows, columns = latent.shape[0], end - skip
    return pl.pallas_call(
        lambda *refs: base_kernel(*refs, skip=skip),
        out_shape=[jax.ShapeDtypeStruct((rows, columns), jnp.float32), TOKEN],
        in_specs=[SMEM, VMEM, VMEM, VMEM] + [ANY] * len(after),
        out_specs=[VMEM, VMEM],
        compiler_params=pltpu.CompilerParams(vmem_limit_bytes=24 * MIB),
        cost_estimate=pl.CostEstimate(flops=1000, bytes_accessed=1000, transcendentals=0),
    )(info, latent, other, weight, *after)


def up_kernel(info, ids, mine, theirs, *refs, base_parts):
    *pieces, out, stack, wide, sems, staged = refs[base_parts:]
    bases = [
        part.at[:, pl.ds(begin, TILE)]
        for part in refs[:base_parts]
        for begin in range(0, part.shape[1], TILE)
    ]
    rank = mine.shape[1] // 2
    if len(pieces) == 1:
        stack[...] = pieces[0][...]
    else:
        own, beside, *received = pieces
        holds = info[1] == 0
        stack[0:rank, :] = own[...]
        stack[rank : 2 * rank, :] = beside[...]
        fill_here(info, holds, received, stack, 2 * rank, rank)
        fill_beside(info, holds, received, stack, 3 * rank, rank)
    lowrank = (mine[...] + theirs[...]).astype(jnp.bfloat16)
    zeros = jnp.zeros_like(lowrank)
    width = 2 * rank
    for lane in range(0, wide.shape[1], width):
        mask = ids[...] == owner_row(info, (lane // rank, lane // rank + 1), rank)
        wide[:, lane : lane + width] = jnp.where(mask, lowrank, zeros)
    copies = []
    tiles, _, tile = staged.shape
    for number in range(tiles):
        place = pl.ds(number * tile, tile)
        delta = jnp.dot(wide[...], stack[:, place], preferred_element_type=jnp.float32)
        total = bases[number][...] + delta.astype(jnp.bfloat16).astype(jnp.float32)
        staged[number] = total.astype(out.dtype)
        copies.append(
            pltpu.make_async_copy(staged.at[number], out.at[:, place], sems.at[number])
        )
        copies[-1].start()
    for copy in copies:
        copy.wait()


def on_device(latent, row_adapter_index, shared_weight, adapter_down_weight, adapter_up_weight):
    rows, half_width = latent.shape
    out_width = shared_weight.shape[1]
    local_adapters, _, rank = adapter_down_weight.shape
    shards = lax.axis_size("shard")
    adapters = shards * local_adapters
    columns = adapters * rank
    index, core = lax.axis_index("shard"), lax.axis_index("tensor")
    holds_down = core == lax.axis_index("replica")
    tiles = out_width // TILE
    cuts = [0, out_width // 6, out_width // 2, out_width]
    down = jnp.swapaxes(adapter_down_weight, 1, 2).reshape(local_adapters * rank, half_width)
    up = adapter_up_weight.reshape(local_adapters * rank, out_width)
    row_ids = row_adapter_index.reshape(1, rows)
    routed = shards == 8 and local_adapters == 1 and lax.axis_size("replica") == 2
    routed = routed and half_width == out_width and tiles % 6 == 0
    lowrank = jax.ShapeDtypeStruct((rows, 2 * rank), jnp.float32)
    if routed:
        sources = [ring_step(index, -step) for step in (0, 1, 3, 2)]
        owners = [a for source in sources for a in (source, source ^ 1)]
    else:
        owners = list(range(adapters))
    info = jnp.stack([jnp.asarray(v, jnp.int32) for v in (core, holds_down, *owners)])
    ids, token = call(
        prepare_kernel,
        [jax.ShapeDtypeStruct((rows, 2 * rank), jnp.int32), TOKEN],
        [VMEM, VMEM, ANY],
        16,
    )(shared_weight, row_ids, info)
    if routed:
        piece = jnp.where(holds_down, down, up)
        line = {1: along_line(piece, shards, 1)}
        other = swap(latent, "tensor")
        down_beside, up_beside = neighbour(down, shards), neighbour(up, shards)
        ready = token
        one, token = pack([(line[1], 0, rank)], token, down_beside)
        back, _ = pack([(piece, 0, rank)], ready)
        line[3] = along_line(back, shards, 3)
        line[2] = along_line(one, shards, 1)
        one_first, one_second = in_plane(one, shards, True), in_plane(one, shards, False)
        part_one, token = base(info, latent, other, shared_weight, [token], cuts[0], cuts[1])
        three, token = pack([(line[3], 0, rank)], token, up_beside)
        three_first, three_second = in_plane(three, shards, True), in_plane(three, shards, False)
        two, token = pack([(line[2], 0, rank)], token)
        two_second = in_plane(two, shards, False)
        turn, token = pack([(one_first, 0, rank)], token, one_second)
        corner_one = in_plane(turn, shards, False)
        two_first = along_line(turn, shards, 1)
        part_two, token = base(info, latent, other, shared_weight, [token], cuts[1], cuts[2])
        turn, token = pack([(three_second, 0, rank)], token, three_first)
        corner_three = in_plane(turn, shards, True)
        turn, token = pack([(two_second, 0, rank)], token)
        corner_two = in_plane(turn, shards, True)
        part_three, token = base(info, latent, other, shared_weight, [token], cuts[2], cuts[3])
        parts = [part_one, part_two, part_three]
        corners = [corner_one, corner_three, corner_two]
        received = [one, three, two, one_first, three_first, two_first]
        received += [one_second, three_second, two_second]
        mine = call(
            down_first_kernel,
            lowrank,
            [SMEM] + [VMEM] * 13 + [ANY],
            16,
            [pltpu.VMEM((columns, half_width), latent.dtype)],
        )(info, ids, latent, down, down_beside, *received, token)
        mine = call(
            down_last_kernel,
            lowrank,
            [SMEM] + [VMEM] * 6,
            16,
            [pltpu.VMEM((4 * rank, half_width), latent.dtype)],
        )(info, ids, latent, mine, *corners)
        up_pieces = [up, up_beside, *received, *corners]
    else:
        other = swap(latent, "tensor")
        parts = []
        for begin, end in zip(cuts[:-1], cuts[1:]):
            part, token = base(info, latent, other, shared_weight, [token], begin, end)
            parts.append(part)
        mine = call(down_whole_kernel, lowrank, [SMEM] + [VMEM] * 3, 48)(
            info, ids, latent, lax.all_gather(down, "shard", axis=0, tiled=True)
        )
        up_pieces = [lax.all_gather(up, "shard", axis=0, tiled=True)]
    theirs = swap(mine, "tensor")

    return pl.pallas_call(
        lambda *refs: up_kernel(*refs, base_parts=len(parts)),
        out_shape=jax.ShapeDtypeStruct((rows, out_width), latent.dtype),
        in_specs=[SMEM] + [VMEM] * (3 + len(parts) + len(up_pieces)),
        out_specs=ANY,
        scratch_shapes=[
            pltpu.VMEM((columns, out_width), latent.dtype),
            pltpu.VMEM((rows, columns), latent.dtype),
            pltpu.SemaphoreType.DMA((tiles,)),
            pltpu.VMEM((tiles, rows, TILE), latent.dtype),
        ],
        compiler_params=pltpu.CompilerParams(vmem_limit_bytes=(24 if routed else 56) * MIB),
    )(info, ids, mine, theirs, *parts, *up_pieces)


def solution(mesh):
    return jax.shard_map(
        on_device,
        mesh=mesh,
        in_specs=(
            P(("replica", "shard"), "tensor"),
            P(("replica", "shard"), None),
            P(None, "tensor"),
            P("shard", "tensor", None),
            P("shard", None, "tensor"),
        ),
        out_specs=P(("replica", "shard"), "tensor"),
        check_vma=False,
    )
```

```python
import jax
import jax.numpy as jnp
import numpy as np
from jax import lax
from jax.experimental import pallas as pl
from jax.experimental.pallas import tpu as pltpu
from jax.sharding import PartitionSpec as P

MIB = 1024 * 1024
CHUNK = 512
TILE = 256
AXES = ("replica", "shard", "tensor")
FIRST_OWNER = 2
COPY = 4 * MIB
SMEM = pl.BlockSpec(memory_space=pltpu.SMEM)
VMEM = pl.BlockSpec(memory_space=pltpu.VMEM)
ANY = pl.BlockSpec(memory_space=pl.ANY)
TOKEN = jax.ShapeDtypeStruct((8, 128), jnp.float32)


def swap(value, axis):
    return lax.ppermute(value, axis, [(0, 1), (1, 0)])


def neighbour(value, shards):
    return lax.ppermute(value, "shard", [(i, i ^ 1) for i in range(shards)])


def ring_step(index, step):
    plane = index >> 1
    place = ((plane ^ (plane >> 1)) + step) & 3
    return ((place ^ (place >> 1)) << 1) | (index & 1)


def along_line(value, shards, step):
    return lax.ppermute(value, "shard", [(i, ring_step(i, step)) for i in range(shards)])


def in_plane(value, shards, first):
    pairs = []
    for r in range(2):
        for s in range(shards):
            for t in range(2):
                to_r, to_s = (r, s ^ 1) if (t == 0) == first else (r ^ 1, s)
                pairs.append(((r * shards + s) * 2 + t, (to_r * shards + to_s) * 2 + t))
    return lax.ppermute(value, AXES, pairs)


def call(kernel, out_shape, in_specs, limit, scratch=(), flops=0, moved=0):
    return pl.pallas_call(
        kernel,
        out_shape=out_shape,
        in_specs=in_specs,
        out_specs=jax.tree.map(lambda _: VMEM, out_shape),
        scratch_shapes=list(scratch),
        compiler_params=pltpu.CompilerParams(vmem_limit_bytes=limit * MIB),
        cost_estimate=pl.CostEstimate(flops=flops, bytes_accessed=moved, transcendentals=0),
    )


def owner_row(info, blocks, rank):
    place = lax.broadcasted_iota(jnp.int32, (1, len(blocks) * rank), 1) // rank
    row = jnp.full(place.shape, -1, jnp.int32)
    for number, block in enumerate(blocks):
        if block is not None:
            row = jnp.where(place == number, info[FIRST_OWNER + block], row)
    return row


def pack(pieces, *after):
    count = len(pieces)
    total = sum(rows for _, _, rows in pieces)
    width, dtype = pieces[0][0].shape[1], pieces[0][0].dtype

    def kernel(*refs):
        out, token = refs[-2:]
        top = 0
        for ref, (_, begin, rows) in zip(refs, pieces):
            out[top : top + rows, :] = ref[begin : begin + rows, :]
            top += rows
        token[...] = jnp.zeros_like(token)

    return call(
        kernel,
        [jax.ShapeDtypeStruct((total, width), dtype), TOKEN],
        [VMEM] * count + [ANY] * len(after),
        4,
        moved=COPY,
    )(*[array for array, _, _ in pieces], *after)


def put(blocks, stack, top, rank):
    for number, block in enumerate(blocks):
        place = top + 2 * number * rank
        stack[place : place + rank, :] = block[...]


def fill_here(info, holds, received, stack, top, rank):
    here, first, second = received[0:3], received[3:6], received[6:9]
    pl.when(holds)(lambda: put(here, stack, top, rank))
    for core, refs in enumerate((second, first)):
        away = jnp.logical_not(holds) & (info[0] == core)
        pl.when(away)(lambda refs=refs: put(refs, stack, top, rank))


def fill_beside(info, holds, received, stack, top, rank, direct=True, corner=True):
    if direct:
        for core, refs in enumerate((received[3:6], received[6:9])):
            pl.when(holds & (info[0] == core))(lambda refs=refs: put(refs, stack, top, rank))
    if corner:
        corners = received[9:12]
        pl.when(jnp.logical_not(holds))(lambda: put(corners, stack, top, rank))


def clear(stack, top, rank, count):
    for number in range(count):
        place = top + 2 * number * rank
        stack[place : place + rank, :] = jnp.zeros((rank, stack.shape[1]), stack.dtype)


def prepare_kernel(weight, *refs):
    refs[-1][...] = weight[0:8, 0:128].astype(jnp.float32)


def spread_rows(row_ids):
    wide = jnp.broadcast_to(row_ids[...].astype(jnp.float32), (128, row_ids.shape[1]))
    return wide.T.astype(jnp.int32)


def masked_products(info, ids, latent, stack, blocks, rank):
    total = None
    width = 2 * rank
    for skip in range(0, stack.shape[0], CHUNK):
        count = min(CHUNK, stack.shape[0] - skip)
        part = lax.dot_general(
            latent[...],
            stack[skip : skip + count, :],
            (((1,), (1,)), ((), ())),
            preferred_element_type=jnp.float32,
        )
        owners = owner_row(info, blocks[skip // rank : (skip + count) // rank], rank)
        for lane in range(0, count, width):
            lanes = slice(lane, lane + width)
            fold = jnp.where(ids[...] == owners[:, lanes], part[:, lanes], 0.0)
            total = fold if total is None else total + fold
    return total


def down_whole_kernel(info, row_ids, latent, stack, out, ids):
    ids[...] = spread_rows(row_ids)
    rank = out.shape[1] // 2
    blocks = range(stack.shape[0] // rank)
    out[...] = masked_products(info, ids, latent, stack, blocks, rank)


def down_first_kernel(info, row_ids, latent, own, beside, *refs):
    *received, _, out, ids, stack = refs
    ids[...] = spread_rows(row_ids)
    rank = own.shape[0]
    holds = info[1] == 1
    stack[0:rank, :] = own[...]
    stack[rank : 2 * rank, :] = beside[...]
    fill_here(info, holds, received, stack, 2 * rank, rank)
    fill_beside(info, holds, received, stack, 3 * rank, rank, corner=False)
    pl.when(jnp.logical_not(holds))(lambda: clear(stack, 3 * rank, rank, 3))
    out[...] = masked_products(info, ids, latent, stack, range(stack.shape[0] // rank), rank)


def down_last_kernel(info, ids, latent, earlier, *refs):
    *corners, out, stack = refs
    rank = out.shape[1] // 2
    holds = info[1] == 1

    @pl.when(holds)
    def _():
        out[...] = earlier[...]

    @pl.when(jnp.logical_not(holds))
    def _():
        for number, corner in enumerate(corners):
            stack[number * rank : (number + 1) * rank, :] = corner[...]
        stack[3 * rank : 4 * rank, :] = jnp.zeros((rank, stack.shape[1]), stack.dtype)
        pair = masked_products(info, ids, latent, stack, (3, 5, 7, None), rank)
        fold = pair[:, :rank] + pair[:, rank:]
        out[...] = earlier[...] + jnp.concatenate([jnp.zeros_like(fold), fold], axis=1)


def base_kernel(info, own, other, weight, *refs, skip):
    out, token = refs[-2:]
    token[...] = jnp.zeros_like(token)
    width = own.shape[1]
    mine = pl.ds(pl.multiple_of(info[0] * width, width), width)
    rest = pl.ds(pl.multiple_of((1 - info[0]) * width, width), width)
    step = min(CHUNK, out.shape[1])
    for begin in range(0, out.shape[1], step):
        place = slice(begin, min(begin + step, out.shape[1]))
        source = slice(skip + begin, skip + place.stop)
        out[:, place] = jnp.dot(
            own[...], weight[mine, source], preferred_element_type=jnp.float32
        ) + jnp.dot(other[...], weight[rest, source], preferred_element_type=jnp.float32)


def base(info, latent, other, weight, after, skip, end):
    rows, columns = latent.shape[0], end - skip
    return pl.pallas_call(
        lambda *refs: base_kernel(*refs, skip=skip),
        out_shape=[jax.ShapeDtypeStruct((rows, columns), jnp.float32), TOKEN],
        in_specs=[SMEM, VMEM, VMEM, VMEM] + [ANY] * len(after),
        out_specs=[VMEM, VMEM],
        compiler_params=pltpu.CompilerParams(vmem_limit_bytes=24 * MIB),
        cost_estimate=pl.CostEstimate(
            flops=4 * rows * latent.shape[1] * columns,
            bytes_accessed=4 * rows * columns,
            transcendentals=0,
        ),
    )(info, latent, other, weight, *after)


def up_kernel(info, ids, mine, theirs, *refs, base_parts):
    *pieces, out, stack, wide, sems, staged = refs[base_parts:]
    bases = [
        part.at[:, pl.ds(begin, TILE)]
        for part in refs[:base_parts]
        for begin in range(0, part.shape[1], TILE)
    ]
    rank = mine.shape[1] // 2
    if len(pieces) == 1:
        stack[...] = pieces[0][...]
    else:
        own, beside, *received = pieces
        holds = info[1] == 0
        stack[0:rank, :] = own[...]
        stack[rank : 2 * rank, :] = beside[...]
        fill_here(info, holds, received, stack, 2 * rank, rank)
        fill_beside(info, holds, received, stack, 3 * rank, rank)
    lowrank = (mine[...] + theirs[...]).astype(jnp.bfloat16)
    zeros = jnp.zeros_like(lowrank)
    width = 2 * rank
    for lane in range(0, wide.shape[1], width):
        mask = ids[...] == owner_row(info, (lane // rank, lane // rank + 1), rank)
        wide[:, lane : lane + width] = jnp.where(mask, lowrank, zeros)
    copies = []
    tiles, _, tile = staged.shape
    for number in range(tiles):
        place = pl.ds(number * tile, tile)
        delta = jnp.dot(wide[...], stack[:, place], preferred_element_type=jnp.float32)
        total = bases[number][...] + delta.astype(jnp.bfloat16).astype(jnp.float32)
        staged[number] = total.astype(out.dtype)
        copies.append(
            pltpu.make_async_copy(staged.at[number], out.at[:, place], sems.at[number])
        )
        copies[-1].start()
    for copy in copies:
        copy.wait()


def on_device(latent, row_adapter_index, shared_weight, adapter_down_weight, adapter_up_weight):
    rows, half_width = latent.shape
    out_width = shared_weight.shape[1]
    local_adapters, _, rank = adapter_down_weight.shape
    shards = lax.axis_size("shard")
    adapters = shards * local_adapters
    columns = adapters * rank
    index, core = lax.axis_index("shard"), lax.axis_index("tensor")
    holds_down = core == lax.axis_index("replica")
    tiles = out_width // TILE
    cuts = [0, out_width // 6, out_width]
    down = jnp.swapaxes(adapter_down_weight, 1, 2).reshape(local_adapters * rank, half_width)
    up = adapter_up_weight.reshape(local_adapters * rank, out_width)
    row_ids = row_adapter_index.reshape(1, rows)
    routed = shards == 8 and local_adapters == 1 and lax.axis_size("replica") == 2
    routed = routed and half_width == out_width and tiles % 6 == 0
    lowrank = jax.ShapeDtypeStruct((rows, 2 * rank), jnp.float32)
    if routed:
        sources = [ring_step(index, -step) for step in (0, 1, 3, 2)]
        owners = [a for source in sources for a in (source, source ^ 1)]
    else:
        owners = list(range(adapters))
    info = jnp.stack([jnp.asarray(v, jnp.int32) for v in (core, holds_down, *owners)])
    (token,) = call(prepare_kernel, [TOKEN], [VMEM, ANY], 16, moved=COPY)(shared_weight, info)
    down_out = [lowrank, jax.ShapeDtypeStruct((rows, 2 * rank), jnp.int32)]
    if routed:
        piece = jnp.where(holds_down, down, up)
        line = {1: along_line(piece, shards, 1)}
        other = swap(latent, "tensor")
        down_beside, up_beside = neighbour(down, shards), neighbour(up, shards)
        ready = token
        one, token = pack([(line[1], 0, rank)], token, down_beside)
        back, _ = pack([(piece, 0, rank)], ready)
        line[3] = along_line(back, shards, 3)
        line[2] = along_line(one, shards, 1)
        one_first, one_second = in_plane(one, shards, True), in_plane(one, shards, False)
        part_one, token = base(info, latent, other, shared_weight, [token], cuts[0], cuts[1])
        three, token = pack([(line[3], 0, rank)], token, up_beside)
        three_first, three_second = in_plane(three, shards, True), in_plane(three, shards, False)
        two, token = pack([(line[2], 0, rank)], token)
        two_second = in_plane(two, shards, False)
        turn, token = pack([(one_first, 0, rank)], token, one_second)
        corner_one = in_plane(turn, shards, False)
        two_first = along_line(turn, shards, 1)
        turn, token = pack([(three_second, 0, rank)], token, three_first)
        corner_three = in_plane(turn, shards, True)
        turn, token = pack([(two_second, 0, rank)], token)
        corner_two = in_plane(turn, shards, True)
        part_two, token = base(info, latent, other, shared_weight, [token], cuts[1], cuts[2])
        parts = [part_one, part_two]
        corners = [corner_one, corner_three, corner_two]
        received = [one, three, two, one_first, three_first, two_first]
        received += [one_second, three_second, two_second]
        mine, ids = call(
            down_first_kernel,
            down_out,
            [SMEM] + [VMEM] * 13 + [ANY],
            16,
            [pltpu.VMEM((columns, half_width), latent.dtype)],
        )(info, row_ids, latent, down, down_beside, *received, token)
        mine = call(
            down_last_kernel,
            lowrank,
            [SMEM] + [VMEM] * 6,
            16,
            [pltpu.VMEM((4 * rank, half_width), latent.dtype)],
        )(info, ids, latent, mine, *corners)
        up_pieces = [up, up_beside, *received, *corners]
    else:
        other = swap(latent, "tensor")
        parts = []
        for begin, end in zip(cuts[:-1], cuts[1:]):
            part, token = base(info, latent, other, shared_weight, [token], begin, end)
            parts.append(part)
        mine, ids = call(down_whole_kernel, down_out, [SMEM] + [VMEM] * 3, 48)(
            info, row_ids, latent, lax.all_gather(down, "shard", axis=0, tiled=True)
        )
        up_pieces = [lax.all_gather(up, "shard", axis=0, tiled=True)]
    theirs = swap(mine, "tensor")

    return pl.pallas_call(
        lambda *refs: up_kernel(*refs, base_parts=len(parts)),
        out_shape=jax.ShapeDtypeStruct((rows, out_width), latent.dtype),
        in_specs=[SMEM] + [VMEM] * (3 + len(parts) + len(up_pieces)),
        out_specs=ANY,
        scratch_shapes=[
            pltpu.VMEM((columns, out_width), latent.dtype),
            pltpu.VMEM((rows, columns), latent.dtype),
            pltpu.SemaphoreType.DMA((tiles,)),
            pltpu.VMEM((tiles, rows, TILE), latent.dtype),
        ],
        compiler_params=pltpu.CompilerParams(vmem_limit_bytes=(24 if routed else 56) * MIB),
    )(info, ids, mine, theirs, *parts, *up_pieces)


def solution(mesh):
    return jax.shard_map(
        on_device,
        mesh=mesh,
        in_specs=(
            P(("replica", "shard"), "tensor"),
            P(("replica", "shard"), None),
            P(None, "tensor"),
            P("shard", "tensor", None),
            P("shard", None, "tensor"),
        ),
        out_specs=P(("replica", "shard"), "tensor"),
        check_vma=False,
    )
```

```python
import jax
import jax.numpy as jnp
import numpy as np
from jax import lax
from jax.experimental import pallas as pl
from jax.experimental.pallas import tpu as pltpu
from jax.sharding import PartitionSpec as P

MIB = 1024 * 1024
CHUNK = 512
TILE = 256
AXES = ("replica", "shard", "tensor")
FIRST_OWNER = 2
COPY = 0
SMEM = pl.BlockSpec(memory_space=pltpu.SMEM)
VMEM = pl.BlockSpec(memory_space=pltpu.VMEM)
ANY = pl.BlockSpec(memory_space=pl.ANY)
TOKEN = jax.ShapeDtypeStruct((8, 128), jnp.float32)


def swap(value, axis):
    return lax.ppermute(value, axis, [(0, 1), (1, 0)])


def neighbour(value, shards):
    return lax.ppermute(value, "shard", [(i, i ^ 1) for i in range(shards)])


def ring_step(index, step):
    plane = index >> 1
    place = ((plane ^ (plane >> 1)) + step) & 3
    return ((place ^ (place >> 1)) << 1) | (index & 1)


def along_line(value, shards, step):
    return lax.ppermute(value, "shard", [(i, ring_step(i, step)) for i in range(shards)])


def in_plane(value, shards, first):
    pairs = []
    for r in range(2):
        for s in range(shards):
            for t in range(2):
                to_r, to_s = (r, s ^ 1) if (t == 0) == first else (r ^ 1, s)
                pairs.append(((r * shards + s) * 2 + t, (to_r * shards + to_s) * 2 + t))
    return lax.ppermute(value, AXES, pairs)


def call(kernel, out_shape, in_specs, limit, scratch=(), flops=0, moved=0):
    return pl.pallas_call(
        kernel,
        out_shape=out_shape,
        in_specs=in_specs,
        out_specs=jax.tree.map(lambda _: VMEM, out_shape),
        scratch_shapes=list(scratch),
        compiler_params=pltpu.CompilerParams(vmem_limit_bytes=limit * MIB),
        cost_estimate=pl.CostEstimate(flops=flops, bytes_accessed=moved, transcendentals=0),
    )


def owner_row(info, blocks, rank):
    place = lax.broadcasted_iota(jnp.int32, (1, len(blocks) * rank), 1) // rank
    row = jnp.full(place.shape, -1, jnp.int32)
    for number, block in enumerate(blocks):
        if block is not None:
            row = jnp.where(place == number, info[FIRST_OWNER + block], row)
    return row


def pack(pieces, *after):
    count = len(pieces)
    total = sum(rows for _, _, rows in pieces)
    width, dtype = pieces[0][0].shape[1], pieces[0][0].dtype

    def kernel(*refs):
        out, token = refs[-2:]
        top = 0
        for ref, (_, begin, rows) in zip(refs, pieces):
            out[top : top + rows, :] = ref[begin : begin + rows, :]
            top += rows
        token[...] = jnp.zeros_like(token)

    return call(
        kernel,
        [jax.ShapeDtypeStruct((total, width), dtype), TOKEN],
        [VMEM] * count + [ANY] * len(after),
        4,
        moved=COPY,
    )(*[array for array, _, _ in pieces], *after)


def put(blocks, stack, top, rank):
    for number, block in enumerate(blocks):
        place = top + 2 * number * rank
        stack[place : place + rank, :] = block[...]


def fill_here(info, holds, received, stack, top, rank):
    here, first, second = received[0:3], received[3:6], received[6:9]
    pl.when(holds)(lambda: put(here, stack, top, rank))
    for core, refs in enumerate((second, first)):
        away = jnp.logical_not(holds) & (info[0] == core)
        pl.when(away)(lambda refs=refs: put(refs, stack, top, rank))


def fill_beside(info, holds, received, stack, top, rank, direct=True, corner=True):
    if direct:
        for core, refs in enumerate((received[3:6], received[6:9])):
            pl.when(holds & (info[0] == core))(lambda refs=refs: put(refs, stack, top, rank))
    if corner:
        corners = received[9:12]
        pl.when(jnp.logical_not(holds))(lambda: put(corners, stack, top, rank))


def clear(stack, top, rank, count):
    for number in range(count):
        place = top + 2 * number * rank
        stack[place : place + rank, :] = jnp.zeros((rank, stack.shape[1]), stack.dtype)


def prepare_kernel(weight, *refs):
    refs[-1][...] = weight[0:8, 0:128].astype(jnp.float32)


def spread_rows(row_ids):
    wide = jnp.broadcast_to(row_ids[...].astype(jnp.float32), (128, row_ids.shape[1]))
    return wide.T.astype(jnp.int32)


def masked_products(info, ids, latent, stack, blocks, rank):
    total = None
    width = 2 * rank
    for skip in range(0, stack.shape[0], CHUNK):
        count = min(CHUNK, stack.shape[0] - skip)
        part = lax.dot_general(
            latent[...],
            stack[skip : skip + count, :],
            (((1,), (1,)), ((), ())),
            preferred_element_type=jnp.float32,
        )
        owners = owner_row(info, blocks[skip // rank : (skip + count) // rank], rank)
        for lane in range(0, count, width):
            lanes = slice(lane, lane + width)
            fold = jnp.where(ids[...] == owners[:, lanes], part[:, lanes], 0.0)
            total = fold if total is None else total + fold
    return total


def down_whole_kernel(info, row_ids, latent, stack, out, ids):
    ids[...] = spread_rows(row_ids)
    rank = out.shape[1] // 2
    blocks = range(stack.shape[0] // rank)
    out[...] = masked_products(info, ids, latent, stack, blocks, rank)


def down_first_kernel(info, row_ids, latent, own, beside, *refs):
    *received, _, out, ids, stack = refs
    ids[...] = spread_rows(row_ids)
    rank = own.shape[0]
    holds = info[1] == 1
    stack[0:rank, :] = own[...]
    stack[rank : 2 * rank, :] = beside[...]
    fill_here(info, holds, received, stack, 2 * rank, rank)
    fill_beside(info, holds, received, stack, 3 * rank, rank, corner=False)
    pl.when(jnp.logical_not(holds))(lambda: clear(stack, 3 * rank, rank, 3))
    out[...] = masked_products(info, ids, latent, stack, range(stack.shape[0] // rank), rank)


def down_last_kernel(info, ids, latent, earlier, *refs):
    *corners, out, stack = refs
    rank = out.shape[1] // 2
    holds = info[1] == 1

    @pl.when(holds)
    def _():
        out[...] = earlier[...]

    @pl.when(jnp.logical_not(holds))
    def _():
        for number, corner in enumerate(corners):
            stack[number * rank : (number + 1) * rank, :] = corner[...]
        stack[3 * rank : 4 * rank, :] = jnp.zeros((rank, stack.shape[1]), stack.dtype)
        pair = masked_products(info, ids, latent, stack, (3, 5, 7, None), rank)
        fold = pair[:, :rank] + pair[:, rank:]
        out[...] = earlier[...] + jnp.concatenate([jnp.zeros_like(fold), fold], axis=1)


def base_kernel(info, own, other, weight, *refs, skip):
    out, token = refs[-2:]
    token[...] = jnp.zeros_like(token)
    width = own.shape[1]
    mine = pl.ds(pl.multiple_of(info[0] * width, width), width)
    rest = pl.ds(pl.multiple_of((1 - info[0]) * width, width), width)
    step = min(CHUNK, out.shape[1])
    for begin in range(0, out.shape[1], step):
        place = slice(begin, min(begin + step, out.shape[1]))
        source = slice(skip + begin, skip + place.stop)
        out[:, place] = jnp.dot(
            own[...], weight[mine, source], preferred_element_type=jnp.float32
        ) + jnp.dot(other[...], weight[rest, source], preferred_element_type=jnp.float32)


def base(info, latent, other, weight, after, skip, end):
    rows, columns = latent.shape[0], end - skip
    return pl.pallas_call(
        lambda *refs: base_kernel(*refs, skip=skip),
        out_shape=[jax.ShapeDtypeStruct((rows, columns), jnp.float32), TOKEN],
        in_specs=[SMEM, VMEM, VMEM, VMEM] + [ANY] * len(after),
        out_specs=[VMEM, VMEM],
        compiler_params=pltpu.CompilerParams(vmem_limit_bytes=24 * MIB),
        cost_estimate=pl.CostEstimate(
            flops=1000,
            bytes_accessed=1000,
            transcendentals=0,
        ),
    )(info, latent, other, weight, *after)


def up_kernel(info, ids, mine, theirs, *refs, base_parts):
    *pieces, out, stack, wide, sems, staged = refs[base_parts:]
    bases = [
        part.at[:, pl.ds(begin, TILE)]
        for part in refs[:base_parts]
        for begin in range(0, part.shape[1], TILE)
    ]
    rank = mine.shape[1] // 2
    if len(pieces) == 1:
        stack[...] = pieces[0][...]
    else:
        own, beside, *received = pieces
        holds = info[1] == 0
        stack[0:rank, :] = own[...]
        stack[rank : 2 * rank, :] = beside[...]
        fill_here(info, holds, received, stack, 2 * rank, rank)
        fill_beside(info, holds, received, stack, 3 * rank, rank)
    lowrank = (mine[...] + theirs[...]).astype(jnp.bfloat16)
    zeros = jnp.zeros_like(lowrank)
    width = 2 * rank
    for lane in range(0, wide.shape[1], width):
        mask = ids[...] == owner_row(info, (lane // rank, lane // rank + 1), rank)
        wide[:, lane : lane + width] = jnp.where(mask, lowrank, zeros)
    copies = []
    tiles, _, tile = staged.shape
    for number in range(tiles):
        place = pl.ds(number * tile, tile)
        delta = jnp.dot(wide[...], stack[:, place], preferred_element_type=jnp.float32)
        total = bases[number][...] + delta.astype(jnp.bfloat16).astype(jnp.float32)
        staged[number] = total.astype(out.dtype)
        copies.append(
            pltpu.make_async_copy(staged.at[number], out.at[:, place], sems.at[number])
        )
        copies[-1].start()
    for copy in copies:
        copy.wait()


def on_device(latent, row_adapter_index, shared_weight, adapter_down_weight, adapter_up_weight):
    rows, half_width = latent.shape
    out_width = shared_weight.shape[1]
    local_adapters, _, rank = adapter_down_weight.shape
    shards = lax.axis_size("shard")
    adapters = shards * local_adapters
    columns = adapters * rank
    index, core = lax.axis_index("shard"), lax.axis_index("tensor")
    holds_down = core == lax.axis_index("replica")
    tiles = out_width // TILE
    cuts = [0, out_width // 3, out_width // 2, out_width]
    down = jnp.swapaxes(adapter_down_weight, 1, 2).reshape(local_adapters * rank, half_width)
    up = adapter_up_weight.reshape(local_adapters * rank, out_width)
    row_ids = row_adapter_index.reshape(1, rows)
    routed = shards == 8 and local_adapters == 1 and lax.axis_size("replica") == 2
    routed = routed and half_width == out_width and tiles % 6 == 0
    lowrank = jax.ShapeDtypeStruct((rows, 2 * rank), jnp.float32)
    if routed:
        sources = [ring_step(index, -step) for step in (0, 1, 3, 2)]
        owners = [a for source in sources for a in (source, source ^ 1)]
    else:
        owners = list(range(adapters))
    info = jnp.stack([jnp.asarray(v, jnp.int32) for v in (core, holds_down, *owners)])
    (token,) = call(prepare_kernel, [TOKEN], [VMEM, ANY], 16, moved=COPY)(shared_weight, info)
    down_out = [lowrank, jax.ShapeDtypeStruct((rows, 2 * rank), jnp.int32)]
    if routed:
        piece = jnp.where(holds_down, down, up)
        line = {1: along_line(piece, shards, 1)}
        other = swap(latent, "tensor")
        down_beside, up_beside = neighbour(down, shards), neighbour(up, shards)
        ready = token
        one, token = pack([(line[1], 0, rank)], token, down_beside, other)
        back, _ = pack([(piece, 0, rank)], ready)
        line[3] = along_line(back, shards, 3)
        line[2] = along_line(one, shards, 1)
        one_first, one_second = in_plane(one, shards, True), in_plane(one, shards, False)
        three, token = pack([(line[3], 0, rank)], token, up_beside)
        three_first, three_second = in_plane(three, shards, True), in_plane(three, shards, False)
        part_one, token = base(info, latent, other, shared_weight, [token], cuts[0], cuts[1])
        two, token = pack([(line[2], 0, rank)], token)
        two_second = in_plane(two, shards, False)
        turn, token = pack([(one_first, 0, rank)], token, one_second)
        corner_one = in_plane(turn, shards, False)
        two_first = along_line(turn, shards, 1)
        part_two, token = base(info, latent, other, shared_weight, [token], cuts[1], cuts[2])
        turn, token = pack([(three_second, 0, rank)], token, three_first)
        corner_three = in_plane(turn, shards, True)
        turn, token = pack([(two_second, 0, rank)], token)
        corner_two = in_plane(turn, shards, True)
        part_three, token = base(info, latent, other, shared_weight, [token], cuts[2], cuts[3])
        parts = [part_one, part_two, part_three]
        corners = [corner_one, corner_three, corner_two]
        received = [one, three, two, one_first, three_first, two_first]
        received += [one_second, three_second, two_second]
        mine, ids = call(
            down_first_kernel,
            down_out,
            [SMEM] + [VMEM] * 13 + [ANY],
            16,
            [pltpu.VMEM((columns, half_width), latent.dtype)],
        )(info, row_ids, latent, down, down_beside, *received, token)
        mine = call(
            down_last_kernel,
            lowrank,
            [SMEM] + [VMEM] * 6,
            16,
            [pltpu.VMEM((4 * rank, half_width), latent.dtype)],
        )(info, ids, latent, mine, *corners)
        up_pieces = [up, up_beside, *received, *corners]
    else:
        other = swap(latent, "tensor")
        parts = []
        for begin, end in zip(cuts[:-1], cuts[1:]):
            part, token = base(info, latent, other, shared_weight, [token], begin, end)
            parts.append(part)
        mine, ids = call(down_whole_kernel, down_out, [SMEM] + [VMEM] * 3, 48)(
            info, row_ids, latent, lax.all_gather(down, "shard", axis=0, tiled=True)
        )
        up_pieces = [lax.all_gather(up, "shard", axis=0, tiled=True)]
    theirs = swap(mine, "tensor")

    return pl.pallas_call(
        lambda *refs: up_kernel(*refs, base_parts=len(parts)),
        out_shape=jax.ShapeDtypeStruct((rows, out_width), latent.dtype),
        in_specs=[SMEM] + [VMEM] * (3 + len(parts) + len(up_pieces)),
        out_specs=ANY,
        scratch_shapes=[
            pltpu.VMEM((columns, out_width), latent.dtype),
            pltpu.VMEM((rows, columns), latent.dtype),
            pltpu.SemaphoreType.DMA((tiles,)),
            pltpu.VMEM((tiles, rows, TILE), latent.dtype),
        ],
        compiler_params=pltpu.CompilerParams(vmem_limit_bytes=(24 if routed else 56) * MIB),
    )(info, ids, mine, theirs, *parts, *up_pieces)


def solution(mesh):
    return jax.shard_map(
        on_device,
        mesh=mesh,
        in_specs=(
            P(("replica", "shard"), "tensor"),
            P(("replica", "shard"), None),
            P(None, "tensor"),
            P("shard", "tensor", None),
            P("shard", None, "tensor"),
        ),
        out_specs=P(("replica", "shard"), "tensor"),
        check_vma=False,
    )
```

```python
import jax
import jax.numpy as jnp
import numpy as np
from jax import lax
from jax.experimental import pallas as pl
from jax.experimental.pallas import tpu as pltpu
from jax.sharding import PartitionSpec as P

MIB = 1024 * 1024
CHUNK = 512
TILE = 256
AXES = ("replica", "shard", "tensor")
FIRST_OWNER = 2
COPY = 0
SMEM = pl.BlockSpec(memory_space=pltpu.SMEM)
VMEM = pl.BlockSpec(memory_space=pltpu.VMEM)
ANY = pl.BlockSpec(memory_space=pl.ANY)
TOKEN = jax.ShapeDtypeStruct((8, 128), jnp.float32)


def swap(value, axis):
    return lax.ppermute(value, axis, [(0, 1), (1, 0)])


def neighbour(value, shards):
    return lax.ppermute(value, "shard", [(i, i ^ 1) for i in range(shards)])


def ring_step(index, step):
    plane = index >> 1
    place = ((plane ^ (plane >> 1)) + step) & 3
    return ((place ^ (place >> 1)) << 1) | (index & 1)


def along_line(value, shards, step):
    return lax.ppermute(value, "shard", [(i, ring_step(i, step)) for i in range(shards)])


def in_plane(value, shards, first):
    pairs = []
    for r in range(2):
        for s in range(shards):
            for t in range(2):
                to_r, to_s = (r, s ^ 1) if (t == 0) == first else (r ^ 1, s)
                pairs.append(((r * shards + s) * 2 + t, (to_r * shards + to_s) * 2 + t))
    return lax.ppermute(value, AXES, pairs)


def call(kernel, out_shape, in_specs, limit, scratch=(), flops=0, moved=0):
    return pl.pallas_call(
        kernel,
        out_shape=out_shape,
        in_specs=in_specs,
        out_specs=jax.tree.map(lambda _: VMEM, out_shape),
        scratch_shapes=list(scratch),
        compiler_params=pltpu.CompilerParams(vmem_limit_bytes=limit * MIB),
        cost_estimate=pl.CostEstimate(flops=flops, bytes_accessed=moved, transcendentals=0),
    )


def owner_row(info, blocks, rank):
    place = lax.broadcasted_iota(jnp.int32, (1, len(blocks) * rank), 1) // rank
    row = jnp.full(place.shape, -1, jnp.int32)
    for number, block in enumerate(blocks):
        if block is not None:
            row = jnp.where(place == number, info[FIRST_OWNER + block], row)
    return row


def pack(pieces, *after):
    count = len(pieces)
    total = sum(rows for _, _, rows in pieces)
    width, dtype = pieces[0][0].shape[1], pieces[0][0].dtype

    def kernel(*refs):
        out, token = refs[-2:]
        top = 0
        for ref, (_, begin, rows) in zip(refs, pieces):
            out[top : top + rows, :] = ref[begin : begin + rows, :]
            top += rows
        token[...] = jnp.zeros_like(token)

    return call(
        kernel,
        [jax.ShapeDtypeStruct((total, width), dtype), TOKEN],
        [VMEM] * count + [ANY] * len(after),
        4,
        moved=COPY,
    )(*[array for array, _, _ in pieces], *after)


def put(blocks, stack, top, rank):
    for number, block in enumerate(blocks):
        place = top + 2 * number * rank
        stack[place : place + rank, :] = block[...]


def fill_here(info, holds, received, stack, top, rank):
    here, first, second = received[0:3], received[3:6], received[6:9]
    pl.when(holds)(lambda: put(here, stack, top, rank))
    for core, refs in enumerate((second, first)):
        away = jnp.logical_not(holds) & (info[0] == core)
        pl.when(away)(lambda refs=refs: put(refs, stack, top, rank))


def fill_beside(info, holds, received, stack, top, rank, direct=True, corner=True):
    if direct:
        for core, refs in enumerate((received[3:6], received[6:9])):
            pl.when(holds & (info[0] == core))(lambda refs=refs: put(refs, stack, top, rank))
    if corner:
        corners = received[9:12]
        pl.when(jnp.logical_not(holds))(lambda: put(corners, stack, top, rank))


def clear(stack, top, rank, count):
    for number in range(count):
        place = top + 2 * number * rank
        stack[place : place + rank, :] = jnp.zeros((rank, stack.shape[1]), stack.dtype)


def prepare_kernel(weight, *refs):
    refs[-1][...] = weight[0:8, 0:128].astype(jnp.float32)


def spread_rows(row_ids):
    wide = jnp.broadcast_to(row_ids[...].astype(jnp.float32), (128, row_ids.shape[1]))
    return wide.T.astype(jnp.int32)


def masked_products(info, ids, latent, stack, blocks, rank):
    total = None
    width = 2 * rank
    for skip in range(0, stack.shape[0], CHUNK):
        count = min(CHUNK, stack.shape[0] - skip)
        part = lax.dot_general(
            latent[...],
            stack[skip : skip + count, :],
            (((1,), (1,)), ((), ())),
            preferred_element_type=jnp.float32,
        )
        owners = owner_row(info, blocks[skip // rank : (skip + count) // rank], rank)
        for lane in range(0, count, width):
            lanes = slice(lane, lane + width)
            fold = jnp.where(ids[...] == owners[:, lanes], part[:, lanes], 0.0)
            total = fold if total is None else total + fold
    return total


def down_whole_kernel(info, row_ids, latent, stack, out, ids):
    ids[...] = spread_rows(row_ids)
    rank = out.shape[1] // 2
    blocks = range(stack.shape[0] // rank)
    out[...] = masked_products(info, ids, latent, stack, blocks, rank)


def down_first_kernel(info, row_ids, latent, own, beside, *refs):
    *received, _, out, ids, stack = refs
    ids[...] = spread_rows(row_ids)
    rank = own.shape[0]
    holds = info[1] == 1
    stack[0:rank, :] = own[...]
    stack[rank : 2 * rank, :] = beside[...]
    fill_here(info, holds, received, stack, 2 * rank, rank)
    fill_beside(info, holds, received, stack, 3 * rank, rank, corner=False)
    pl.when(jnp.logical_not(holds))(lambda: clear(stack, 3 * rank, rank, 3))
    out[...] = masked_products(info, ids, latent, stack, range(stack.shape[0] // rank), rank)


def down_last_kernel(info, ids, latent, earlier, *refs):
    *corners, out, stack = refs
    rank = out.shape[1] // 2
    holds = info[1] == 1

    @pl.when(holds)
    def _():
        out[...] = earlier[...]

    @pl.when(jnp.logical_not(holds))
    def _():
        for number, corner in enumerate(corners):
            stack[number * rank : (number + 1) * rank, :] = corner[...]
        stack[3 * rank : 4 * rank, :] = jnp.zeros((rank, stack.shape[1]), stack.dtype)
        pair = masked_products(info, ids, latent, stack, (3, 5, 7, None), rank)
        fold = pair[:, :rank] + pair[:, rank:]
        out[...] = earlier[...] + jnp.concatenate([jnp.zeros_like(fold), fold], axis=1)


def base_kernel(info, own, other, weight, *refs, skip):
    out, token = refs[-2:]
    token[...] = jnp.zeros_like(token)
    width = own.shape[1]
    mine = pl.ds(pl.multiple_of(info[0] * width, width), width)
    rest = pl.ds(pl.multiple_of((1 - info[0]) * width, width), width)
    step = min(CHUNK, out.shape[1])
    for begin in range(0, out.shape[1], step):
        place = slice(begin, min(begin + step, out.shape[1]))
        source = slice(skip + begin, skip + place.stop)
        out[:, place] = jnp.dot(
            own[...], weight[mine, source], preferred_element_type=jnp.float32
        ) + jnp.dot(other[...], weight[rest, source], preferred_element_type=jnp.float32)


def base(info, latent, other, weight, after, skip, end):
    rows, columns = latent.shape[0], end - skip
    return pl.pallas_call(
        lambda *refs: base_kernel(*refs, skip=skip),
        out_shape=[jax.ShapeDtypeStruct((rows, columns), jnp.float32), TOKEN],
        in_specs=[SMEM, VMEM, VMEM, VMEM] + [ANY] * len(after),
        out_specs=[VMEM, VMEM],
        compiler_params=pltpu.CompilerParams(vmem_limit_bytes=24 * MIB),
        cost_estimate=pl.CostEstimate(
            flops=1000,
            bytes_accessed=1000,
            transcendentals=0,
        ),
    )(info, latent, other, weight, *after)


def up_kernel(info, ids, mine, theirs, *refs, base_parts):
    *pieces, out, stack, wide, sems, staged = refs[base_parts:]
    bases = [
        part.at[:, pl.ds(begin, TILE)]
        for part in refs[:base_parts]
        for begin in range(0, part.shape[1], TILE)
    ]
    rank = mine.shape[1] // 2
    if len(pieces) == 1:
        stack[...] = pieces[0][...]
    else:
        own, beside, *received = pieces
        holds = info[1] == 0
        stack[0:rank, :] = own[...]
        stack[rank : 2 * rank, :] = beside[...]
        fill_here(info, holds, received, stack, 2 * rank, rank)
        fill_beside(info, holds, received, stack, 3 * rank, rank)
    lowrank = (mine[...] + theirs[...]).astype(jnp.bfloat16)
    zeros = jnp.zeros_like(lowrank)
    width = 2 * rank
    for lane in range(0, wide.shape[1], width):
        mask = ids[...] == owner_row(info, (lane // rank, lane // rank + 1), rank)
        wide[:, lane : lane + width] = jnp.where(mask, lowrank, zeros)
    copies = []
    tiles, _, tile = staged.shape
    for number in range(tiles):
        place = pl.ds(number * tile, tile)
        delta = jnp.dot(wide[...], stack[:, place], preferred_element_type=jnp.float32)
        total = bases[number][...] + delta.astype(jnp.bfloat16).astype(jnp.float32)
        staged[number] = total.astype(out.dtype)
        copies.append(
            pltpu.make_async_copy(staged.at[number], out.at[:, place], sems.at[number])
        )
        copies[-1].start()
    for copy in copies:
        copy.wait()


def on_device(latent, row_adapter_index, shared_weight, adapter_down_weight, adapter_up_weight):
    rows, half_width = latent.shape
    out_width = shared_weight.shape[1]
    local_adapters, _, rank = adapter_down_weight.shape
    shards = lax.axis_size("shard")
    adapters = shards * local_adapters
    columns = adapters * rank
    index, core = lax.axis_index("shard"), lax.axis_index("tensor")
    holds_down = core == lax.axis_index("replica")
    tiles = out_width // TILE
    cuts = [0, out_width // 6, out_width // 2, out_width]
    down = jnp.swapaxes(adapter_down_weight, 1, 2).reshape(local_adapters * rank, half_width)
    up = adapter_up_weight.reshape(local_adapters * rank, out_width)
    row_ids = row_adapter_index.reshape(1, rows)
    routed = shards == 8 and local_adapters == 1 and lax.axis_size("replica") == 2
    routed = routed and half_width == out_width and tiles % 6 == 0
    lowrank = jax.ShapeDtypeStruct((rows, 2 * rank), jnp.float32)
    if routed:
        sources = [ring_step(index, -step) for step in (0, 1, 3, 2)]
        owners = [a for source in sources for a in (source, source ^ 1)]
    else:
        owners = list(range(adapters))
    info = jnp.stack([jnp.asarray(v, jnp.int32) for v in (core, holds_down, *owners)])
    (token,) = call(prepare_kernel, [TOKEN], [VMEM, ANY], 16, moved=COPY)(shared_weight, info)
    down_out = [lowrank, jax.ShapeDtypeStruct((rows, 2 * rank), jnp.int32)]
    if routed:
        piece = jnp.where(holds_down, down, up)
        line = {1: along_line(piece, shards, 1)}
        other = swap(latent, "tensor")
        down_beside, up_beside = neighbour(down, shards), neighbour(up, shards)
        ready = token
        one, token = pack([(line[1], 0, rank)], token, down_beside, other)
        back, _ = pack([(piece, 0, rank)], ready)
        line[3] = along_line(back, shards, 3)
        line[2] = along_line(one, shards, 1)
        one_first, one_second = in_plane(one, shards, True), in_plane(one, shards, False)
        part_one, token = base(info, latent, other, shared_weight, [token], cuts[0], cuts[1])
        three, token = pack([(line[3], 0, rank)], token)
        three_first, three_second = in_plane(three, shards, True), in_plane(three, shards, False)
        part_two, token = base(info, latent, other, shared_weight, [token, up_beside], cuts[1], cuts[2])
        two, token = pack([(line[2], 0, rank)], token)
        two_second = in_plane(two, shards, False)
        turn, token = pack([(one_first, 0, rank)], token, one_second)
        corner_one = in_plane(turn, shards, False)
        two_first = along_line(turn, shards, 1)
        turn, token = pack([(three_second, 0, rank)], token, three_first)
        corner_three = in_plane(turn, shards, True)
        turn, token = pack([(two_second, 0, rank)], token)
        corner_two = in_plane(turn, shards, True)
        part_three, token = base(info, latent, other, shared_weight, [token], cuts[2], cuts[3])
        parts = [part_one, part_two, part_three]
        corners = [corner_one, corner_three, corner_two]
        received = [one, three, two, one_first, three_first, two_first]
        received += [one_second, three_second, two_second]
        mine, ids = call(
            down_first_kernel,
            down_out,
            [SMEM] + [VMEM] * 13 + [ANY],
            16,
            [pltpu.VMEM((columns, half_width), latent.dtype)],
        )(info, row_ids, latent, down, down_beside, *received, token)
        mine = call(
            down_last_kernel,
            lowrank,
            [SMEM] + [VMEM] * 6,
            16,
            [pltpu.VMEM((4 * rank, half_width), latent.dtype)],
        )(info, ids, latent, mine, *corners)
        up_pieces = [up, up_beside, *received, *corners]
    else:
        other = swap(latent, "tensor")
        parts = []
        for begin, end in zip(cuts[:-1], cuts[1:]):
            part, token = base(info, latent, other, shared_weight, [token], begin, end)
            parts.append(part)
        mine, ids = call(down_whole_kernel, down_out, [SMEM] + [VMEM] * 3, 48)(
            info, row_ids, latent, lax.all_gather(down, "shard", axis=0, tiled=True)
        )
        up_pieces = [lax.all_gather(up, "shard", axis=0, tiled=True)]
    theirs = swap(mine, "tensor")

    return pl.pallas_call(
        lambda *refs: up_kernel(*refs, base_parts=len(parts)),
        out_shape=jax.ShapeDtypeStruct((rows, out_width), latent.dtype),
        in_specs=[SMEM] + [VMEM] * (3 + len(parts) + len(up_pieces)),
        out_specs=ANY,
        scratch_shapes=[
            pltpu.VMEM((columns, out_width), latent.dtype),
            pltpu.VMEM((rows, columns), latent.dtype),
            pltpu.SemaphoreType.DMA((tiles,)),
            pltpu.VMEM((tiles, rows, TILE), latent.dtype),
        ],
        compiler_params=pltpu.CompilerParams(vmem_limit_bytes=(24 if routed else 56) * MIB),
    )(info, ids, mine, theirs, *parts, *up_pieces)


def solution(mesh):
    return jax.shard_map(
        on_device,
        mesh=mesh,
        in_specs=(
            P(("replica", "shard"), "tensor"),
            P(("replica", "shard"), None),
            P(None, "tensor"),
            P("shard", "tensor", None),
            P("shard", None, "tensor"),
        ),
        out_specs=P(("replica", "shard"), "tensor"),
        check_vma=False,
    )
```

```python
import jax
import jax.numpy as jnp
import numpy as np
from jax import lax
from jax.experimental import pallas as pl
from jax.experimental.pallas import tpu as pltpu
from jax.sharding import PartitionSpec as P

MIB = 1024 * 1024
CHUNK = 512
TILE = 256
AXES = ("replica", "shard", "tensor")
FIRST_OWNER = 2
COPY = 0
SMEM = pl.BlockSpec(memory_space=pltpu.SMEM)
VMEM = pl.BlockSpec(memory_space=pltpu.VMEM)
ANY = pl.BlockSpec(memory_space=pl.ANY)
TOKEN = jax.ShapeDtypeStruct((8, 128), jnp.float32)


def swap(value, axis):
    return lax.ppermute(value, axis, [(0, 1), (1, 0)])


def neighbour(value, shards):
    return lax.ppermute(value, "shard", [(i, i ^ 1) for i in range(shards)])


def ring_step(index, step):
    plane = index >> 1
    place = ((plane ^ (plane >> 1)) + step) & 3
    return ((place ^ (place >> 1)) << 1) | (index & 1)


def along_line(value, shards, step):
    return lax.ppermute(value, "shard", [(i, ring_step(i, step)) for i in range(shards)])


def in_plane(value, shards, first):
    pairs = []
    for r in range(2):
        for s in range(shards):
            for t in range(2):
                to_r, to_s = (r, s ^ 1) if (t == 0) == first else (r ^ 1, s)
                pairs.append(((r * shards + s) * 2 + t, (to_r * shards + to_s) * 2 + t))
    return lax.ppermute(value, AXES, pairs)


def call(kernel, out_shape, in_specs, limit, scratch=(), flops=0, moved=0):
    return pl.pallas_call(
        kernel,
        out_shape=out_shape,
        in_specs=in_specs,
        out_specs=jax.tree.map(lambda _: VMEM, out_shape),
        scratch_shapes=list(scratch),
        compiler_params=pltpu.CompilerParams(vmem_limit_bytes=limit * MIB),
        cost_estimate=pl.CostEstimate(flops=flops, bytes_accessed=moved, transcendentals=0),
    )


def owner_row(info, blocks, rank):
    place = lax.broadcasted_iota(jnp.int32, (1, len(blocks) * rank), 1) // rank
    row = jnp.full(place.shape, -1, jnp.int32)
    for number, block in enumerate(blocks):
        if block is not None:
            row = jnp.where(place == number, info[FIRST_OWNER + block], row)
    return row


def pack(pieces, *after):
    count = len(pieces)
    total = sum(rows for _, _, rows in pieces)
    width, dtype = pieces[0][0].shape[1], pieces[0][0].dtype

    def kernel(*refs):
        out, token = refs[-2:]
        top = 0
        for ref, (_, begin, rows) in zip(refs, pieces):
            out[top : top + rows, :] = ref[begin : begin + rows, :]
            top += rows
        token[...] = jnp.zeros_like(token)

    return call(
        kernel,
        [jax.ShapeDtypeStruct((total, width), dtype), TOKEN],
        [VMEM] * count + [ANY] * len(after),
        4,
        moved=COPY,
    )(*[array for array, _, _ in pieces], *after)


def put(blocks, stack, top, rank):
    for number, block in enumerate(blocks):
        place = top + 2 * number * rank
        stack[place : place + rank, :] = block[...]


def fill_here(info, holds, received, stack, top, rank):
    here, first, second = received[0:3], received[3:6], received[6:9]
    pl.when(holds)(lambda: put(here, stack, top, rank))
    for core, refs in enumerate((second, first)):
        away = jnp.logical_not(holds) & (info[0] == core)
        pl.when(away)(lambda refs=refs: put(refs, stack, top, rank))


def fill_beside(info, holds, received, stack, top, rank, direct=True, corner=True):
    if direct:
        for core, refs in enumerate((received[3:6], received[6:9])):
            pl.when(holds & (info[0] == core))(lambda refs=refs: put(refs, stack, top, rank))
    if corner:
        corners = received[9:12]
        pl.when(jnp.logical_not(holds))(lambda: put(corners, stack, top, rank))


def clear(stack, top, rank, count):
    for number in range(count):
        place = top + 2 * number * rank
        stack[place : place + rank, :] = jnp.zeros((rank, stack.shape[1]), stack.dtype)


def prepare_kernel(weight, *refs):
    refs[-1][...] = weight[0:8, 0:128].astype(jnp.float32)


def spread_rows(row_ids):
    wide = jnp.broadcast_to(row_ids[...].astype(jnp.float32), (128, row_ids.shape[1]))
    return wide.T.astype(jnp.int32)


def masked_products(info, ids, latent, stack, blocks, rank):
    total = None
    width = 2 * rank
    for skip in range(0, stack.shape[0], CHUNK):
        count = min(CHUNK, stack.shape[0] - skip)
        part = lax.dot_general(
            latent[...],
            stack[skip : skip + count, :],
            (((1,), (1,)), ((), ())),
            preferred_element_type=jnp.float32,
        )
        owners = owner_row(info, blocks[skip // rank : (skip + count) // rank], rank)
        for lane in range(0, count, width):
            lanes = slice(lane, lane + width)
            fold = jnp.where(ids[...] == owners[:, lanes], part[:, lanes], 0.0)
            total = fold if total is None else total + fold
    return total


def down_whole_kernel(info, row_ids, latent, stack, out, ids):
    ids[...] = spread_rows(row_ids)
    rank = out.shape[1] // 2
    blocks = range(stack.shape[0] // rank)
    out[...] = masked_products(info, ids, latent, stack, blocks, rank)


def down_first_kernel(info, row_ids, latent, own, beside, *refs):
    *received, _, out, ids, stack = refs
    ids[...] = spread_rows(row_ids)
    rank = own.shape[0]
    holds = info[1] == 1
    stack[0:rank, :] = own[...]
    stack[rank : 2 * rank, :] = beside[...]
    fill_here(info, holds, received, stack, 2 * rank, rank)
    fill_beside(info, holds, received, stack, 3 * rank, rank, corner=False)
    pl.when(jnp.logical_not(holds))(lambda: clear(stack, 3 * rank, rank, 3))
    out[...] = masked_products(info, ids, latent, stack, range(stack.shape[0] // rank), rank)


def down_last_kernel(info, ids, latent, earlier, *refs):
    *corners, out, stack = refs
    rank = out.shape[1] // 2
    holds = info[1] == 1

    @pl.when(holds)
    def _():
        out[...] = earlier[...]

    @pl.when(jnp.logical_not(holds))
    def _():
        for number, corner in enumerate(corners):
            stack[number * rank : (number + 1) * rank, :] = corner[...]
        stack[3 * rank : 4 * rank, :] = jnp.zeros((rank, stack.shape[1]), stack.dtype)
        pair = masked_products(info, ids, latent, stack, (3, 5, 7, None), rank)
        fold = pair[:, :rank] + pair[:, rank:]
        out[...] = earlier[...] + jnp.concatenate([jnp.zeros_like(fold), fold], axis=1)


def base_kernel(info, own, other, weight, *refs, skip):
    out, token = refs[-2:]
    token[...] = jnp.zeros_like(token)
    width = own.shape[1]
    mine = pl.ds(pl.multiple_of(info[0] * width, width), width)
    rest = pl.ds(pl.multiple_of((1 - info[0]) * width, width), width)
    step = min(CHUNK, out.shape[1])
    for begin in range(0, out.shape[1], step):
        place = slice(begin, min(begin + step, out.shape[1]))
        source = slice(skip + begin, skip + place.stop)
        out[:, place] = jnp.dot(
            own[...], weight[mine, source], preferred_element_type=jnp.float32
        ) + jnp.dot(other[...], weight[rest, source], preferred_element_type=jnp.float32)


def base(info, latent, other, weight, after, skip, end):
    rows, columns = latent.shape[0], end - skip
    return pl.pallas_call(
        lambda *refs: base_kernel(*refs, skip=skip),
        out_shape=[jax.ShapeDtypeStruct((rows, columns), jnp.float32), TOKEN],
        in_specs=[SMEM, VMEM, VMEM, VMEM] + [ANY] * len(after),
        out_specs=[VMEM, VMEM],
        compiler_params=pltpu.CompilerParams(vmem_limit_bytes=24 * MIB),
        cost_estimate=pl.CostEstimate(
            flops=1000,
            bytes_accessed=1000,
            transcendentals=0,
        ),
    )(info, latent, other, weight, *after)


def up_kernel(info, ids, mine, theirs, *refs, base_parts):
    *pieces, out, stack, wide, sems, staged = refs[base_parts:]
    bases = [
        part.at[:, pl.ds(begin, TILE)]
        for part in refs[:base_parts]
        for begin in range(0, part.shape[1], TILE)
    ]
    rank = mine.shape[1] // 2
    if len(pieces) == 1:
        stack[...] = pieces[0][...]
    else:
        own, beside, *received = pieces
        holds = info[1] == 0
        stack[0:rank, :] = own[...]
        stack[rank : 2 * rank, :] = beside[...]
        fill_here(info, holds, received, stack, 2 * rank, rank)
        fill_beside(info, holds, received, stack, 3 * rank, rank)
    lowrank = (mine[...] + theirs[...]).astype(jnp.bfloat16)
    zeros = jnp.zeros_like(lowrank)
    width = 2 * rank
    for lane in range(0, wide.shape[1], width):
        mask = ids[...] == owner_row(info, (lane // rank, lane // rank + 1), rank)
        wide[:, lane : lane + width] = jnp.where(mask, lowrank, zeros)
    copies = []
    tiles, _, tile = staged.shape
    for number in range(tiles):
        place = pl.ds(number * tile, tile)
        delta = jnp.dot(wide[...], stack[:, place], preferred_element_type=jnp.float32)
        total = bases[number][...] + delta.astype(jnp.bfloat16).astype(jnp.float32)
        staged[number] = total.astype(out.dtype)
        copies.append(
            pltpu.make_async_copy(staged.at[number], out.at[:, place], sems.at[number])
        )
        copies[-1].start()
    for copy in copies:
        copy.wait()


def on_device(latent, row_adapter_index, shared_weight, adapter_down_weight, adapter_up_weight):
    rows, half_width = latent.shape
    out_width = shared_weight.shape[1]
    local_adapters, _, rank = adapter_down_weight.shape
    shards = lax.axis_size("shard")
    adapters = shards * local_adapters
    columns = adapters * rank
    index, core = lax.axis_index("shard"), lax.axis_index("tensor")
    holds_down = core == lax.axis_index("replica")
    tiles = out_width // TILE
    cuts = [0, out_width // 6, out_width // 2, out_width]
    down = jnp.swapaxes(adapter_down_weight, 1, 2).reshape(local_adapters * rank, half_width)
    up = adapter_up_weight.reshape(local_adapters * rank, out_width)
    row_ids = row_adapter_index.reshape(1, rows)
    routed = shards == 8 and local_adapters == 1 and lax.axis_size("replica") == 2
    routed = routed and half_width == out_width and tiles % 6 == 0
    lowrank = jax.ShapeDtypeStruct((rows, 2 * rank), jnp.float32)
    if routed:
        sources = [ring_step(index, -step) for step in (0, 1, 3, 2)]
        owners = [a for source in sources for a in (source, source ^ 1)]
    else:
        owners = list(range(adapters))
    info = jnp.stack([jnp.asarray(v, jnp.int32) for v in (core, holds_down, *owners)])
    (token,) = call(prepare_kernel, [TOKEN], [VMEM, ANY], 16, moved=COPY)(shared_weight, info)
    down_out = [lowrank, jax.ShapeDtypeStruct((rows, 2 * rank), jnp.int32)]
    if routed:
        piece = jnp.where(holds_down, down, up)
        line = {1: along_line(piece, shards, 1)}
        other = swap(latent, "tensor")
        down_beside, up_beside = neighbour(down, shards), neighbour(up, shards)
        ready = token
        one, token = pack([(line[1], 0, rank)], token, down_beside, up_beside, other)
        back, _ = pack([(piece, 0, rank)], ready)
        line[3] = along_line(back, shards, 3)
        line[2] = along_line(one, shards, 1)
        one_first, one_second = in_plane(one, shards, True), in_plane(one, shards, False)
        part_one, token = base(info, latent, other, shared_weight, [token], cuts[0], cuts[1])
        three, token = pack([(line[3], 0, rank)], token)
        three_first, three_second = in_plane(three, shards, True), in_plane(three, shards, False)
        part_two, token = base(info, latent, other, shared_weight, [token], cuts[1], cuts[2])
        two, token = pack([(line[2], 0, rank)], token)
        two_second = in_plane(two, shards, False)
        turn, token = pack([(one_first, 0, rank)], token, one_second)
        corner_one = in_plane(turn, shards, False)
        two_first = along_line(turn, shards, 1)
        turn, token = pack([(three_second, 0, rank)], token, three_first)
        corner_three = in_plane(turn, shards, True)
        turn, token = pack([(two_second, 0, rank)], token)
        corner_two = in_plane(turn, shards, True)
        part_three, token = base(info, latent, other, shared_weight, [token], cuts[2], cuts[3])
        parts = [part_one, part_two, part_three]
        corners = [corner_one, corner_three, corner_two]
        received = [one, three, two, one_first, three_first, two_first]
        received += [one_second, three_second, two_second]
        mine, ids = call(
            down_first_kernel,
            down_out,
            [SMEM] + [VMEM] * 13 + [ANY],
            16,
            [pltpu.VMEM((columns, half_width), latent.dtype)],
        )(info, row_ids, latent, down, down_beside, *received, token)
        mine = call(
            down_last_kernel,
            lowrank,
            [SMEM] + [VMEM] * 6,
            16,
            [pltpu.VMEM((4 * rank, half_width), latent.dtype)],
        )(info, ids, latent, mine, *corners)
        up_pieces = [up, up_beside, *received, *corners]
    else:
        other = swap(latent, "tensor")
        parts = []
        for begin, end in zip(cuts[:-1], cuts[1:]):
            part, token = base(info, latent, other, shared_weight, [token], begin, end)
            parts.append(part)
        mine, ids = call(down_whole_kernel, down_out, [SMEM] + [VMEM] * 3, 48)(
            info, row_ids, latent, lax.all_gather(down, "shard", axis=0, tiled=True)
        )
        up_pieces = [lax.all_gather(up, "shard", axis=0, tiled=True)]
    theirs = swap(mine, "tensor")

    return pl.pallas_call(
        lambda *refs: up_kernel(*refs, base_parts=len(parts)),
        out_shape=jax.ShapeDtypeStruct((rows, out_width), latent.dtype),
        in_specs=[SMEM] + [VMEM] * (3 + len(parts) + len(up_pieces)),
        out_specs=ANY,
        scratch_shapes=[
            pltpu.VMEM((columns, out_width), latent.dtype),
            pltpu.VMEM((rows, columns), latent.dtype),
            pltpu.SemaphoreType.DMA((tiles,)),
            pltpu.VMEM((tiles, rows, TILE), latent.dtype),
        ],
        compiler_params=pltpu.CompilerParams(vmem_limit_bytes=(24 if routed else 56) * MIB),
    )(info, ids, mine, theirs, *parts, *up_pieces)


def solution(mesh):
    return jax.shard_map(
        on_device,
        mesh=mesh,
        in_specs=(
            P(("replica", "shard"), "tensor"),
            P(("replica", "shard"), None),
            P(None, "tensor"),
            P("shard", "tensor", None),
            P("shard", None, "tensor"),
        ),
        out_specs=P(("replica", "shard"), "tensor"),
        check_vma=False,
    )
```

```python
import jax
import jax.numpy as jnp
import numpy as np
from jax import lax
from jax.experimental import pallas as pl
from jax.experimental.pallas import tpu as pltpu
from jax.sharding import PartitionSpec as P

MIB = 1024 * 1024
CHUNK = 512
TILE = 256
AXES = ("replica", "shard", "tensor")
FIRST_OWNER = 2
COPY = 0
SMEM = pl.BlockSpec(memory_space=pltpu.SMEM)
VMEM = pl.BlockSpec(memory_space=pltpu.VMEM)
ANY = pl.BlockSpec(memory_space=pl.ANY)
TOKEN = jax.ShapeDtypeStruct((8, 128), jnp.float32)


def swap(value, axis):
    return lax.ppermute(value, axis, [(0, 1), (1, 0)])


def neighbour(value, shards):
    return lax.ppermute(value, "shard", [(i, i ^ 1) for i in range(shards)])


def ring_step(index, step):
    plane = index >> 1
    place = ((plane ^ (plane >> 1)) + step) & 3
    return ((place ^ (place >> 1)) << 1) | (index & 1)


def along_line(value, shards, step):
    return lax.ppermute(value, "shard", [(i, ring_step(i, step)) for i in range(shards)])


def in_plane(value, shards, first):
    pairs = []
    for r in range(2):
        for s in range(shards):
            for t in range(2):
                to_r, to_s = (r, s ^ 1) if (t == 0) == first else (r ^ 1, s)
                pairs.append(((r * shards + s) * 2 + t, (to_r * shards + to_s) * 2 + t))
    return lax.ppermute(value, AXES, pairs)


def call(kernel, out_shape, in_specs, limit, scratch=(), flops=0, moved=0):
    return pl.pallas_call(
        kernel,
        out_shape=out_shape,
        in_specs=in_specs,
        out_specs=jax.tree.map(lambda _: VMEM, out_shape),
        scratch_shapes=list(scratch),
        compiler_params=pltpu.CompilerParams(vmem_limit_bytes=limit * MIB),
        cost_estimate=pl.CostEstimate(flops=flops, bytes_accessed=moved, transcendentals=0),
    )


def owner_row(info, blocks, rank):
    place = lax.broadcasted_iota(jnp.int32, (1, len(blocks) * rank), 1) // rank
    row = jnp.full(place.shape, -1, jnp.int32)
    for number, block in enumerate(blocks):
        if block is not None:
            row = jnp.where(place == number, info[FIRST_OWNER + block], row)
    return row


def pack(pieces, *after):
    count = len(pieces)
    total = sum(rows for _, _, rows in pieces)
    width, dtype = pieces[0][0].shape[1], pieces[0][0].dtype

    def kernel(*refs):
        out, token = refs[-2:]
        top = 0
        for ref, (_, begin, rows) in zip(refs, pieces):
            out[top : top + rows, :] = ref[begin : begin + rows, :]
            top += rows
        token[...] = jnp.zeros_like(token)

    return call(
        kernel,
        [jax.ShapeDtypeStruct((total, width), dtype), TOKEN],
        [VMEM] * count + [ANY] * len(after),
        4,
        moved=COPY,
    )(*[array for array, _, _ in pieces], *after)


def put(blocks, stack, top, rank):
    for number, block in enumerate(blocks):
        place = top + 2 * number * rank
        stack[place : place + rank, :] = block[...]


def fill_here(info, holds, received, stack, top, rank):
    here, first, second = received[0:3], received[3:6], received[6:9]
    pl.when(holds)(lambda: put(here, stack, top, rank))
    for core, refs in enumerate((second, first)):
        away = jnp.logical_not(holds) & (info[0] == core)
        pl.when(away)(lambda refs=refs: put(refs, stack, top, rank))


def fill_beside(info, holds, received, stack, top, rank, direct=True, corner=True):
    if direct:
        for core, refs in enumerate((received[3:6], received[6:9])):
            pl.when(holds & (info[0] == core))(lambda refs=refs: put(refs, stack, top, rank))
    if corner:
        corners = received[9:12]
        pl.when(jnp.logical_not(holds))(lambda: put(corners, stack, top, rank))


def clear(stack, top, rank, count):
    for number in range(count):
        place = top + 2 * number * rank
        stack[place : place + rank, :] = jnp.zeros((rank, stack.shape[1]), stack.dtype)


def prepare_kernel(weight, *refs):
    refs[-1][...] = weight[0:8, 0:128].astype(jnp.float32)


def spread_rows(row_ids):
    wide = jnp.broadcast_to(row_ids[...].astype(jnp.float32), (128, row_ids.shape[1]))
    return wide.T.astype(jnp.int32)


def masked_products(info, ids, latent, stack, blocks, rank):
    total = None
    width = 2 * rank
    for skip in range(0, stack.shape[0], CHUNK):
        count = min(CHUNK, stack.shape[0] - skip)
        part = lax.dot_general(
            latent[...],
            stack[skip : skip + count, :],
            (((1,), (1,)), ((), ())),
            preferred_element_type=jnp.float32,
        )
        owners = owner_row(info, blocks[skip // rank : (skip + count) // rank], rank)
        for lane in range(0, count, width):
            lanes = slice(lane, lane + width)
            fold = jnp.where(ids[...] == owners[:, lanes], part[:, lanes], 0.0)
            total = fold if total is None else total + fold
    return total


def down_whole_kernel(info, row_ids, latent, stack, out, ids):
    ids[...] = spread_rows(row_ids)
    rank = out.shape[1] // 2
    blocks = range(stack.shape[0] // rank)
    out[...] = masked_products(info, ids, latent, stack, blocks, rank)


def down_first_kernel(info, row_ids, latent, own, beside, *refs):
    *received, _, out, ids, stack = refs
    ids[...] = spread_rows(row_ids)
    rank = own.shape[0]
    holds = info[1] == 1
    stack[0:rank, :] = own[...]
    stack[rank : 2 * rank, :] = beside[...]
    fill_here(info, holds, received, stack, 2 * rank, rank)
    fill_beside(info, holds, received, stack, 3 * rank, rank, corner=False)
    pl.when(jnp.logical_not(holds))(lambda: clear(stack, 3 * rank, rank, 3))
    out[...] = masked_products(info, ids, latent, stack, range(stack.shape[0] // rank), rank)


def down_last_kernel(info, ids, latent, earlier, *refs):
    *corners, out, stack = refs
    rank = out.shape[1] // 2
    holds = info[1] == 1

    @pl.when(holds)
    def _():
        out[...] = earlier[...]

    @pl.when(jnp.logical_not(holds))
    def _():
        for number, corner in enumerate(corners):
            stack[number * rank : (number + 1) * rank, :] = corner[...]
        stack[3 * rank : 4 * rank, :] = jnp.zeros((rank, stack.shape[1]), stack.dtype)
        pair = masked_products(info, ids, latent, stack, (3, 5, 7, None), rank)
        fold = pair[:, :rank] + pair[:, rank:]
        out[...] = earlier[...] + jnp.concatenate([jnp.zeros_like(fold), fold], axis=1)


def base_kernel(info, own, other, weight, *refs, skip):
    out, token = refs[-2:]
    token[...] = jnp.zeros_like(token)
    width = own.shape[1]
    mine = pl.ds(pl.multiple_of(info[0] * width, width), width)
    rest = pl.ds(pl.multiple_of((1 - info[0]) * width, width), width)
    step = min(CHUNK, out.shape[1])
    for begin in range(0, out.shape[1], step):
        place = slice(begin, min(begin + step, out.shape[1]))
        source = slice(skip + begin, skip + place.stop)
        out[:, place] = jnp.dot(
            own[...], weight[mine, source], preferred_element_type=jnp.float32
        ) + jnp.dot(other[...], weight[rest, source], preferred_element_type=jnp.float32)


def base(info, latent, other, weight, after, skip, end):
    rows, columns = latent.shape[0], end - skip
    return pl.pallas_call(
        lambda *refs: base_kernel(*refs, skip=skip),
        out_shape=[jax.ShapeDtypeStruct((rows, columns), jnp.float32), TOKEN],
        in_specs=[SMEM, VMEM, VMEM, VMEM] + [ANY] * len(after),
        out_specs=[VMEM, VMEM],
        compiler_params=pltpu.CompilerParams(vmem_limit_bytes=24 * MIB),
        cost_estimate=pl.CostEstimate(
            flops=1000,
            bytes_accessed=1000,
            transcendentals=0,
        ),
    )(info, latent, other, weight, *after)


def up_kernel(info, ids, mine, theirs, *refs, base_parts):
    *pieces, out, stack, wide, sems, staged = refs[base_parts:]
    bases = [
        part.at[:, pl.ds(begin, TILE)]
        for part in refs[:base_parts]
        for begin in range(0, part.shape[1], TILE)
    ]
    rank = mine.shape[1] // 2
    if len(pieces) == 1:
        stack[...] = pieces[0][...]
    else:
        own, beside, *received = pieces
        holds = info[1] == 0
        stack[0:rank, :] = own[...]
        stack[rank : 2 * rank, :] = beside[...]
        fill_here(info, holds, received, stack, 2 * rank, rank)
        fill_beside(info, holds, received, stack, 3 * rank, rank)
    lowrank = (mine[...] + theirs[...]).astype(jnp.bfloat16)
    zeros = jnp.zeros_like(lowrank)
    width = 2 * rank
    for lane in range(0, wide.shape[1], width):
        mask = ids[...] == owner_row(info, (lane // rank, lane // rank + 1), rank)
        wide[:, lane : lane + width] = jnp.where(mask, lowrank, zeros)
    copies = []
    tiles, _, tile = staged.shape
    for number in range(tiles):
        place = pl.ds(number * tile, tile)
        delta = jnp.dot(wide[...], stack[:, place], preferred_element_type=jnp.float32)
        total = bases[number][...] + delta.astype(jnp.bfloat16).astype(jnp.float32)
        staged[number] = total.astype(out.dtype)
        copies.append(
            pltpu.make_async_copy(staged.at[number], out.at[:, place], sems.at[number])
        )
        copies[-1].start()
    for copy in copies:
        copy.wait()


def on_device(latent, row_adapter_index, shared_weight, adapter_down_weight, adapter_up_weight):
    rows, half_width = latent.shape
    out_width = shared_weight.shape[1]
    local_adapters, _, rank = adapter_down_weight.shape
    shards = lax.axis_size("shard")
    adapters = shards * local_adapters
    columns = adapters * rank
    index, core = lax.axis_index("shard"), lax.axis_index("tensor")
    holds_down = core == lax.axis_index("replica")
    tiles = out_width // TILE
    cuts = [0, out_width // 6, out_width // 2, out_width]
    down = jnp.swapaxes(adapter_down_weight, 1, 2).reshape(local_adapters * rank, half_width)
    up = adapter_up_weight.reshape(local_adapters * rank, out_width)
    row_ids = row_adapter_index.reshape(1, rows)
    routed = shards == 8 and local_adapters == 1 and lax.axis_size("replica") == 2
    routed = routed and half_width == out_width and tiles % 6 == 0
    lowrank = jax.ShapeDtypeStruct((rows, 2 * rank), jnp.float32)
    if routed:
        sources = [ring_step(index, -step) for step in (0, 1, 3, 2)]
        owners = [a for source in sources for a in (source, source ^ 1)]
    else:
        owners = list(range(adapters))
    info = jnp.stack([jnp.asarray(v, jnp.int32) for v in (core, holds_down, *owners)])
    (token,) = call(prepare_kernel, [TOKEN], [VMEM, ANY], 16, moved=COPY)(shared_weight, info)
    down_out = [lowrank, jax.ShapeDtypeStruct((rows, 2 * rank), jnp.int32)]
    if routed:
        piece = jnp.where(holds_down, down, up)
        line = {1: along_line(piece, shards, 1)}
        other = swap(latent, "tensor")
        down_beside, up_beside = neighbour(down, shards), neighbour(up, shards)
        ready = token
        one, token = pack([(line[1], 0, rank)], token, down_beside)
        back, _ = pack([(piece, 0, rank)], ready, other)
        line[3] = along_line(back, shards, 3)
        line[2] = along_line(one, shards, 1)
        one_first, one_second = in_plane(one, shards, True), in_plane(one, shards, False)
        part_one, token = base(info, latent, other, shared_weight, [token], cuts[0], cuts[1])
        three, token = pack([(line[3], 0, rank)], token, up_beside)
        three_first, three_second = in_plane(three, shards, True), in_plane(three, shards, False)
        part_two, token = base(info, latent, other, shared_weight, [token], cuts[1], cuts[2])
        two, token = pack([(line[2], 0, rank)], token)
        two_second = in_plane(two, shards, False)
        turn, token = pack([(one_first, 0, rank)], token, one_second)
        corner_one = in_plane(turn, shards, False)
        two_first = along_line(turn, shards, 1)
        turn, token = pack([(three_second, 0, rank)], token, three_first)
        corner_three = in_plane(turn, shards, True)
        turn, token = pack([(two_second, 0, rank)], token)
        corner_two = in_plane(turn, shards, True)
        part_three, token = base(info, latent, other, shared_weight, [token], cuts[2], cuts[3])
        parts = [part_one, part_two, part_three]
        corners = [corner_one, corner_three, corner_two]
        received = [one, three, two, one_first, three_first, two_first]
        received += [one_second, three_second, two_second]
        mine, ids = call(
            down_first_kernel,
            down_out,
            [SMEM] + [VMEM] * 13 + [ANY],
            16,
            [pltpu.VMEM((columns, half_width), latent.dtype)],
        )(info, row_ids, latent, down, down_beside, *received, token)
        mine = call(
            down_last_kernel,
            lowrank,
            [SMEM] + [VMEM] * 6,
            16,
            [pltpu.VMEM((4 * rank, half_width), latent.dtype)],
        )(info, ids, latent, mine, *corners)
        up_pieces = [up, up_beside, *received, *corners]
    else:
        other = swap(latent, "tensor")
        parts = []
        for begin, end in zip(cuts[:-1], cuts[1:]):
            part, token = base(info, latent, other, shared_weight, [token], begin, end)
            parts.append(part)
        mine, ids = call(down_whole_kernel, down_out, [SMEM] + [VMEM] * 3, 48)(
            info, row_ids, latent, lax.all_gather(down, "shard", axis=0, tiled=True)
        )
        up_pieces = [lax.all_gather(up, "shard", axis=0, tiled=True)]
    theirs = swap(mine, "tensor")

    return pl.pallas_call(
        lambda *refs: up_kernel(*refs, base_parts=len(parts)),
        out_shape=jax.ShapeDtypeStruct((rows, out_width), latent.dtype),
        in_specs=[SMEM] + [VMEM] * (3 + len(parts) + len(up_pieces)),
        out_specs=ANY,
        scratch_shapes=[
            pltpu.VMEM((columns, out_width), latent.dtype),
            pltpu.VMEM((rows, columns), latent.dtype),
            pltpu.SemaphoreType.DMA((tiles,)),
            pltpu.VMEM((tiles, rows, TILE), latent.dtype),
        ],
        compiler_params=pltpu.CompilerParams(vmem_limit_bytes=(24 if routed else 56) * MIB),
    )(info, ids, mine, theirs, *parts, *up_pieces)


def solution(mesh):
    return jax.shard_map(
        on_device,
        mesh=mesh,
        in_specs=(
            P(("replica", "shard"), "tensor"),
            P(("replica", "shard"), None),
            P(None, "tensor"),
            P("shard", "tensor", None),
            P("shard", None, "tensor"),
        ),
        out_specs=P(("replica", "shard"), "tensor"),
        check_vma=False,
    )
```

```python
import jax
import jax.numpy as jnp
import numpy as np
from jax import lax
from jax.experimental import pallas as pl
from jax.experimental.pallas import tpu as pltpu
from jax.sharding import PartitionSpec as P

MIB = 1024 * 1024
CHUNK = 512
TILE = 256
AXES = ("replica", "shard", "tensor")
FIRST_OWNER = 2
COPY = 0
VMEM = pl.BlockSpec(memory_space=pltpu.VMEM)
ANY = pl.BlockSpec(memory_space=pl.ANY)
TOKEN = jax.ShapeDtypeStruct((8, 128), jnp.float32)


def swap(value, axis):
    return lax.ppermute(value, axis, [(0, 1), (1, 0)])


def neighbour(value, shards):
    return lax.ppermute(value, "shard", [(i, i ^ 1) for i in range(shards)])


def ring_step(index, step):
    plane = index >> 1
    place = ((plane ^ (plane >> 1)) + step) & 3
    return ((place ^ (place >> 1)) << 1) | (index & 1)


def along_line(value, shards, step):
    return lax.ppermute(value, "shard", [(i, ring_step(i, step)) for i in range(shards)])


def in_plane(value, shards, first):
    pairs = []
    for r in range(2):
        for s in range(shards):
            for t in range(2):
                to_r, to_s = (r, s ^ 1) if (t == 0) == first else (r ^ 1, s)
                pairs.append(((r * shards + s) * 2 + t, (to_r * shards + to_s) * 2 + t))
    return lax.ppermute(value, AXES, pairs)


def call(kernel, out_shape, in_specs, limit, scratch=(), flops=0, moved=0):
    return pl.pallas_call(
        kernel,
        out_shape=out_shape,
        in_specs=in_specs,
        out_specs=jax.tree.map(lambda _: VMEM, out_shape),
        scratch_shapes=list(scratch),
        compiler_params=pltpu.CompilerParams(vmem_limit_bytes=limit * MIB),
        cost_estimate=pl.CostEstimate(flops=flops, bytes_accessed=moved, transcendentals=0),
    )


def place_of_device(routed, shards, adapters):
    core, index = lax.axis_index("tensor"), lax.axis_index("shard")
    holds_down = (core == lax.axis_index("replica")).astype(jnp.int32)
    owners = range(adapters)
    if routed:
        sources = [ring_step(index, -step) for step in (0, 1, 3, 2)]
        owners = [a for source in sources for a in (source, source ^ 1)]
    return [core, holds_down, *owners]


def owner_row(info, blocks, rank):
    place = lax.broadcasted_iota(jnp.int32, (1, len(blocks) * rank), 1) // rank
    row = jnp.full(place.shape, -1, jnp.int32)
    for number, block in enumerate(blocks):
        if block is not None:
            row = jnp.where(place == number, info[FIRST_OWNER + block], row)
    return row


def pack(pieces, *after):
    count = len(pieces)
    total = sum(rows for _, _, rows in pieces)
    width, dtype = pieces[0][0].shape[1], pieces[0][0].dtype

    def kernel(*refs):
        out, token = refs[-2:]
        top = 0
        for ref, (_, begin, rows) in zip(refs, pieces):
            out[top : top + rows, :] = ref[begin : begin + rows, :]
            top += rows
        token[...] = jnp.zeros_like(token)

    return call(
        kernel,
        [jax.ShapeDtypeStruct((total, width), dtype), TOKEN],
        [VMEM] * count + [ANY] * len(after),
        4,
        moved=COPY,
    )(*[array for array, _, _ in pieces], *after)


def put(blocks, stack, top, rank):
    for number, block in enumerate(blocks):
        place = top + 2 * number * rank
        stack[place : place + rank, :] = block[...]


def fill_here(info, holds, received, stack, top, rank):
    here, first, second = received[0:3], received[3:6], received[6:9]
    pl.when(holds)(lambda: put(here, stack, top, rank))
    for core, refs in enumerate((second, first)):
        away = jnp.logical_not(holds) & (info[0] == core)
        pl.when(away)(lambda refs=refs: put(refs, stack, top, rank))


def fill_beside(info, holds, received, stack, top, rank, direct=True, corner=True):
    if direct:
        for core, refs in enumerate((received[3:6], received[6:9])):
            pl.when(holds & (info[0] == core))(lambda refs=refs: put(refs, stack, top, rank))
    if corner:
        corners = received[9:12]
        pl.when(jnp.logical_not(holds))(lambda: put(corners, stack, top, rank))


def clear(stack, top, rank, count):
    for number in range(count):
        place = top + 2 * number * rank
        stack[place : place + rank, :] = jnp.zeros((rank, stack.shape[1]), stack.dtype)


def prepare_kernel(weight, *refs):
    refs[-1][...] = weight[0:8, 0:128].astype(jnp.float32)


def spread_rows(row_ids):
    wide = jnp.broadcast_to(row_ids[...].astype(jnp.float32), (128, row_ids.shape[1]))
    return wide.T.astype(jnp.int32)


def masked_products(info, ids, latent, stack, blocks, rank):
    total = None
    width = 2 * rank
    for skip in range(0, stack.shape[0], CHUNK):
        count = min(CHUNK, stack.shape[0] - skip)
        part = lax.dot_general(
            latent[...],
            stack[skip : skip + count, :],
            (((1,), (1,)), ((), ())),
            preferred_element_type=jnp.float32,
        )
        owners = owner_row(info, blocks[skip // rank : (skip + count) // rank], rank)
        for lane in range(0, count, width):
            lanes = slice(lane, lane + width)
            fold = jnp.where(ids[...] == owners[:, lanes], part[:, lanes], 0.0)
            total = fold if total is None else total + fold
    return total


def down_whole_kernel(info, row_ids, latent, stack, out, ids):
    ids[...] = spread_rows(row_ids)
    rank = out.shape[1] // 2
    blocks = range(stack.shape[0] // rank)
    out[...] = masked_products(info, ids, latent, stack, blocks, rank)


def down_first_kernel(info, row_ids, latent, own, beside, *refs):
    *received, _, out, ids, stack = refs
    ids[...] = spread_rows(row_ids)
    rank = own.shape[0]
    holds = info[1] == 1
    stack[0:rank, :] = own[...]
    stack[rank : 2 * rank, :] = beside[...]
    fill_here(info, holds, received, stack, 2 * rank, rank)
    fill_beside(info, holds, received, stack, 3 * rank, rank, corner=False)
    pl.when(jnp.logical_not(holds))(lambda: clear(stack, 3 * rank, rank, 3))
    out[...] = masked_products(info, ids, latent, stack, range(stack.shape[0] // rank), rank)


def down_last_kernel(info, ids, latent, earlier, *refs):
    *corners, out, stack = refs
    rank = out.shape[1] // 2
    holds = info[1] == 1

    @pl.when(holds)
    def _():
        out[...] = earlier[...]

    @pl.when(jnp.logical_not(holds))
    def _():
        for number, corner in enumerate(corners):
            stack[number * rank : (number + 1) * rank, :] = corner[...]
        stack[3 * rank : 4 * rank, :] = jnp.zeros((rank, stack.shape[1]), stack.dtype)
        pair = masked_products(info, ids, latent, stack, (3, 5, 7, None), rank)
        fold = pair[:, :rank] + pair[:, rank:]
        out[...] = earlier[...] + jnp.concatenate([jnp.zeros_like(fold), fold], axis=1)


def base_kernel(info, own, other, weight, *refs, skip):
    out, token = refs[-2:]
    token[...] = jnp.zeros_like(token)
    width = own.shape[1]
    mine = pl.ds(pl.multiple_of(info[0] * width, width), width)
    rest = pl.ds(pl.multiple_of((1 - info[0]) * width, width), width)
    step = min(CHUNK, out.shape[1])
    for begin in range(0, out.shape[1], step):
        place = slice(begin, min(begin + step, out.shape[1]))
        source = slice(skip + begin, skip + place.stop)
        out[:, place] = jnp.dot(
            own[...], weight[mine, source], preferred_element_type=jnp.float32
        ) + jnp.dot(other[...], weight[rest, source], preferred_element_type=jnp.float32)


def base(placed, latent, other, weight, after, skip, end):
    rows, columns = latent.shape[0], end - skip
    return pl.pallas_call(
        placed(base_kernel, skip=skip),
        out_shape=[jax.ShapeDtypeStruct((rows, columns), jnp.float32), TOKEN],
        in_specs=[VMEM, VMEM, VMEM] + [ANY] * len(after),
        out_specs=[VMEM, VMEM],
        compiler_params=pltpu.CompilerParams(vmem_limit_bytes=24 * MIB),
        cost_estimate=pl.CostEstimate(
            flops=1000,
            bytes_accessed=1000,
            transcendentals=0,
        ),
    )(latent, other, weight, *after)


def up_kernel(info, ids, mine, theirs, *refs, base_parts):
    *pieces, out, stack, wide, sems, staged = refs[base_parts:]
    bases = [
        part.at[:, pl.ds(begin, TILE)]
        for part in refs[:base_parts]
        for begin in range(0, part.shape[1], TILE)
    ]
    rank = mine.shape[1] // 2
    if len(pieces) == 1:
        stack[...] = pieces[0][...]
    else:
        own, beside, *received = pieces
        holds = info[1] == 0
        stack[0:rank, :] = own[...]
        stack[rank : 2 * rank, :] = beside[...]
        fill_here(info, holds, received, stack, 2 * rank, rank)
        fill_beside(info, holds, received, stack, 3 * rank, rank)
    lowrank = (mine[...] + theirs[...]).astype(jnp.bfloat16)
    zeros = jnp.zeros_like(lowrank)
    width = 2 * rank
    for lane in range(0, wide.shape[1], width):
        mask = ids[...] == owner_row(info, (lane // rank, lane // rank + 1), rank)
        wide[:, lane : lane + width] = jnp.where(mask, lowrank, zeros)
    copies = []
    tiles, _, tile = staged.shape
    for number in range(tiles):
        place = pl.ds(number * tile, tile)
        delta = jnp.dot(wide[...], stack[:, place], preferred_element_type=jnp.float32)
        total = bases[number][...] + delta.astype(jnp.bfloat16).astype(jnp.float32)
        staged[number] = total.astype(out.dtype)
        copies.append(
            pltpu.make_async_copy(staged.at[number], out.at[:, place], sems.at[number])
        )
        copies[-1].start()
    for copy in copies:
        copy.wait()


def on_device(latent, row_adapter_index, shared_weight, adapter_down_weight, adapter_up_weight):
    rows, half_width = latent.shape
    out_width = shared_weight.shape[1]
    local_adapters, _, rank = adapter_down_weight.shape
    shards = lax.axis_size("shard")
    adapters = shards * local_adapters
    columns = adapters * rank
    holds_down = lax.axis_index("tensor") == lax.axis_index("replica")
    tiles = out_width // TILE
    cuts = [0, out_width // 6, out_width // 2, out_width]
    down = jnp.swapaxes(adapter_down_weight, 1, 2).reshape(local_adapters * rank, half_width)
    up = adapter_up_weight.reshape(local_adapters * rank, out_width)
    row_ids = row_adapter_index.reshape(1, rows)
    routed = shards == 8 and local_adapters == 1 and lax.axis_size("replica") == 2
    routed = routed and half_width == out_width and tiles % 6 == 0
    lowrank = jax.ShapeDtypeStruct((rows, 2 * rank), jnp.float32)

    def placed(kernel, **options):
        def inner(*refs):
            return kernel(place_of_device(routed, shards, adapters), *refs, **options)

        return inner

    (token,) = call(prepare_kernel, [TOKEN], [VMEM], 16, moved=COPY)(shared_weight)
    down_out = [lowrank, jax.ShapeDtypeStruct((rows, 2 * rank), jnp.int32)]
    if routed:
        piece = jnp.where(holds_down, down, up)
        line = {1: along_line(piece, shards, 1)}
        other = swap(latent, "tensor")
        down_beside, up_beside = neighbour(down, shards), neighbour(up, shards)
        ready = token
        one, token = pack([(line[1], 0, rank)], token, down_beside, other)
        back, _ = pack([(piece, 0, rank)], ready)
        line[3] = along_line(back, shards, 3)
        line[2] = along_line(one, shards, 1)
        one_first, one_second = in_plane(one, shards, True), in_plane(one, shards, False)
        part_one, token = base(placed, latent, other, shared_weight, [token], cuts[0], cuts[1])
        three, token = pack([(line[3], 0, rank)], token)
        three_first, three_second = in_plane(three, shards, True), in_plane(three, shards, False)
        part_two, token = base(placed, latent, other, shared_weight, [token, up_beside], cuts[1], cuts[2])
        two, token = pack([(line[2], 0, rank)], token)
        two_second = in_plane(two, shards, False)
        turn, token = pack([(one_first, 0, rank)], token, one_second)
        corner_one = in_plane(turn, shards, False)
        two_first = along_line(turn, shards, 1)
        turn, token = pack([(three_second, 0, rank)], token, three_first)
        corner_three = in_plane(turn, shards, True)
        turn, token = pack([(two_second, 0, rank)], token)
        corner_two = in_plane(turn, shards, True)
        part_three, token = base(placed, latent, other, shared_weight, [token], cuts[2], cuts[3])
        parts = [part_one, part_two, part_three]
        corners = [corner_one, corner_three, corner_two]
        received = [one, three, two, one_first, three_first, two_first]
        received += [one_second, three_second, two_second]
        mine, ids = call(
            placed(down_first_kernel),
            down_out,
            [VMEM] * 13 + [ANY],
            16,
            [pltpu.VMEM((columns, half_width), latent.dtype)],
        )(row_ids, latent, down, down_beside, *received, token)
        mine = call(
            placed(down_last_kernel),
            lowrank,
            [VMEM] * 6,
            16,
            [pltpu.VMEM((4 * rank, half_width), latent.dtype)],
        )(ids, latent, mine, *corners)
        up_pieces = [up, up_beside, *received, *corners]
    else:
        other = swap(latent, "tensor")
        parts = []
        for begin, end in zip(cuts[:-1], cuts[1:]):
            part, token = base(placed, latent, other, shared_weight, [token], begin, end)
            parts.append(part)
        mine, ids = call(placed(down_whole_kernel), down_out, [VMEM] * 3, 48)(
            row_ids, latent, lax.all_gather(down, "shard", axis=0, tiled=True)
        )
        up_pieces = [lax.all_gather(up, "shard", axis=0, tiled=True)]
    theirs = swap(mine, "tensor")

    return pl.pallas_call(
        placed(up_kernel, base_parts=len(parts)),
        out_shape=jax.ShapeDtypeStruct((rows, out_width), latent.dtype),
        in_specs=[VMEM] * (3 + len(parts) + len(up_pieces)),
        out_specs=ANY,
        scratch_shapes=[
            pltpu.VMEM((columns, out_width), latent.dtype),
            pltpu.VMEM((rows, columns), latent.dtype),
            pltpu.SemaphoreType.DMA((tiles,)),
            pltpu.VMEM((tiles, rows, TILE), latent.dtype),
        ],
        compiler_params=pltpu.CompilerParams(vmem_limit_bytes=(24 if routed else 56) * MIB),
    )(ids, mine, theirs, *parts, *up_pieces)


def solution(mesh):
    return jax.shard_map(
        on_device,
        mesh=mesh,
        in_specs=(
            P(("replica", "shard"), "tensor"),
            P(("replica", "shard"), None),
            P(None, "tensor"),
            P("shard", "tensor", None),
            P("shard", None, "tensor"),
        ),
        out_specs=P(("replica", "shard"), "tensor"),
        check_vma=False,
    )
```

```python
import jax
import jax.numpy as jnp
import numpy as np
from jax import lax
from jax.experimental import pallas as pl
from jax.experimental.pallas import tpu as pltpu
from jax.sharding import PartitionSpec as P

MIB = 1024 * 1024
CHUNK = 512
TILE = 256
AXES = ("replica", "shard", "tensor")
FIRST_OWNER = 2
COPY = 0
VMEM = pl.BlockSpec(memory_space=pltpu.VMEM)
ANY = pl.BlockSpec(memory_space=pl.ANY)
TOKEN = jax.ShapeDtypeStruct((8, 128), jnp.float32)


def swap(value, axis):
    return lax.ppermute(value, axis, [(0, 1), (1, 0)])


def neighbour(value, shards):
    return lax.ppermute(value, "shard", [(i, i ^ 1) for i in range(shards)])


def ring_step(index, step):
    plane = index >> 1
    place = ((plane ^ (plane >> 1)) + step) & 3
    return ((place ^ (place >> 1)) << 1) | (index & 1)


def along_line(value, shards, step):
    return lax.ppermute(value, "shard", [(i, ring_step(i, step)) for i in range(shards)])


def in_plane(value, shards, first):
    pairs = []
    for r in range(2):
        for s in range(shards):
            for t in range(2):
                to_r, to_s = (r, s ^ 1) if (t == 0) == first else (r ^ 1, s)
                pairs.append(((r * shards + s) * 2 + t, (to_r * shards + to_s) * 2 + t))
    return lax.ppermute(value, AXES, pairs)


def call(kernel, out_shape, in_specs, limit, scratch=(), flops=0, moved=0):
    return pl.pallas_call(
        kernel,
        out_shape=out_shape,
        in_specs=in_specs,
        out_specs=jax.tree.map(lambda _: VMEM, out_shape),
        scratch_shapes=list(scratch),
        compiler_params=pltpu.CompilerParams(vmem_limit_bytes=limit * MIB),
        cost_estimate=pl.CostEstimate(flops=flops, bytes_accessed=moved, transcendentals=0),
    )


def place_of_device(routed, shards, adapters):
    core, index = lax.axis_index("tensor"), lax.axis_index("shard")
    holds_down = (core == lax.axis_index("replica")).astype(jnp.int32)
    owners = range(adapters)
    if routed:
        sources = [ring_step(index, -step) for step in (0, 1, 3, 2)]
        owners = [a for source in sources for a in (source, source ^ 1)]
    return [core, holds_down, *owners]


def owner_row(info, blocks, rank):
    place = lax.broadcasted_iota(jnp.int32, (1, len(blocks) * rank), 1) // rank
    row = jnp.full(place.shape, -1, jnp.int32)
    for number, block in enumerate(blocks):
        if block is not None:
            row = jnp.where(place == number, info[FIRST_OWNER + block], row)
    return row


def pack(pieces, *after, tokens=1):
    count = len(pieces)
    total = sum(rows for _, _, rows in pieces)
    width, dtype = pieces[0][0].shape[1], pieces[0][0].dtype

    def kernel(*refs):
        out = refs[count + len(after)]
        top = 0
        for ref, (_, begin, rows) in zip(refs, pieces):
            out[top : top + rows, :] = ref[begin : begin + rows, :]
            top += rows
        for token in refs[count + len(after) + 1 :]:
            token[...] = jnp.zeros_like(token)

    return call(
        kernel,
        [jax.ShapeDtypeStruct((total, width), dtype)] + [TOKEN] * tokens,
        [VMEM] * count + [ANY] * len(after),
        4,
        moved=COPY,
    )(*[array for array, _, _ in pieces], *after)


def put(blocks, stack, top, rank):
    for number, block in enumerate(blocks):
        place = top + 2 * number * rank
        stack[place : place + rank, :] = block[...]


def fill_here(info, holds, received, stack, top, rank):
    here, first, second = received[0:3], received[3:6], received[6:9]
    pl.when(holds)(lambda: put(here, stack, top, rank))
    for core, refs in enumerate((second, first)):
        away = jnp.logical_not(holds) & (info[0] == core)
        pl.when(away)(lambda refs=refs: put(refs, stack, top, rank))


def fill_beside(info, holds, received, stack, top, rank, direct=True, corner=True):
    if direct:
        for core, refs in enumerate((received[3:6], received[6:9])):
            pl.when(holds & (info[0] == core))(lambda refs=refs: put(refs, stack, top, rank))
    if corner:
        corners = received[9:12]
        pl.when(jnp.logical_not(holds))(lambda: put(corners, stack, top, rank))


def clear(stack, top, rank, count):
    for number in range(count):
        place = top + 2 * number * rank
        stack[place : place + rank, :] = jnp.zeros((rank, stack.shape[1]), stack.dtype)


def prepare_kernel(weight, *refs):
    refs[-1][...] = weight[0:8, 0:128].astype(jnp.float32)


def spread_rows(row_ids):
    wide = jnp.broadcast_to(row_ids[...].astype(jnp.float32), (128, row_ids.shape[1]))
    return wide.T.astype(jnp.int32)


def masked_products(info, ids, latent, stack, blocks, rank):
    total = None
    width = 2 * rank
    for skip in range(0, stack.shape[0], CHUNK):
        count = min(CHUNK, stack.shape[0] - skip)
        part = lax.dot_general(
            latent[...],
            stack[skip : skip + count, :],
            (((1,), (1,)), ((), ())),
            preferred_element_type=jnp.float32,
        )
        owners = owner_row(info, blocks[skip // rank : (skip + count) // rank], rank)
        for lane in range(0, count, width):
            lanes = slice(lane, lane + width)
            fold = jnp.where(ids[...] == owners[:, lanes], part[:, lanes], 0.0)
            total = fold if total is None else total + fold
    return total


def down_whole_kernel(info, row_ids, latent, stack, out, ids):
    ids[...] = spread_rows(row_ids)
    rank = out.shape[1] // 2
    blocks = range(stack.shape[0] // rank)
    out[...] = masked_products(info, ids, latent, stack, blocks, rank)


def down_first_kernel(info, row_ids, latent, own, beside, *refs):
    *received, _, out, ids, stack = refs
    ids[...] = spread_rows(row_ids)
    rank = own.shape[0]
    holds = info[1] == 1
    stack[0:rank, :] = own[...]
    stack[rank : 2 * rank, :] = beside[...]
    fill_here(info, holds, received, stack, 2 * rank, rank)
    fill_beside(info, holds, received, stack, 3 * rank, rank, corner=False)
    pl.when(jnp.logical_not(holds))(lambda: clear(stack, 3 * rank, rank, 3))
    out[...] = masked_products(info, ids, latent, stack, range(stack.shape[0] // rank), rank)


def down_last_kernel(info, ids, latent, earlier, *refs):
    *corners, out, stack = refs
    rank = out.shape[1] // 2
    holds = info[1] == 1

    @pl.when(holds)
    def _():
        out[...] = earlier[...]

    @pl.when(jnp.logical_not(holds))
    def _():
        for number, corner in enumerate(corners):
            stack[number * rank : (number + 1) * rank, :] = corner[...]
        stack[3 * rank : 4 * rank, :] = jnp.zeros((rank, stack.shape[1]), stack.dtype)
        pair = masked_products(info, ids, latent, stack, (3, 5, 7, None), rank)
        fold = pair[:, :rank] + pair[:, rank:]
        out[...] = earlier[...] + jnp.concatenate([jnp.zeros_like(fold), fold], axis=1)


def base_kernel(info, own, other, weight, *refs, skip):
    out, token = refs[-2:]
    token[...] = jnp.zeros_like(token)
    width = own.shape[1]
    mine = pl.ds(pl.multiple_of(info[0] * width, width), width)
    rest = pl.ds(pl.multiple_of((1 - info[0]) * width, width), width)
    step = min(CHUNK, out.shape[1])
    for begin in range(0, out.shape[1], step):
        place = slice(begin, min(begin + step, out.shape[1]))
        source = slice(skip + begin, skip + place.stop)
        out[:, place] = jnp.dot(
            own[...], weight[mine, source], preferred_element_type=jnp.float32
        ) + jnp.dot(other[...], weight[rest, source], preferred_element_type=jnp.float32)


def base(placed, latent, other, weight, after, skip, end):
    rows, columns = latent.shape[0], end - skip
    return pl.pallas_call(
        placed(base_kernel, skip=skip),
        out_shape=[jax.ShapeDtypeStruct((rows, columns), jnp.float32), TOKEN],
        in_specs=[VMEM, VMEM, VMEM] + [ANY] * len(after),
        out_specs=[VMEM, VMEM],
        compiler_params=pltpu.CompilerParams(vmem_limit_bytes=24 * MIB),
        cost_estimate=pl.CostEstimate(
            flops=1000,
            bytes_accessed=1000,
            transcendentals=0,
        ),
    )(latent, other, weight, *after)


def up_kernel(info, ids, mine, theirs, *refs, base_parts):
    *pieces, out, stack, wide, sems, staged = refs[base_parts:]
    bases = [
        part.at[:, pl.ds(begin, TILE)]
        for part in refs[:base_parts]
        for begin in range(0, part.shape[1], TILE)
    ]
    rank = mine.shape[1] // 2
    if len(pieces) == 1:
        stack[...] = pieces[0][...]
    else:
        own, beside, *received = pieces
        holds = info[1] == 0
        stack[0:rank, :] = own[...]
        stack[rank : 2 * rank, :] = beside[...]
        fill_here(info, holds, received, stack, 2 * rank, rank)
        fill_beside(info, holds, received, stack, 3 * rank, rank)
    lowrank = (mine[...] + theirs[...]).astype(jnp.bfloat16)
    zeros = jnp.zeros_like(lowrank)
    width = 2 * rank
    for lane in range(0, wide.shape[1], width):
        mask = ids[...] == owner_row(info, (lane // rank, lane // rank + 1), rank)
        wide[:, lane : lane + width] = jnp.where(mask, lowrank, zeros)
    copies = []
    tiles, _, tile = staged.shape
    for number in range(tiles):
        place = pl.ds(number * tile, tile)
        delta = jnp.dot(wide[...], stack[:, place], preferred_element_type=jnp.float32)
        total = bases[number][...] + delta.astype(jnp.bfloat16).astype(jnp.float32)
        staged[number] = total.astype(out.dtype)
        copies.append(
            pltpu.make_async_copy(staged.at[number], out.at[:, place], sems.at[number])
        )
        copies[-1].start()
    for copy in copies:
        copy.wait()


def on_device(latent, row_adapter_index, shared_weight, adapter_down_weight, adapter_up_weight):
    rows, half_width = latent.shape
    out_width = shared_weight.shape[1]
    local_adapters, _, rank = adapter_down_weight.shape
    shards = lax.axis_size("shard")
    adapters = shards * local_adapters
    columns = adapters * rank
    holds_down = lax.axis_index("tensor") == lax.axis_index("replica")
    tiles = out_width // TILE
    cuts = [0, out_width // 6, out_width // 2, out_width]
    down = jnp.swapaxes(adapter_down_weight, 1, 2).reshape(local_adapters * rank, half_width)
    up = adapter_up_weight.reshape(local_adapters * rank, out_width)
    row_ids = row_adapter_index.reshape(1, rows)
    routed = shards == 8 and local_adapters == 1 and lax.axis_size("replica") == 2
    routed = routed and half_width == out_width and tiles % 6 == 0
    lowrank = jax.ShapeDtypeStruct((rows, 2 * rank), jnp.float32)

    def placed(kernel, **options):
        def inner(*refs):
            return kernel(place_of_device(routed, shards, adapters), *refs, **options)

        return inner

    (token,) = call(prepare_kernel, [TOKEN], [VMEM], 16, moved=COPY)(shared_weight)
    down_out = [lowrank, jax.ShapeDtypeStruct((rows, 2 * rank), jnp.int32)]
    if routed:
        piece = jnp.where(holds_down, down, up)
        line = {1: along_line(piece, shards, 1)}
        other = swap(latent, "tensor")
        down_beside, up_beside = neighbour(down, shards), neighbour(up, shards)
        ready = token
        one, token = pack([(line[1], 0, rank)], token, down_beside, other)
        (back,) = pack([(piece, 0, rank)], ready, tokens=0)
        line[3] = along_line(back, shards, 3)
        line[2] = along_line(one, shards, 1)
        one_first, one_second = in_plane(one, shards, True), in_plane(one, shards, False)
        part_one, token = base(placed, latent, other, shared_weight, [token], cuts[0], cuts[1])
        three, token = pack([(line[3], 0, rank)], token)
        three_first, three_second = in_plane(three, shards, True), in_plane(three, shards, False)
        part_two, token = base(placed, latent, other, shared_weight, [token, up_beside], cuts[1], cuts[2])
        two, token = pack([(line[2], 0, rank)], token)
        two_second = in_plane(two, shards, False)
        turn, token = pack([(one_first, 0, rank)], token, one_second)
        corner_one = in_plane(turn, shards, False)
        two_first = along_line(turn, shards, 1)
        turn, token = pack([(three_second, 0, rank)], token, three_first)
        corner_three = in_plane(turn, shards, True)
        turn, token = pack([(two_second, 0, rank)], token)
        corner_two = in_plane(turn, shards, True)
        part_three, token = base(placed, latent, other, shared_weight, [token], cuts[2], cuts[3])
        parts = [part_one, part_two, part_three]
        corners = [corner_one, corner_three, corner_two]
        received = [one, three, two, one_first, three_first, two_first]
        received += [one_second, three_second, two_second]
        mine, ids = call(
            placed(down_first_kernel),
            down_out,
            [VMEM] * 13 + [ANY],
            16,
            [pltpu.VMEM((columns, half_width), latent.dtype)],
        )(row_ids, latent, down, down_beside, *received, token)
        mine = call(
            placed(down_last_kernel),
            lowrank,
            [VMEM] * 6,
            16,
            [pltpu.VMEM((4 * rank, half_width), latent.dtype)],
        )(ids, latent, mine, *corners)
        up_pieces = [up, up_beside, *received, *corners]
    else:
        other = swap(latent, "tensor")
        parts = []
        for begin, end in zip(cuts[:-1], cuts[1:]):
            part, token = base(placed, latent, other, shared_weight, [token], begin, end)
            parts.append(part)
        mine, ids = call(placed(down_whole_kernel), down_out, [VMEM] * 3, 48)(
            row_ids, latent, lax.all_gather(down, "shard", axis=0, tiled=True)
        )
        up_pieces = [lax.all_gather(up, "shard", axis=0, tiled=True)]
    theirs = swap(mine, "tensor")

    return pl.pallas_call(
        placed(up_kernel, base_parts=len(parts)),
        out_shape=jax.ShapeDtypeStruct((rows, out_width), latent.dtype),
        in_specs=[VMEM] * (3 + len(parts) + len(up_pieces)),
        out_specs=ANY,
        scratch_shapes=[
            pltpu.VMEM((columns, out_width), latent.dtype),
            pltpu.VMEM((rows, columns), latent.dtype),
            pltpu.SemaphoreType.DMA((tiles,)),
            pltpu.VMEM((tiles, rows, TILE), latent.dtype),
        ],
        compiler_params=pltpu.CompilerParams(vmem_limit_bytes=(24 if routed else 56) * MIB),
    )(ids, mine, theirs, *parts, *up_pieces)


def solution(mesh):
    return jax.shard_map(
        on_device,
        mesh=mesh,
        in_specs=(
            P(("replica", "shard"), "tensor"),
            P(("replica", "shard"), None),
            P(None, "tensor"),
            P("shard", "tensor", None),
            P("shard", None, "tensor"),
        ),
        out_specs=P(("replica", "shard"), "tensor"),
        check_vma=False,
    )
```

```python
import jax
import jax.numpy as jnp
import numpy as np
from jax import lax
from jax.experimental import pallas as pl
from jax.experimental.pallas import tpu as pltpu
from jax.sharding import PartitionSpec as P

MIB = 1024 * 1024
CHUNK = 512
TILE = 256
AXES = ("replica", "shard", "tensor")
FIRST_OWNER = 2
COPY = 0
VMEM = pl.BlockSpec(memory_space=pltpu.VMEM)
ANY = pl.BlockSpec(memory_space=pl.ANY)
TOKEN = jax.ShapeDtypeStruct((8, 128), jnp.float32)


def swap(value, axis):
    return lax.ppermute(value, axis, [(0, 1), (1, 0)])


def neighbour(value, shards):
    return lax.ppermute(value, "shard", [(i, i ^ 1) for i in range(shards)])


def ring_step(index, step):
    plane = index >> 1
    place = ((plane ^ (plane >> 1)) + step) & 3
    return ((place ^ (place >> 1)) << 1) | (index & 1)


def along_line(value, shards, step):
    return lax.ppermute(value, "shard", [(i, ring_step(i, step)) for i in range(shards)])


def in_plane(value, shards, first):
    pairs = []
    for r in range(2):
        for s in range(shards):
            for t in range(2):
                to_r, to_s = (r, s ^ 1) if (t == 0) == first else (r ^ 1, s)
                pairs.append(((r * shards + s) * 2 + t, (to_r * shards + to_s) * 2 + t))
    return lax.ppermute(value, AXES, pairs)


def call(kernel, out_shape, in_specs, limit, scratch=(), flops=0, moved=0):
    return pl.pallas_call(
        kernel,
        out_shape=out_shape,
        in_specs=in_specs,
        out_specs=jax.tree.map(lambda _: VMEM, out_shape),
        scratch_shapes=list(scratch),
        compiler_params=pltpu.CompilerParams(vmem_limit_bytes=limit * MIB),
        cost_estimate=pl.CostEstimate(flops=flops, bytes_accessed=moved, transcendentals=0),
    )


def place_of_device(routed, shards, adapters):
    core, index = lax.axis_index("tensor"), lax.axis_index("shard")
    holds_down = (core == lax.axis_index("replica")).astype(jnp.int32)
    owners = range(adapters)
    if routed:
        sources = [ring_step(index, -step) for step in (0, 1, 3, 2)]
        owners = [a for source in sources for a in (source, source ^ 1)]
    return [core, holds_down, *owners]


def owner_row(info, blocks, rank):
    place = lax.broadcasted_iota(jnp.int32, (1, len(blocks) * rank), 1) // rank
    row = jnp.full(place.shape, -1, jnp.int32)
    for number, block in enumerate(blocks):
        if block is not None:
            row = jnp.where(place == number, info[FIRST_OWNER + block], row)
    return row


def pack(pieces, *after):
    count = len(pieces)
    total = sum(rows for _, _, rows in pieces)
    width, dtype = pieces[0][0].shape[1], pieces[0][0].dtype

    def kernel(*refs):
        out, token = refs[-2:]
        top = 0
        for ref, (_, begin, rows) in zip(refs, pieces):
            out[top : top + rows, :] = ref[begin : begin + rows, :]
            top += rows
        token[...] = jnp.zeros_like(token)

    return call(
        kernel,
        [jax.ShapeDtypeStruct((total, width), dtype), TOKEN],
        [VMEM] * count + [ANY] * len(after),
        4,
        moved=COPY,
    )(*[array for array, _, _ in pieces], *after)


def put(blocks, stack, top, rank):
    for number, block in enumerate(blocks):
        place = top + 2 * number * rank
        stack[place : place + rank, :] = block[...]


def fill_here(info, holds, received, stack, top, rank):
    here, first, second = received[0:3], received[3:6], received[6:9]
    pl.when(holds)(lambda: put(here, stack, top, rank))
    for core, refs in enumerate((second, first)):
        away = jnp.logical_not(holds) & (info[0] == core)
        pl.when(away)(lambda refs=refs: put(refs, stack, top, rank))


def fill_beside(info, holds, received, stack, top, rank, direct=True, corner=True):
    if direct:
        for core, refs in enumerate((received[3:6], received[6:9])):
            pl.when(holds & (info[0] == core))(lambda refs=refs: put(refs, stack, top, rank))
    if corner:
        corners = received[9:12]
        pl.when(jnp.logical_not(holds))(lambda: put(corners, stack, top, rank))


def clear(stack, top, rank, count):
    for number in range(count):
        place = top + 2 * number * rank
        stack[place : place + rank, :] = jnp.zeros((rank, stack.shape[1]), stack.dtype)


def prepare_kernel(weight, *refs):
    refs[-1][...] = weight[0:8, 0:128].astype(jnp.float32)


def spread_rows(row_ids):
    wide = jnp.broadcast_to(row_ids[...].astype(jnp.float32), (128, row_ids.shape[1]))
    return wide.T.astype(jnp.int32)


def masked_products(info, ids, latent, stack, blocks, rank):
    total = None
    width = 2 * rank
    for skip in range(0, stack.shape[0], CHUNK):
        count = min(CHUNK, stack.shape[0] - skip)
        part = lax.dot_general(
            latent[...],
            stack[skip : skip + count, :],
            (((1,), (1,)), ((), ())),
            preferred_element_type=jnp.float32,
        )
        owners = owner_row(info, blocks[skip // rank : (skip + count) // rank], rank)
        for lane in range(0, count, width):
            lanes = slice(lane, lane + width)
            fold = jnp.where(ids[...] == owners[:, lanes], part[:, lanes], 0.0)
            total = fold if total is None else total + fold
    return total


def down_whole_kernel(info, row_ids, latent, stack, out, ids):
    ids[...] = spread_rows(row_ids)
    rank = out.shape[1] // 2
    blocks = range(stack.shape[0] // rank)
    out[...] = masked_products(info, ids, latent, stack, blocks, rank)


def down_first_kernel(info, row_ids, latent, own, beside, *refs):
    *received, _, out, ids, stack = refs
    ids[...] = spread_rows(row_ids)
    rank = own.shape[0]
    holds = info[1] == 1
    stack[0:rank, :] = own[...]
    stack[rank : 2 * rank, :] = beside[...]
    fill_here(info, holds, received, stack, 2 * rank, rank)
    fill_beside(info, holds, received, stack, 3 * rank, rank, corner=False)
    pl.when(jnp.logical_not(holds))(lambda: clear(stack, 3 * rank, rank, 3))
    out[...] = masked_products(info, ids, latent, stack, range(stack.shape[0] // rank), rank)


def down_last_kernel(info, ids, latent, earlier, *refs):
    *corners, out, stack = refs
    rank = out.shape[1] // 2
    holds = info[1] == 1

    @pl.when(holds)
    def _():
        out[...] = earlier[...]

    @pl.when(jnp.logical_not(holds))
    def _():
        for number, corner in enumerate(corners):
            stack[number * rank : (number + 1) * rank, :] = corner[...]
        stack[3 * rank : 4 * rank, :] = jnp.zeros((rank, stack.shape[1]), stack.dtype)
        pair = masked_products(info, ids, latent, stack, (3, 5, 7, None), rank)
        fold = pair[:, :rank] + pair[:, rank:]
        out[...] = earlier[...] + jnp.concatenate([jnp.zeros_like(fold), fold], axis=1)


def base_kernel(info, own, other, weight, *refs, skip):
    out, token = refs[-2:]
    token[...] = jnp.zeros_like(token)
    width = own.shape[1]
    mine = pl.ds(pl.multiple_of(info[0] * width, width), width)
    rest = pl.ds(pl.multiple_of((1 - info[0]) * width, width), width)
    step = min(CHUNK, out.shape[1])
    for begin in range(0, out.shape[1], step):
        place = slice(begin, min(begin + step, out.shape[1]))
        source = slice(skip + begin, skip + place.stop)
        out[:, place] = jnp.dot(
            own[...], weight[mine, source], preferred_element_type=jnp.float32
        ) + jnp.dot(other[...], weight[rest, source], preferred_element_type=jnp.float32)


def base(placed, latent, other, weight, after, skip, end):
    rows, columns = latent.shape[0], end - skip
    return pl.pallas_call(
        placed(base_kernel, skip=skip),
        out_shape=[jax.ShapeDtypeStruct((rows, columns), jnp.float32), TOKEN],
        in_specs=[VMEM, VMEM, VMEM] + [ANY] * len(after),
        out_specs=[VMEM, VMEM],
        compiler_params=pltpu.CompilerParams(vmem_limit_bytes=24 * MIB),
        cost_estimate=pl.CostEstimate(
            flops=1000,
            bytes_accessed=1000,
            transcendentals=0,
        ),
    )(latent, other, weight, *after)


def up_kernel(info, ids, mine, theirs, *refs, base_parts):
    *pieces, out, stack, wide, sems, staged = refs[base_parts:]
    bases = [
        part.at[:, pl.ds(begin, TILE)]
        for part in refs[:base_parts]
        for begin in range(0, part.shape[1], TILE)
    ]
    rank = mine.shape[1] // 2
    if len(pieces) == 1:
        stack[...] = pieces[0][...]
    else:
        own, beside, *received = pieces
        holds = info[1] == 0
        stack[0:rank, :] = own[...]
        stack[rank : 2 * rank, :] = beside[...]
        fill_here(info, holds, received, stack, 2 * rank, rank)
        fill_beside(info, holds, received, stack, 3 * rank, rank)
    lowrank = (mine[...] + theirs[...]).astype(jnp.bfloat16)
    zeros = jnp.zeros_like(lowrank)
    width = 2 * rank
    for lane in range(0, wide.shape[1], width):
        mask = ids[...] == owner_row(info, (lane // rank, lane // rank + 1), rank)
        wide[:, lane : lane + width] = jnp.where(mask, lowrank, zeros)
    copies = []
    tiles, _, tile = staged.shape
    for number in range(tiles):
        place = pl.ds(number * tile, tile)
        delta = jnp.dot(wide[...], stack[:, place], preferred_element_type=jnp.float32)
        total = bases[number][...] + delta.astype(jnp.bfloat16).astype(jnp.float32)
        staged[number] = total.astype(out.dtype)
        copies.append(
            pltpu.make_async_copy(staged.at[number], out.at[:, place], sems.at[number])
        )
        copies[-1].start()
    for copy in copies:
        copy.wait()


def on_device(latent, row_adapter_index, shared_weight, adapter_down_weight, adapter_up_weight):
    rows, half_width = latent.shape
    out_width = shared_weight.shape[1]
    local_adapters, _, rank = adapter_down_weight.shape
    shards = lax.axis_size("shard")
    adapters = shards * local_adapters
    columns = adapters * rank
    holds_down = lax.axis_index("tensor") == lax.axis_index("replica")
    tiles = out_width // TILE
    cuts = [0, out_width // 6, out_width // 2, out_width]
    down = jnp.swapaxes(adapter_down_weight, 1, 2).reshape(local_adapters * rank, half_width)
    up = adapter_up_weight.reshape(local_adapters * rank, out_width)
    row_ids = row_adapter_index.reshape(1, rows)
    routed = shards == 8 and local_adapters == 1 and lax.axis_size("replica") == 2
    routed = routed and half_width == out_width and tiles % 6 == 0
    lowrank = jax.ShapeDtypeStruct((rows, 2 * rank), jnp.float32)

    def placed(kernel, **options):
        def inner(*refs):
            return kernel(place_of_device(routed, shards, adapters), *refs, **options)

        return inner

    (token,) = call(prepare_kernel, [TOKEN], [VMEM], 16, moved=COPY)(shared_weight)
    down_out = [lowrank, jax.ShapeDtypeStruct((rows, 2 * rank), jnp.int32)]
    if routed:
        piece = jnp.where(holds_down, down, up)
        line = {1: along_line(piece, shards, 1)}
        other = swap(latent, "tensor")
        down_beside, up_beside = neighbour(down, shards), neighbour(up, shards)
        ready = token
        one, token = pack([(line[1], 0, rank)], token, down_beside, other)
        back, _ = pack([(piece, 0, rank)], ready)
        line[3] = along_line(back, shards, 3)
        line[2] = along_line(one, shards, 1)
        one_first, one_second = in_plane(one, shards, True), in_plane(one, shards, False)
        part_one, token = base(placed, latent, other, shared_weight, [token], cuts[0], cuts[1])
        three, token = pack([(line[3], 0, rank)], token)
        three_first, three_second = in_plane(three, shards, True), in_plane(three, shards, False)
        part_two, token = base(placed, latent, other, shared_weight, [token, up_beside], cuts[1], cuts[2])
        turn, token = pack([(one_first, 0, rank)], token, one_second)
        corner_one = in_plane(turn, shards, False)
        two_first = along_line(turn, shards, 1)
        two, token = pack([(line[2], 0, rank)], token)
        two_second = in_plane(two, shards, False)
        turn, token = pack([(three_second, 0, rank)], token, three_first)
        corner_three = in_plane(turn, shards, True)
        turn, token = pack([(two_second, 0, rank)], token)
        corner_two = in_plane(turn, shards, True)
        part_three, token = base(placed, latent, other, shared_weight, [token], cuts[2], cuts[3])
        parts = [part_one, part_two, part_three]
        corners = [corner_one, corner_three, corner_two]
        received = [one, three, two, one_first, three_first, two_first]
        received += [one_second, three_second, two_second]
        mine, ids = call(
            placed(down_first_kernel),
            down_out,
            [VMEM] * 13 + [ANY],
            16,
            [pltpu.VMEM((columns, half_width), latent.dtype)],
        )(row_ids, latent, down, down_beside, *received, token)
        mine = call(
            placed(down_last_kernel),
            lowrank,
            [VMEM] * 6,
            16,
            [pltpu.VMEM((4 * rank, half_width), latent.dtype)],
        )(ids, latent, mine, *corners)
        up_pieces = [up, up_beside, *received, *corners]
    else:
        other = swap(latent, "tensor")
        parts = []
        for begin, end in zip(cuts[:-1], cuts[1:]):
            part, token = base(placed, latent, other, shared_weight, [token], begin, end)
            parts.append(part)
        mine, ids = call(placed(down_whole_kernel), down_out, [VMEM] * 3, 48)(
            row_ids, latent, lax.all_gather(down, "shard", axis=0, tiled=True)
        )
        up_pieces = [lax.all_gather(up, "shard", axis=0, tiled=True)]
    theirs = swap(mine, "tensor")

    return pl.pallas_call(
        placed(up_kernel, base_parts=len(parts)),
        out_shape=jax.ShapeDtypeStruct((rows, out_width), latent.dtype),
        in_specs=[VMEM] * (3 + len(parts) + len(up_pieces)),
        out_specs=ANY,
        scratch_shapes=[
            pltpu.VMEM((columns, out_width), latent.dtype),
            pltpu.VMEM((rows, columns), latent.dtype),
            pltpu.SemaphoreType.DMA((tiles,)),
            pltpu.VMEM((tiles, rows, TILE), latent.dtype),
        ],
        compiler_params=pltpu.CompilerParams(vmem_limit_bytes=(24 if routed else 56) * MIB),
    )(ids, mine, theirs, *parts, *up_pieces)


def solution(mesh):
    return jax.shard_map(
        on_device,
        mesh=mesh,
        in_specs=(
            P(("replica", "shard"), "tensor"),
            P(("replica", "shard"), None),
            P(None, "tensor"),
            P("shard", "tensor", None),
            P("shard", None, "tensor"),
        ),
        out_specs=P(("replica", "shard"), "tensor"),
        check_vma=False,
    )
```

```python
import jax
import jax.numpy as jnp
import numpy as np
from jax import lax
from jax.experimental import pallas as pl
from jax.experimental.pallas import tpu as pltpu
from jax.sharding import PartitionSpec as P

MIB = 1024 * 1024
CHUNK = 512
TILE = 256
AXES = ("replica", "shard", "tensor")
FIRST_OWNER = 2
COPY = 0
VMEM = pl.BlockSpec(memory_space=pltpu.VMEM)
ANY = pl.BlockSpec(memory_space=pl.ANY)
TOKEN = jax.ShapeDtypeStruct((8, 128), jnp.float32)


def swap(value, axis):
    return lax.ppermute(value, axis, [(0, 1), (1, 0)])


def neighbour(value, shards):
    return lax.ppermute(value, "shard", [(i, i ^ 1) for i in range(shards)])


def ring_step(index, step):
    plane = index >> 1
    place = ((plane ^ (plane >> 1)) + step) & 3
    return ((place ^ (place >> 1)) << 1) | (index & 1)


def along_line(value, shards, step):
    return lax.ppermute(value, "shard", [(i, ring_step(i, step)) for i in range(shards)])


def in_plane(value, shards, first):
    pairs = []
    for r in range(2):
        for s in range(shards):
            for t in range(2):
                to_r, to_s = (r, s ^ 1) if (t == 0) == first else (r ^ 1, s)
                pairs.append(((r * shards + s) * 2 + t, (to_r * shards + to_s) * 2 + t))
    return lax.ppermute(value, AXES, pairs)


def call(kernel, out_shape, in_specs, limit, scratch=(), flops=0, moved=0):
    return pl.pallas_call(
        kernel,
        out_shape=out_shape,
        in_specs=in_specs,
        out_specs=jax.tree.map(lambda _: VMEM, out_shape),
        scratch_shapes=list(scratch),
        compiler_params=pltpu.CompilerParams(vmem_limit_bytes=limit * MIB),
        cost_estimate=pl.CostEstimate(flops=flops, bytes_accessed=moved, transcendentals=0),
    )


def place_of_device(routed, shards, adapters):
    core, index = lax.axis_index("tensor"), lax.axis_index("shard")
    holds_down = (core == lax.axis_index("replica")).astype(jnp.int32)
    owners = range(adapters)
    if routed:
        sources = [ring_step(index, -step) for step in (0, 1, 3, 2)]
        owners = [a for source in sources for a in (source, source ^ 1)]
    return [core, holds_down, *owners]


def owner_row(info, blocks, rank):
    place = lax.broadcasted_iota(jnp.int32, (1, len(blocks) * rank), 1) // rank
    row = jnp.full(place.shape, -1, jnp.int32)
    for number, block in enumerate(blocks):
        if block is not None:
            row = jnp.where(place == number, info[FIRST_OWNER + block], row)
    return row


def pack(pieces, *after, tokens=1):
    count = len(pieces)
    total = sum(rows for _, _, rows in pieces)
    width, dtype = pieces[0][0].shape[1], pieces[0][0].dtype

    def kernel(*refs):
        out = refs[count + len(after)]
        top = 0
        for ref, (_, begin, rows) in zip(refs, pieces):
            out[top : top + rows, :] = ref[begin : begin + rows, :]
            top += rows
        for token in refs[count + len(after) + 1 :]:
            token[...] = jnp.zeros_like(token)

    return call(
        kernel,
        [jax.ShapeDtypeStruct((total, width), dtype)] + [TOKEN] * tokens,
        [VMEM] * count + [ANY] * len(after),
        4,
        moved=COPY,
    )(*[array for array, _, _ in pieces], *after)


def put(blocks, stack, top, rank):
    for number, block in enumerate(blocks):
        place = top + 2 * number * rank
        stack[place : place + rank, :] = block[...]


def fill_here(info, holds, received, stack, top, rank):
    here, first, second = received[0:3], received[3:6], received[6:9]
    pl.when(holds)(lambda: put(here, stack, top, rank))
    for core, refs in enumerate((second, first)):
        away = jnp.logical_not(holds) & (info[0] == core)
        pl.when(away)(lambda refs=refs: put(refs, stack, top, rank))


def fill_beside(info, holds, received, stack, top, rank, direct=True, corner=True):
    if direct:
        for core, refs in enumerate((received[3:6], received[6:9])):
            pl.when(holds & (info[0] == core))(lambda refs=refs: put(refs, stack, top, rank))
    if corner:
        corners = received[9:12]
        pl.when(jnp.logical_not(holds))(lambda: put(corners, stack, top, rank))


def clear(stack, top, rank, count):
    for number in range(count):
        place = top + 2 * number * rank
        stack[place : place + rank, :] = jnp.zeros((rank, stack.shape[1]), stack.dtype)


def prepare_kernel(weight, *refs):
    refs[-1][...] = weight[0:8, 0:128].astype(jnp.float32)


def spread_rows(row_ids):
    wide = jnp.broadcast_to(row_ids[...].astype(jnp.float32), (128, row_ids.shape[1]))
    return wide.T.astype(jnp.int32)


def masked_products(info, ids, latent, stack, blocks, rank):
    total = None
    width = 2 * rank
    for skip in range(0, stack.shape[0], CHUNK):
        count = min(CHUNK, stack.shape[0] - skip)
        part = lax.dot_general(
            latent[...],
            stack[skip : skip + count, :],
            (((1,), (1,)), ((), ())),
            preferred_element_type=jnp.float32,
        )
        owners = owner_row(info, blocks[skip // rank : (skip + count) // rank], rank)
        for lane in range(0, count, width):
            lanes = slice(lane, lane + width)
            fold = jnp.where(ids[...] == owners[:, lanes], part[:, lanes], 0.0)
            total = fold if total is None else total + fold
    return total


def down_whole_kernel(info, row_ids, latent, stack, out, ids):
    ids[...] = spread_rows(row_ids)
    rank = out.shape[1] // 2
    blocks = range(stack.shape[0] // rank)
    out[...] = masked_products(info, ids, latent, stack, blocks, rank)


def down_first_kernel(info, row_ids, latent, own, beside, *refs):
    *received, _, out, ids, stack = refs
    ids[...] = spread_rows(row_ids)
    rank = own.shape[0]
    holds = info[1] == 1
    stack[0:rank, :] = own[...]
    stack[rank : 2 * rank, :] = beside[...]
    fill_here(info, holds, received, stack, 2 * rank, rank)
    fill_beside(info, holds, received, stack, 3 * rank, rank, corner=False)
    pl.when(jnp.logical_not(holds))(lambda: clear(stack, 3 * rank, rank, 3))
    out[...] = masked_products(info, ids, latent, stack, range(stack.shape[0] // rank), rank)


def down_last_kernel(info, ids, latent, earlier, *refs):
    *corners, out, stack = refs
    rank = out.shape[1] // 2
    holds = info[1] == 1

    @pl.when(holds)
    def _():
        out[...] = earlier[...]

    @pl.when(jnp.logical_not(holds))
    def _():
        for number, corner in enumerate(corners):
            stack[number * rank : (number + 1) * rank, :] = corner[...]
        stack[3 * rank : 4 * rank, :] = jnp.zeros((rank, stack.shape[1]), stack.dtype)
        pair = masked_products(info, ids, latent, stack, (3, 5, 7, None), rank)
        fold = pair[:, :rank] + pair[:, rank:]
        out[...] = earlier[...] + jnp.concatenate([jnp.zeros_like(fold), fold], axis=1)


def base_kernel(info, own, other, weight, *refs, skip):
    out, token = refs[-2:]
    token[...] = jnp.zeros_like(token)
    width = own.shape[1]
    mine = pl.ds(pl.multiple_of(info[0] * width, width), width)
    rest = pl.ds(pl.multiple_of((1 - info[0]) * width, width), width)
    step = min(CHUNK, out.shape[1])
    for begin in range(0, out.shape[1], step):
        place = slice(begin, min(begin + step, out.shape[1]))
        source = slice(skip + begin, skip + place.stop)
        out[:, place] = jnp.dot(
            own[...], weight[mine, source], preferred_element_type=jnp.float32
        ) + jnp.dot(other[...], weight[rest, source], preferred_element_type=jnp.float32)


def base(placed, latent, other, weight, after, skip, end):
    rows, columns = latent.shape[0], end - skip
    return pl.pallas_call(
        placed(base_kernel, skip=skip),
        out_shape=[jax.ShapeDtypeStruct((rows, columns), jnp.float32), TOKEN],
        in_specs=[VMEM, VMEM, VMEM] + [ANY] * len(after),
        out_specs=[VMEM, VMEM],
        compiler_params=pltpu.CompilerParams(vmem_limit_bytes=24 * MIB),
        cost_estimate=pl.CostEstimate(
            flops=1000,
            bytes_accessed=1000,
            transcendentals=0,
        ),
    )(latent, other, weight, *after)


def up_kernel(info, ids, mine, theirs, *refs, base_parts):
    *pieces, out, stack, wide, sems, staged = refs[base_parts:]
    bases = [
        part.at[:, pl.ds(begin, TILE)]
        for part in refs[:base_parts]
        for begin in range(0, part.shape[1], TILE)
    ]
    rank = mine.shape[1] // 2
    if len(pieces) == 1:
        stack[...] = pieces[0][...]
    else:
        own, beside, *received = pieces
        holds = info[1] == 0
        stack[0:rank, :] = own[...]
        stack[rank : 2 * rank, :] = beside[...]
        fill_here(info, holds, received, stack, 2 * rank, rank)
        fill_beside(info, holds, received, stack, 3 * rank, rank)
    lowrank = (mine[...] + theirs[...]).astype(jnp.bfloat16)
    zeros = jnp.zeros_like(lowrank)
    width = 2 * rank
    for lane in range(0, wide.shape[1], width):
        mask = ids[...] == owner_row(info, (lane // rank, lane // rank + 1), rank)
        wide[:, lane : lane + width] = jnp.where(mask, lowrank, zeros)
    copies = []
    tiles, _, tile = staged.shape
    for number in range(tiles):
        place = pl.ds(number * tile, tile)
        delta = jnp.dot(wide[...], stack[:, place], preferred_element_type=jnp.float32)
        total = bases[number][...] + delta.astype(jnp.bfloat16).astype(jnp.float32)
        staged[number] = total.astype(out.dtype)
        copies.append(
            pltpu.make_async_copy(staged.at[number], out.at[:, place], sems.at[number])
        )
        copies[-1].start()
    for copy in copies:
        copy.wait()


def on_device(latent, row_adapter_index, shared_weight, adapter_down_weight, adapter_up_weight):
    rows, half_width = latent.shape
    out_width = shared_weight.shape[1]
    local_adapters, _, rank = adapter_down_weight.shape
    shards = lax.axis_size("shard")
    adapters = shards * local_adapters
    columns = adapters * rank
    holds_down = lax.axis_index("tensor") == lax.axis_index("replica")
    tiles = out_width // TILE
    cuts = [0, out_width // 6, out_width // 2, out_width]
    down = jnp.swapaxes(adapter_down_weight, 1, 2).reshape(local_adapters * rank, half_width)
    up = adapter_up_weight.reshape(local_adapters * rank, out_width)
    row_ids = row_adapter_index.reshape(1, rows)
    routed = shards == 8 and local_adapters == 1 and lax.axis_size("replica") == 2
    routed = routed and half_width == out_width and tiles % 6 == 0
    lowrank = jax.ShapeDtypeStruct((rows, 2 * rank), jnp.float32)

    def placed(kernel, **options):
        def inner(*refs):
            return kernel(place_of_device(routed, shards, adapters), *refs, **options)

        return inner

    (token,) = call(prepare_kernel, [TOKEN], [VMEM], 16, moved=COPY)(shared_weight)
    down_out = [lowrank, jax.ShapeDtypeStruct((rows, 2 * rank), jnp.int32)]
    if routed:
        piece = jnp.where(holds_down, down, up)
        line = {1: along_line(piece, shards, 1)}
        other = swap(latent, "tensor")
        down_beside, up_beside = neighbour(down, shards), neighbour(up, shards)
        ready = token
        one, token = pack([(line[1], 0, rank)], token, down_beside, other)
        (back,) = pack([(piece, 0, rank)], ready, line[1], tokens=0)
        line[3] = along_line(back, shards, 3)
        line[2] = along_line(one, shards, 1)
        one_first, one_second = in_plane(one, shards, True), in_plane(one, shards, False)
        part_one, token = base(placed, latent, other, shared_weight, [token], cuts[0], cuts[1])
        three, token = pack([(line[3], 0, rank)], token)
        three_first, three_second = in_plane(three, shards, True), in_plane(three, shards, False)
        part_two, token = base(placed, latent, other, shared_weight, [token, up_beside], cuts[1], cuts[2])
        two, token = pack([(line[2], 0, rank)], token)
        two_second = in_plane(two, shards, False)
        turn, token = pack([(one_first, 0, rank)], token, one_second)
        corner_one = in_plane(turn, shards, False)
        two_first = along_line(turn, shards, 1)
        turn, token = pack([(three_second, 0, rank)], token, three_first)
        corner_three = in_plane(turn, shards, True)
        turn, token = pack([(two_second, 0, rank)], token)
        corner_two = in_plane(turn, shards, True)
        part_three, token = base(placed, latent, other, shared_weight, [token], cuts[2], cuts[3])
        parts = [part_one, part_two, part_three]
        corners = [corner_one, corner_three, corner_two]
        received = [one, three, two, one_first, three_first, two_first]
        received += [one_second, three_second, two_second]
        mine, ids = call(
            placed(down_first_kernel),
            down_out,
            [VMEM] * 13 + [ANY],
            16,
            [pltpu.VMEM((columns, half_width), latent.dtype)],
        )(row_ids, latent, down, down_beside, *received, token)
        mine = call(
            placed(down_last_kernel),
            lowrank,
            [VMEM] * 6,
            16,
            [pltpu.VMEM((4 * rank, half_width), latent.dtype)],
        )(ids, latent, mine, *corners)
        up_pieces = [up, up_beside, *received, *corners]
    else:
        other = swap(latent, "tensor")
        parts = []
        for begin, end in zip(cuts[:-1], cuts[1:]):
            part, token = base(placed, latent, other, shared_weight, [token], begin, end)
            parts.append(part)
        mine, ids = call(placed(down_whole_kernel), down_out, [VMEM] * 3, 48)(
            row_ids, latent, lax.all_gather(down, "shard", axis=0, tiled=True)
        )
        up_pieces = [lax.all_gather(up, "shard", axis=0, tiled=True)]
    theirs = swap(mine, "tensor")

    return pl.pallas_call(
        placed(up_kernel, base_parts=len(parts)),
        out_shape=jax.ShapeDtypeStruct((rows, out_width), latent.dtype),
        in_specs=[VMEM] * (3 + len(parts) + len(up_pieces)),
        out_specs=ANY,
        scratch_shapes=[
            pltpu.VMEM((columns, out_width), latent.dtype),
            pltpu.VMEM((rows, columns), latent.dtype),
            pltpu.SemaphoreType.DMA((tiles,)),
            pltpu.VMEM((tiles, rows, TILE), latent.dtype),
        ],
        compiler_params=pltpu.CompilerParams(vmem_limit_bytes=(24 if routed else 56) * MIB),
    )(ids, mine, theirs, *parts, *up_pieces)


def solution(mesh):
    return jax.shard_map(
        on_device,
        mesh=mesh,
        in_specs=(
            P(("replica", "shard"), "tensor"),
            P(("replica", "shard"), None),
            P(None, "tensor"),
            P("shard", "tensor", None),
            P("shard", None, "tensor"),
        ),
        out_specs=P(("replica", "shard"), "tensor"),
        check_vma=False,
    )
```

```python
import jax
import jax.numpy as jnp
import numpy as np
from jax import lax
from jax.experimental import pallas as pl
from jax.experimental.pallas import tpu as pltpu
from jax.sharding import PartitionSpec as P

MIB = 1024 * 1024
CHUNK = 512
TILE = 256
AXES = ("replica", "shard", "tensor")
FIRST_OWNER = 2
COPY = 0
VMEM = pl.BlockSpec(memory_space=pltpu.VMEM)
ANY = pl.BlockSpec(memory_space=pl.ANY)
TOKEN = jax.ShapeDtypeStruct((8, 128), jnp.float32)


def swap(value, axis):
    return lax.ppermute(value, axis, [(0, 1), (1, 0)])


def neighbour(value, shards):
    return lax.ppermute(value, "shard", [(i, i ^ 1) for i in range(shards)])


def ring_step(index, step):
    plane = index >> 1
    place = ((plane ^ (plane >> 1)) + step) & 3
    return ((place ^ (place >> 1)) << 1) | (index & 1)


def along_line(value, shards, step):
    return lax.ppermute(value, "shard", [(i, ring_step(i, step)) for i in range(shards)])


def in_plane(value, shards, first):
    pairs = []
    for r in range(2):
        for s in range(shards):
            for t in range(2):
                to_r, to_s = (r, s ^ 1) if (t == 0) == first else (r ^ 1, s)
                pairs.append(((r * shards + s) * 2 + t, (to_r * shards + to_s) * 2 + t))
    return lax.ppermute(value, AXES, pairs)


def call(kernel, out_shape, in_specs, limit, scratch=(), flops=0, moved=0):
    return pl.pallas_call(
        kernel,
        out_shape=out_shape,
        in_specs=in_specs,
        out_specs=jax.tree.map(lambda _: VMEM, out_shape),
        scratch_shapes=list(scratch),
        compiler_params=pltpu.CompilerParams(vmem_limit_bytes=limit * MIB),
        cost_estimate=pl.CostEstimate(flops=flops, bytes_accessed=moved, transcendentals=0),
    )


def place_of_device(routed, shards, adapters):
    core, index = lax.axis_index("tensor"), lax.axis_index("shard")
    holds_down = (core == lax.axis_index("replica")).astype(jnp.int32)
    owners = range(adapters)
    if routed:
        sources = [ring_step(index, -step) for step in (0, 1, 3, 2)]
        owners = [a for source in sources for a in (source, source ^ 1)]
    return [core, holds_down, *owners]


def owner_row(info, blocks, rank):
    place = lax.broadcasted_iota(jnp.int32, (1, len(blocks) * rank), 1) // rank
    row = jnp.full(place.shape, -1, jnp.int32)
    for number, block in enumerate(blocks):
        if block is not None:
            row = jnp.where(place == number, info[FIRST_OWNER + block], row)
    return row


def pack(pieces, *after):
    count = len(pieces)
    total = sum(rows for _, _, rows in pieces)
    width, dtype = pieces[0][0].shape[1], pieces[0][0].dtype

    def kernel(*refs):
        out, token = refs[-2:]
        top = 0
        for ref, (_, begin, rows) in zip(refs, pieces):
            out[top : top + rows, :] = ref[begin : begin + rows, :]
            top += rows
        token[...] = jnp.zeros_like(token)

    return call(
        kernel,
        [jax.ShapeDtypeStruct((total, width), dtype), TOKEN],
        [VMEM] * count + [ANY] * len(after),
        4,
        moved=COPY,
    )(*[array for array, _, _ in pieces], *after)


def put(blocks, stack, top, rank):
    for number, block in enumerate(blocks):
        place = top + 2 * number * rank
        stack[place : place + rank, :] = block[...]


def fill_here(info, holds, received, stack, top, rank):
    here, first, second = received[0:3], received[3:6], received[6:9]
    pl.when(holds)(lambda: put(here, stack, top, rank))
    for core, refs in enumerate((second, first)):
        away = jnp.logical_not(holds) & (info[0] == core)
        pl.when(away)(lambda refs=refs: put(refs, stack, top, rank))


def fill_beside(info, holds, received, stack, top, rank, direct=True, corner=True):
    if direct:
        for core, refs in enumerate((received[3:6], received[6:9])):
            pl.when(holds & (info[0] == core))(lambda refs=refs: put(refs, stack, top, rank))
    if corner:
        corners = received[9:12]
        pl.when(jnp.logical_not(holds))(lambda: put(corners, stack, top, rank))


def clear(stack, top, rank, count):
    for number in range(count):
        place = top + 2 * number * rank
        stack[place : place + rank, :] = jnp.zeros((rank, stack.shape[1]), stack.dtype)


def prepare_kernel(weight, *refs):
    refs[-1][...] = weight[0:8, 0:128].astype(jnp.float32)


def spread_rows(row_ids):
    wide = jnp.broadcast_to(row_ids[...].astype(jnp.float32), (128, row_ids.shape[1]))
    return wide.T.astype(jnp.int32)


def masked_products(info, ids, latent, stack, blocks, rank):
    total = None
    width = 2 * rank
    for skip in range(0, stack.shape[0], CHUNK):
        count = min(CHUNK, stack.shape[0] - skip)
        part = lax.dot_general(
            latent[...],
            stack[skip : skip + count, :],
            (((1,), (1,)), ((), ())),
            preferred_element_type=jnp.float32,
        )
        owners = owner_row(info, blocks[skip // rank : (skip + count) // rank], rank)
        for lane in range(0, count, width):
            lanes = slice(lane, lane + width)
            fold = jnp.where(ids[...] == owners[:, lanes], part[:, lanes], 0.0)
            total = fold if total is None else total + fold
    return total


def down_whole_kernel(info, row_ids, latent, stack, out, ids):
    ids[...] = spread_rows(row_ids)
    rank = out.shape[1] // 2
    blocks = range(stack.shape[0] // rank)
    out[...] = masked_products(info, ids, latent, stack, blocks, rank)


def down_first_kernel(info, row_ids, latent, own, beside, *refs):
    *received, _, out, ids, stack = refs
    ids[...] = spread_rows(row_ids)
    rank = own.shape[0]
    holds = info[1] == 1
    stack[0:rank, :] = own[...]
    stack[rank : 2 * rank, :] = beside[...]
    fill_here(info, holds, received, stack, 2 * rank, rank)
    fill_beside(info, holds, received, stack, 3 * rank, rank, corner=False)
    pl.when(jnp.logical_not(holds))(lambda: clear(stack, 3 * rank, rank, 3))
    out[...] = masked_products(info, ids, latent, stack, range(stack.shape[0] // rank), rank)


def down_last_kernel(info, ids, latent, earlier, *refs):
    *corners, out, stack = refs
    rank = out.shape[1] // 2
    holds = info[1] == 1

    @pl.when(holds)
    def _():
        out[...] = earlier[...]

    @pl.when(jnp.logical_not(holds))
    def _():
        for number, corner in enumerate(corners):
            stack[number * rank : (number + 1) * rank, :] = corner[...]
        stack[3 * rank : 4 * rank, :] = jnp.zeros((rank, stack.shape[1]), stack.dtype)
        pair = masked_products(info, ids, latent, stack, (3, 5, 7, None), rank)
        fold = pair[:, :rank] + pair[:, rank:]
        out[...] = earlier[...] + jnp.concatenate([jnp.zeros_like(fold), fold], axis=1)


def base_kernel(info, own, other, weight, *refs, skip):
    out, token = refs[-2:]
    token[...] = jnp.zeros_like(token)
    width = own.shape[1]
    mine = pl.ds(pl.multiple_of(info[0] * width, width), width)
    rest = pl.ds(pl.multiple_of((1 - info[0]) * width, width), width)
    step = min(CHUNK, out.shape[1])
    for begin in range(0, out.shape[1], step):
        place = slice(begin, min(begin + step, out.shape[1]))
        source = slice(skip + begin, skip + place.stop)
        out[:, place] = jnp.dot(
            own[...], weight[mine, source], preferred_element_type=jnp.float32
        ) + jnp.dot(other[...], weight[rest, source], preferred_element_type=jnp.float32)


def base(placed, latent, other, weight, after, skip, end):
    rows, columns = latent.shape[0], end - skip
    return pl.pallas_call(
        placed(base_kernel, skip=skip),
        out_shape=[jax.ShapeDtypeStruct((rows, columns), jnp.float32), TOKEN],
        in_specs=[VMEM, VMEM, VMEM] + [ANY] * len(after),
        out_specs=[VMEM, VMEM],
        compiler_params=pltpu.CompilerParams(vmem_limit_bytes=24 * MIB),
        cost_estimate=pl.CostEstimate(
            flops=1000,
            bytes_accessed=1000,
            transcendentals=0,
        ),
    )(latent, other, weight, *after)


def up_kernel(info, ids, mine, theirs, *refs, base_parts):
    *pieces, out, stack, wide, sems, staged = refs[base_parts:]
    bases = [
        part.at[:, pl.ds(begin, TILE)]
        for part in refs[:base_parts]
        for begin in range(0, part.shape[1], TILE)
    ]
    rank = mine.shape[1] // 2
    if len(pieces) == 1:
        stack[...] = pieces[0][...]
    else:
        own, beside, *received = pieces
        holds = info[1] == 0
        stack[0:rank, :] = own[...]
        stack[rank : 2 * rank, :] = beside[...]
        fill_here(info, holds, received, stack, 2 * rank, rank)
        fill_beside(info, holds, received, stack, 3 * rank, rank)
    lowrank = (mine[...] + theirs[...]).astype(jnp.bfloat16)
    zeros = jnp.zeros_like(lowrank)
    width = 2 * rank
    for lane in range(0, wide.shape[1], width):
        mask = ids[...] == owner_row(info, (lane // rank, lane // rank + 1), rank)
        wide[:, lane : lane + width] = jnp.where(mask, lowrank, zeros)
    copies = []
    tiles, _, tile = staged.shape
    for number in range(tiles):
        place = pl.ds(number * tile, tile)
        delta = jnp.dot(wide[...], stack[:, place], preferred_element_type=jnp.float32)
        total = bases[number][...] + delta.astype(jnp.bfloat16).astype(jnp.float32)
        staged[number] = total.astype(out.dtype)
        copies.append(
            pltpu.make_async_copy(staged.at[number], out.at[:, place], sems.at[number])
        )
        copies[-1].start()
    for copy in copies:
        copy.wait()


def on_device(latent, row_adapter_index, shared_weight, adapter_down_weight, adapter_up_weight):
    rows, half_width = latent.shape
    out_width = shared_weight.shape[1]
    local_adapters, _, rank = adapter_down_weight.shape
    shards = lax.axis_size("shard")
    adapters = shards * local_adapters
    columns = adapters * rank
    holds_down = lax.axis_index("tensor") == lax.axis_index("replica")
    tiles = out_width // TILE
    cuts = [0, out_width // 3, out_width // 2, out_width]
    down = jnp.swapaxes(adapter_down_weight, 1, 2).reshape(local_adapters * rank, half_width)
    up = adapter_up_weight.reshape(local_adapters * rank, out_width)
    row_ids = row_adapter_index.reshape(1, rows)
    routed = shards == 8 and local_adapters == 1 and lax.axis_size("replica") == 2
    routed = routed and half_width == out_width and tiles % 6 == 0
    lowrank = jax.ShapeDtypeStruct((rows, 2 * rank), jnp.float32)

    def placed(kernel, **options):
        def inner(*refs):
            return kernel(place_of_device(routed, shards, adapters), *refs, **options)

        return inner

    (token,) = call(prepare_kernel, [TOKEN], [VMEM], 16, moved=COPY)(shared_weight)
    down_out = [lowrank, jax.ShapeDtypeStruct((rows, 2 * rank), jnp.int32)]
    if routed:
        piece = jnp.where(holds_down, down, up)
        line = {1: along_line(piece, shards, 1)}
        other = swap(latent, "tensor")
        down_beside, up_beside = neighbour(down, shards), neighbour(up, shards)
        ready = token
        one, token = pack([(line[1], 0, rank)], token, down_beside, other)
        back, _ = pack([(piece, 0, rank)], ready)
        line[3] = along_line(back, shards, 3)
        line[2] = along_line(one, shards, 1)
        one_first, one_second = in_plane(one, shards, True), in_plane(one, shards, False)
        part_one, token = base(placed, latent, other, shared_weight, [token], cuts[0], cuts[1])
        three, token = pack([(line[3], 0, rank)], token)
        three_first, three_second = in_plane(three, shards, True), in_plane(three, shards, False)
        part_two, token = base(placed, latent, other, shared_weight, [token, up_beside], cuts[1], cuts[2])
        two, token = pack([(line[2], 0, rank)], token)
        two_second = in_plane(two, shards, False)
        turn, token = pack([(one_first, 0, rank)], token, one_second)
        corner_one = in_plane(turn, shards, False)
        two_first = along_line(turn, shards, 1)
        turn, token = pack([(three_second, 0, rank)], token, three_first)
        corner_three = in_plane(turn, shards, True)
        turn, token = pack([(two_second, 0, rank)], token)
        corner_two = in_plane(turn, shards, True)
        part_three, token = base(placed, latent, other, shared_weight, [token], cuts[2], cuts[3])
        parts = [part_one, part_two, part_three]
        corners = [corner_one, corner_three, corner_two]
        received = [one, three, two, one_first, three_first, two_first]
        received += [one_second, three_second, two_second]
        mine, ids = call(
            placed(down_first_kernel),
            down_out,
            [VMEM] * 13 + [ANY],
            16,
            [pltpu.VMEM((columns, half_width), latent.dtype)],
        )(row_ids, latent, down, down_beside, *received, token)
        mine = call(
            placed(down_last_kernel),
            lowrank,
            [VMEM] * 6,
            16,
            [pltpu.VMEM((4 * rank, half_width), latent.dtype)],
        )(ids, latent, mine, *corners)
        up_pieces = [up, up_beside, *received, *corners]
    else:
        other = swap(latent, "tensor")
        parts = []
        for begin, end in zip(cuts[:-1], cuts[1:]):
            part, token = base(placed, latent, other, shared_weight, [token], begin, end)
            parts.append(part)
        mine, ids = call(placed(down_whole_kernel), down_out, [VMEM] * 3, 48)(
            row_ids, latent, lax.all_gather(down, "shard", axis=0, tiled=True)
        )
        up_pieces = [lax.all_gather(up, "shard", axis=0, tiled=True)]
    theirs = swap(mine, "tensor")

    return pl.pallas_call(
        placed(up_kernel, base_parts=len(parts)),
        out_shape=jax.ShapeDtypeStruct((rows, out_width), latent.dtype),
        in_specs=[VMEM] * (3 + len(parts) + len(up_pieces)),
        out_specs=ANY,
        scratch_shapes=[
            pltpu.VMEM((columns, out_width), latent.dtype),
            pltpu.VMEM((rows, columns), latent.dtype),
            pltpu.SemaphoreType.DMA((tiles,)),
            pltpu.VMEM((tiles, rows, TILE), latent.dtype),
        ],
        compiler_params=pltpu.CompilerParams(vmem_limit_bytes=(24 if routed else 56) * MIB),
    )(ids, mine, theirs, *parts, *up_pieces)


def solution(mesh):
    return jax.shard_map(
        on_device,
        mesh=mesh,
        in_specs=(
            P(("replica", "shard"), "tensor"),
            P(("replica", "shard"), None),
            P(None, "tensor"),
            P("shard", "tensor", None),
            P("shard", None, "tensor"),
        ),
        out_specs=P(("replica", "shard"), "tensor"),
        check_vma=False,
    )
```

```python
import jax
import jax.numpy as jnp
import numpy as np
from jax import lax
from jax.experimental import pallas as pl
from jax.experimental.pallas import tpu as pltpu
from jax.sharding import PartitionSpec as P

MIB = 1024 * 1024
CHUNK = 512
TILE = 256
AXES = ("replica", "shard", "tensor")
FIRST_OWNER = 2
COPY = 0
VMEM = pl.BlockSpec(memory_space=pltpu.VMEM)
ANY = pl.BlockSpec(memory_space=pl.ANY)
TOKEN = jax.ShapeDtypeStruct((8, 128), jnp.float32)


def swap(value, axis):
    return lax.ppermute(value, axis, [(0, 1), (1, 0)])


def neighbour(value, shards):
    return lax.ppermute(value, "shard", [(i, i ^ 1) for i in range(shards)])


def ring_step(index, step):
    plane = index >> 1
    place = ((plane ^ (plane >> 1)) + step) & 3
    return ((place ^ (place >> 1)) << 1) | (index & 1)


def along_line(value, shards, step):
    return lax.ppermute(value, "shard", [(i, ring_step(i, step)) for i in range(shards)])


def in_plane(value, shards, first):
    pairs = []
    for r in range(2):
        for s in range(shards):
            for t in range(2):
                to_r, to_s = (r, s ^ 1) if (t == 0) == first else (r ^ 1, s)
                pairs.append(((r * shards + s) * 2 + t, (to_r * shards + to_s) * 2 + t))
    return lax.ppermute(value, AXES, pairs)


def call(kernel, out_shape, in_specs, limit, scratch=(), flops=0, moved=0):
    return pl.pallas_call(
        kernel,
        out_shape=out_shape,
        in_specs=in_specs,
        out_specs=jax.tree.map(lambda _: VMEM, out_shape),
        scratch_shapes=list(scratch),
        compiler_params=pltpu.CompilerParams(vmem_limit_bytes=limit * MIB),
        cost_estimate=pl.CostEstimate(flops=flops, bytes_accessed=moved, transcendentals=0),
    )


def place_of_device(routed, shards, adapters):
    core, index = lax.axis_index("tensor"), lax.axis_index("shard")
    holds_down = (core == lax.axis_index("replica")).astype(jnp.int32)
    owners = range(adapters)
    if routed:
        sources = [ring_step(index, -step) for step in (0, 1, 3, 2)]
        owners = [a for source in sources for a in (source, source ^ 1)]
    return [core, holds_down, *owners]


def owner_row(info, blocks, rank):
    place = lax.broadcasted_iota(jnp.int32, (1, len(blocks) * rank), 1) // rank
    row = jnp.full(place.shape, -1, jnp.int32)
    for number, block in enumerate(blocks):
        if block is not None:
            row = jnp.where(place == number, info[FIRST_OWNER + block], row)
    return row


def pack(pieces, *after):
    count = len(pieces)
    total = sum(rows for _, _, rows in pieces)
    width, dtype = pieces[0][0].shape[1], pieces[0][0].dtype

    def kernel(*refs):
        out, token = refs[-2:]
        top = 0
        for ref, (_, begin, rows) in zip(refs, pieces):
            out[top : top + rows, :] = ref[begin : begin + rows, :]
            top += rows
        token[...] = jnp.zeros_like(token)

    return call(
        kernel,
        [jax.ShapeDtypeStruct((total, width), dtype), TOKEN],
        [VMEM] * count + [ANY] * len(after),
        4,
        moved=COPY,
    )(*[array for array, _, _ in pieces], *after)


def put(blocks, stack, top, rank):
    for number, block in enumerate(blocks):
        place = top + 2 * number * rank
        stack[place : place + rank, :] = block[...]


def fill_here(info, holds, received, stack, top, rank):
    here, first, second = received[0:3], received[3:6], received[6:9]
    pl.when(holds)(lambda: put(here, stack, top, rank))
    for core, refs in enumerate((second, first)):
        away = jnp.logical_not(holds) & (info[0] == core)
        pl.when(away)(lambda refs=refs: put(refs, stack, top, rank))


def fill_beside(info, holds, received, stack, top, rank, direct=True, corner=True):
    if direct:
        for core, refs in enumerate((received[3:6], received[6:9])):
            pl.when(holds & (info[0] == core))(lambda refs=refs: put(refs, stack, top, rank))
    if corner:
        corners = received[9:12]
        pl.when(jnp.logical_not(holds))(lambda: put(corners, stack, top, rank))


def clear(stack, top, rank, count):
    for number in range(count):
        place = top + 2 * number * rank
        stack[place : place + rank, :] = jnp.zeros((rank, stack.shape[1]), stack.dtype)


def prepare_kernel(weight, *refs):
    refs[-1][...] = weight[0:8, 0:128].astype(jnp.float32)


def spread_rows(row_ids):
    wide = jnp.broadcast_to(row_ids[...].astype(jnp.float32), (128, row_ids.shape[1]))
    return wide.T.astype(jnp.int32)


def masked_products(info, ids, latent, stack, blocks, rank):
    total = None
    width = 2 * rank
    for skip in range(0, stack.shape[0], CHUNK):
        count = min(CHUNK, stack.shape[0] - skip)
        part = lax.dot_general(
            latent[...],
            stack[skip : skip + count, :],
            (((1,), (1,)), ((), ())),
            preferred_element_type=jnp.float32,
        )
        owners = owner_row(info, blocks[skip // rank : (skip + count) // rank], rank)
        for lane in range(0, count, width):
            lanes = slice(lane, lane + width)
            fold = jnp.where(ids[...] == owners[:, lanes], part[:, lanes], 0.0)
            total = fold if total is None else total + fold
    return total


def down_whole_kernel(info, row_ids, latent, stack, out, ids):
    ids[...] = spread_rows(row_ids)
    rank = out.shape[1] // 2
    blocks = range(stack.shape[0] // rank)
    out[...] = masked_products(info, ids, latent, stack, blocks, rank)


def down_first_kernel(info, row_ids, latent, own, beside, *refs):
    *received, _, out, ids, stack = refs
    ids[...] = spread_rows(row_ids)
    rank = own.shape[0]
    holds = info[1] == 1
    stack[0:rank, :] = own[...]
    stack[rank : 2 * rank, :] = beside[...]
    fill_here(info, holds, received, stack, 2 * rank, rank)
    fill_beside(info, holds, received, stack, 3 * rank, rank, corner=False)
    pl.when(jnp.logical_not(holds))(lambda: clear(stack, 3 * rank, rank, 3))
    out[...] = masked_products(info, ids, latent, stack, range(stack.shape[0] // rank), rank)


def down_last_kernel(info, ids, latent, earlier, *refs):
    *corners, out, stack = refs
    rank = out.shape[1] // 2
    holds = info[1] == 1

    @pl.when(holds)
    def _():
        out[...] = earlier[...]

    @pl.when(jnp.logical_not(holds))
    def _():
        for number, corner in enumerate(corners):
            stack[number * rank : (number + 1) * rank, :] = corner[...]
        stack[3 * rank : 4 * rank, :] = jnp.zeros((rank, stack.shape[1]), stack.dtype)
        pair = masked_products(info, ids, latent, stack, (3, 5, 7, None), rank)
        fold = pair[:, :rank] + pair[:, rank:]
        out[...] = earlier[...] + jnp.concatenate([jnp.zeros_like(fold), fold], axis=1)


def base_kernel(info, own, other, weight, *refs, skip):
    out, token = refs[-2:]
    token[...] = jnp.zeros_like(token)
    width = own.shape[1]
    mine = pl.ds(pl.multiple_of(info[0] * width, width), width)
    rest = pl.ds(pl.multiple_of((1 - info[0]) * width, width), width)
    step = min(CHUNK, out.shape[1])
    for begin in range(0, out.shape[1], step):
        place = slice(begin, min(begin + step, out.shape[1]))
        source = slice(skip + begin, skip + place.stop)
        out[:, place] = jnp.dot(
            own[...], weight[mine, source], preferred_element_type=jnp.float32
        ) + jnp.dot(other[...], weight[rest, source], preferred_element_type=jnp.float32)


def base(placed, latent, other, weight, after, skip, end):
    rows, columns = latent.shape[0], end - skip
    return pl.pallas_call(
        placed(base_kernel, skip=skip),
        out_shape=[jax.ShapeDtypeStruct((rows, columns), jnp.float32), TOKEN],
        in_specs=[VMEM, VMEM, VMEM] + [ANY] * len(after),
        out_specs=[VMEM, VMEM],
        compiler_params=pltpu.CompilerParams(vmem_limit_bytes=24 * MIB),
        cost_estimate=pl.CostEstimate(
            flops=1000,
            bytes_accessed=1000,
            transcendentals=0,
        ),
    )(latent, other, weight, *after)


def up_kernel(info, ids, mine, theirs, *refs, base_parts):
    *pieces, out, stack, wide, sems, staged = refs[base_parts:]
    bases = [
        part.at[:, pl.ds(begin, TILE)]
        for part in refs[:base_parts]
        for begin in range(0, part.shape[1], TILE)
    ]
    rank = mine.shape[1] // 2
    if len(pieces) == 1:
        stack[...] = pieces[0][...]
    else:
        own, beside, *received = pieces
        holds = info[1] == 0
        stack[0:rank, :] = own[...]
        stack[rank : 2 * rank, :] = beside[...]
        fill_here(info, holds, received, stack, 2 * rank, rank)
        fill_beside(info, holds, received, stack, 3 * rank, rank)
    lowrank = (mine[...] + theirs[...]).astype(jnp.bfloat16)
    zeros = jnp.zeros_like(lowrank)
    width = 2 * rank
    for lane in range(0, wide.shape[1], width):
        mask = ids[...] == owner_row(info, (lane // rank, lane // rank + 1), rank)
        wide[:, lane : lane + width] = jnp.where(mask, lowrank, zeros)
    copies = []
    tiles, _, tile = staged.shape
    for number in range(tiles):
        place = pl.ds(number * tile, tile)
        delta = jnp.dot(wide[...], stack[:, place], preferred_element_type=jnp.float32)
        total = bases[number][...] + delta.astype(jnp.bfloat16).astype(jnp.float32)
        staged[number] = total.astype(out.dtype)
        copies.append(
            pltpu.make_async_copy(staged.at[number], out.at[:, place], sems.at[number])
        )
        copies[-1].start()
    for copy in copies:
        copy.wait()


def on_device(latent, row_adapter_index, shared_weight, adapter_down_weight, adapter_up_weight):
    rows, half_width = latent.shape
    out_width = shared_weight.shape[1]
    local_adapters, _, rank = adapter_down_weight.shape
    shards = lax.axis_size("shard")
    adapters = shards * local_adapters
    columns = adapters * rank
    holds_down = lax.axis_index("tensor") == lax.axis_index("replica")
    tiles = out_width // TILE
    cuts = [0, out_width // 3, out_width // 2, out_width]
    down = jnp.swapaxes(adapter_down_weight, 1, 2).reshape(local_adapters * rank, half_width)
    up = adapter_up_weight.reshape(local_adapters * rank, out_width)
    row_ids = row_adapter_index.reshape(1, rows)
    routed = shards == 8 and local_adapters == 1 and lax.axis_size("replica") == 2
    routed = routed and half_width == out_width and tiles % 6 == 0
    lowrank = jax.ShapeDtypeStruct((rows, 2 * rank), jnp.float32)

    def placed(kernel, **options):
        def inner(*refs):
            return kernel(place_of_device(routed, shards, adapters), *refs, **options)

        return inner

    (token,) = call(prepare_kernel, [TOKEN], [VMEM], 16, moved=COPY)(shared_weight)
    down_out = [lowrank, jax.ShapeDtypeStruct((rows, 2 * rank), jnp.int32)]
    if routed:
        piece = jnp.where(holds_down, down, up)
        line = {1: along_line(piece, shards, 1)}
        other = swap(latent, "tensor")
        down_beside, up_beside = neighbour(down, shards), neighbour(up, shards)
        ready = token
        one, token = pack([(line[1], 0, rank)], token, down_beside, other)
        back, _ = pack([(piece, 0, rank)], ready)
        line[3] = along_line(back, shards, 3)
        line[2] = along_line(one, shards, 1)
        one_first, one_second = in_plane(one, shards, True), in_plane(one, shards, False)
        part_one, token = base(placed, latent, other, shared_weight, [token], cuts[0], cuts[1])
        three, token = pack([(line[3], 0, rank)], token)
        three_first, three_second = in_plane(three, shards, True), in_plane(three, shards, False)
        two, token = pack([(line[2], 0, rank)], token)
        two_second = in_plane(two, shards, False)
        part_two, token = base(placed, latent, other, shared_weight, [token, up_beside], cuts[1], cuts[2])
        turn, token = pack([(one_first, 0, rank)], token, one_second)
        corner_one = in_plane(turn, shards, False)
        two_first = along_line(turn, shards, 1)
        turn, token = pack([(three_second, 0, rank)], token, three_first)
        corner_three = in_plane(turn, shards, True)
        turn, token = pack([(two_second, 0, rank)], token)
        corner_two = in_plane(turn, shards, True)
        part_three, token = base(placed, latent, other, shared_weight, [token], cuts[2], cuts[3])
        parts = [part_one, part_two, part_three]
        corners = [corner_one, corner_three, corner_two]
        received = [one, three, two, one_first, three_first, two_first]
        received += [one_second, three_second, two_second]
        mine, ids = call(
            placed(down_first_kernel),
            down_out,
            [VMEM] * 13 + [ANY],
            16,
            [pltpu.VMEM((columns, half_width), latent.dtype)],
        )(row_ids, latent, down, down_beside, *received, token)
        mine = call(
            placed(down_last_kernel),
            lowrank,
            [VMEM] * 6,
            16,
            [pltpu.VMEM((4 * rank, half_width), latent.dtype)],
        )(ids, latent, mine, *corners)
        up_pieces = [up, up_beside, *received, *corners]
    else:
        other = swap(latent, "tensor")
        parts = []
        for begin, end in zip(cuts[:-1], cuts[1:]):
            part, token = base(placed, latent, other, shared_weight, [token], begin, end)
            parts.append(part)
        mine, ids = call(placed(down_whole_kernel), down_out, [VMEM] * 3, 48)(
            row_ids, latent, lax.all_gather(down, "shard", axis=0, tiled=True)
        )
        up_pieces = [lax.all_gather(up, "shard", axis=0, tiled=True)]
    theirs = swap(mine, "tensor")

    return pl.pallas_call(
        placed(up_kernel, base_parts=len(parts)),
        out_shape=jax.ShapeDtypeStruct((rows, out_width), latent.dtype),
        in_specs=[VMEM] * (3 + len(parts) + len(up_pieces)),
        out_specs=ANY,
        scratch_shapes=[
            pltpu.VMEM((columns, out_width), latent.dtype),
            pltpu.VMEM((rows, columns), latent.dtype),
            pltpu.SemaphoreType.DMA((tiles,)),
            pltpu.VMEM((tiles, rows, TILE), latent.dtype),
        ],
        compiler_params=pltpu.CompilerParams(vmem_limit_bytes=(24 if routed else 56) * MIB),
    )(ids, mine, theirs, *parts, *up_pieces)


def solution(mesh):
    return jax.shard_map(
        on_device,
        mesh=mesh,
        in_specs=(
            P(("replica", "shard"), "tensor"),
            P(("replica", "shard"), None),
            P(None, "tensor"),
            P("shard", "tensor", None),
            P("shard", None, "tensor"),
        ),
        out_specs=P(("replica", "shard"), "tensor"),
        check_vma=False,
    )
```
